32 devices in a mesh: rows: 16 (over z, y, x), grp: 2 (over core).
Axes of the slice: x: 2, y: 2, z: 4, core: 2. Of those that a mesh axis runs over, the one named last changes fastest.
Arguments:
- latent: float32 [8, 192, 512], P('grp', 'rows'), may hold values from -6 to 6
- w_first: float32 [2, 9, 32, 1], replicated, may hold values from -2 to 2
- b_first: float32 [2, 32], replicated, may hold values from -3 to 3
- w_mid: bfloat16 [2, 9, 32, 32], replicated, may hold values from -0.375 to 0.375
- b_mid: float32 [2, 32], replicated, may hold values from -3 to 3
- w_last: bfloat16 [2, 9, 2, 32], replicated, may hold values from -0.375 to 0.375
- b_last: float32 [2, 2], replicated, may hold values from -3 to 3
- vis_u: int32 [65536], replicated, may hold values from 0 to 191
- vis_v: int32 [65536], replicated, may hold values from 0 to 511
- observed: float32 [2, 65536], replicated, may hold values from -6 to 6
- vis_weight: float32 [65536], replicated, may hold values from 0.25 to 4
Outputs:
- images: float32 [8, 192, 512], P('grp', 'rows')
- loss: float32 [], replicated
- grad_first: float32 [2, 9, 32, 1], replicated
- grad_mid: float32 [2, 9, 32, 32], replicated
- grad_last: float32 [2, 9, 2, 32], replicated
- grad_bias_first: float32 [2, 32], replicated
- grad_bias_mid: float32 [2, 32], replicated
- grad_bias_last: float32 [2, 2], replicated
The draws below stay inside these ranges and needn't reach their ends.
All inputs are finite; a program needn't handle non-finite values.
Results may differ from the reference program's by a relative error of at most 0.0023.
Values may be sent and summed in bfloat16 or wider, within the bound.
No kernel may reach another device: no remote copies, remote signals or barrier semaphores. Data moves between devices by JAX's collectives and lax.ppermute only.
A program may use at most 320 MiB of HBM per device.

```python
import math
import jax
import jax.numpy as jnp
from jax import lax

W = 512
CH = 32
LAYERS = 2
NVIS = 65536
H = 192
BATCH = 8


def plant(entries, rng, smallest, top_value):
    spot = [jax.random.randint(jax.random.fold_in(rng, axis), (), 0, length) for axis, length in enumerate(entries.shape)]
    main_axis = entries.shape.index(max(entries.shape))
    neighbour = spot[:main_axis] + [(spot[main_axis] + 1) % entries.shape[main_axis]] + spot[main_axis + 1:]
    return entries.at[tuple(spot)].set(smallest).at[tuple(neighbour)].set(top_value)


def block_levels(key, dims, cuts, low, largest):
    gain = 1.0
    for position, blocks in cuts:
        steps = jax.random.uniform(jax.random.fold_in(jax.random.fold_in(key, 6), position), (blocks,), jnp.float32, low / len(cuts), largest / len(cuts))
        gain = gain * jnp.repeat(jnp.exp(steps), dims[position] // blocks).reshape((-1,) + (1,) * (len(dims) - 1 - position))
    return gain


def noise(own_key, shape, spread, limit, split=(), kind=jnp.bfloat16):
    entries = jax.random.normal(own_key, shape, jnp.float32) * spread
    if len(split) > 0:
        entries = block_levels(own_key, shape, split, -0.22, 0.18) * entries
    return jnp.clip(entries, min=-limit, max=limit).astype(kind)


def setup_inputs(seed: int = 0) -> dict:
    seeds = jax.random.split(jax.random.key(seed), 12)
    latent = noise(seeds[0], (BATCH, H, W), 1.0, 6.0, ((0, 2), (1, 16)), jnp.float32)
    w_first = noise(seeds[1], (LAYERS, 9, CH, 1), 9 ** -0.5, 2.0, (), jnp.float32)
    b_first = noise(seeds[2], (LAYERS, CH), 0.5, 3.0, (), jnp.float32)
    w_mid = noise(seeds[3], (LAYERS, 9, CH, CH), (9 * CH) ** -0.5, 0.375)
    b_mid = noise(seeds[4], (LAYERS, CH), 0.5, 3.0, (), jnp.float32)
    w_last = noise(seeds[5], (LAYERS, 9, 2, CH), (9 * CH) ** -0.5, 0.375)
    b_last = noise(seeds[6], (LAYERS, 2), 0.5, 3.0, (), jnp.float32)
    vis_u = plant(jax.random.randint(seeds[7], (NVIS,), 0, H), jax.random.fold_in(seeds[7], 1), 0, H - 1).astype(jnp.int32)
    vis_v = plant(jax.random.randint(seeds[8], (NVIS,), 0, W), jax.random.fold_in(seeds[8], 1), 0, W - 1).astype(jnp.int32)
    observed = noise(seeds[9], (2, NVIS), 1.0, 6.0, (), jnp.float32)
    vis_weight = jnp.clip(jnp.exp(jax.random.uniform(seeds[10], (NVIS,), jnp.float32, math.log(0.25), math.log(4.0))), 0.25, 4.0)
    return {"latent": latent, "w_first": w_first, "b_first": b_first, "w_mid": w_mid, "b_mid": b_mid, "w_last": w_last, "b_last": b_last, "vis_u": vis_u, "vis_v": vis_v, "observed": observed, "vis_weight": vis_weight}


def mult(pattern, first_op, second_op):
    return jnp.einsum(pattern, first_op.astype(jnp.float32), second_op.astype(jnp.float32), precision=lax.Precision.HIGHEST)

def conv_fwd(padded, weight, row_count, col_count):
    running = None
    for tap_id in range(9):
        off_row, off_col = divmod(tap_id, 3)
        window = padded[:, :, off_row:off_row + row_count, off_col:off_col + col_count]
        tap_term = mult('oi,sirw->sorw', weight[tap_id], window)
        running = tap_term if running is None else running + tap_term
    return running

def conv_back(padded_cot, weight, row_count, col_count):
    running = None
    for tap_id in range(9):
        off_row, off_col = divmod(tap_id, 3)
        window = padded_cot[:, :, 2 - off_row:2 - off_row + row_count, 2 - off_col:2 - off_col + col_count]
        tap_term = mult('oi,sorw->sirw', weight[tap_id], window)
        running = tap_term if running is None else running + tap_term
    return running

def weight_grad(cotangent, padded, row_count, col_count):
    pieces = []
    for tap_id in range(9):
        off_row, off_col = divmod(tap_id, 3)
        window = padded[:, :, off_row:off_row + row_count, off_col:off_col + col_count]
        pieces.append(mult('sorw,sirw->oi', cotangent, window))
    return jnp.stack(pieces)

def pad_both(field):
    return jnp.pad(field, ((0, 0), (0, 0), (1, 1), (1, 1)))

def silu_slope(pre_act):
    sigma = jax.nn.sigmoid(pre_act)
    return sigma * (1.0 + pre_act * (1.0 - sigma))

def one_sample(latent_img, w_first, b_first, w_mid, b_mid, w_last, b_last, vis_u, vis_v, observed, vis_weight, batch_size):
    height, img_width = latent_img.shape
    half_cols = img_width // 2
    layers = w_first.shape[0]
    vis_total = vis_u.shape[0]
    left_half = latent_img[None, :, :half_cols]
    right_half = latent_img[None, :, half_cols:]
    logdet = jnp.float32(0.0)
    stored = []
    for layer_id in range(layers):
        if layer_id % 2 == 0:
            cond_half, target = (left_half, right_half)
        else:
            cond_half, target = (right_half, left_half)
        cond_pad = pad_both(cond_half[:, None])
        pre_one = conv_fwd(cond_pad, w_first[layer_id], height, half_cols) + b_first[layer_id][None, :, None, None]
        hidden_one = pad_both(jax.nn.silu(pre_one).astype(jnp.bfloat16))
        pre_mid = conv_fwd(hidden_one, w_mid[layer_id], height, half_cols) + b_mid[layer_id][None, :, None, None]
        hidden_two = pad_both(jax.nn.silu(pre_mid).astype(jnp.bfloat16))
        raw_out = conv_fwd(hidden_two, w_last[layer_id], height, half_cols) + b_last[layer_id][None, :, None, None]
        log_scale = jnp.tanh(raw_out[:, 0])
        new_target = target * jnp.exp(log_scale) + raw_out[:, 1]
        logdet = logdet + jnp.sum(log_scale)
        stored.append((cond_pad, pre_one, hidden_one, pre_mid, hidden_two, log_scale, target))
        if layer_id % 2 == 0:
            right_half = new_target
        else:
            left_half = new_target
    image_out = jnp.concatenate([left_half, right_half], axis=2)[0]
    norm_scale = 1.0 / math.sqrt(height * img_width)
    spectrum = jnp.fft.fft2(image_out) * norm_scale
    picked = spectrum[vis_u, vis_v]
    resid_re = jnp.real(picked) - observed[0]
    resid_im = jnp.imag(picked) - observed[1]
    data_term = jnp.sum(vis_weight * (resid_re * resid_re + resid_im * resid_im)) / vis_total
    factor = 2.0 / (vis_total * batch_size)
    weighted = factor * vis_weight * (resid_re + 1j * resid_im)
    grid = jnp.zeros((height, img_width), spectrum.dtype).at[vis_u, vis_v].add(weighted)
    cot_image = (jnp.real(jnp.fft.ifft2(grid)) * (height * img_width) * norm_scale).astype(jnp.float32)
    cot_left = cot_image[None, :, :half_cols]
    cot_right = cot_image[None, :, half_cols:]
    grads = [[None] * layers for unused in range(6)]
    for layer_id in reversed(range(layers)):
        cond_pad, pre_one, hidden_one, pre_mid, hidden_two, log_scale, target = stored[layer_id]
        if layer_id % 2 == 0:
            cot_cond, cot_new = (cot_left, cot_right)
        else:
            cot_cond, cot_new = (cot_right, cot_left)
        grow_by = jnp.exp(log_scale)
        cot_target = cot_new * grow_by
        cot_log = cot_new * target * grow_by - 1.0 / (batch_size * height * img_width)
        cot_raw = jnp.stack([cot_log * (1.0 - log_scale * log_scale), cot_new], axis=1).astype(jnp.bfloat16)
        grads[2][layer_id] = weight_grad(cot_raw, hidden_two, height, half_cols)
        grads[5][layer_id] = lax.optimization_barrier(jnp.sum(cot_raw.astype(jnp.float32), axis=(0, 2, 3)))
        cot_h2 = conv_back(pad_both(cot_raw), w_last[layer_id], height, half_cols)
        cot_pre_mid = (cot_h2 * silu_slope(pre_mid)).astype(jnp.bfloat16)
        grads[1][layer_id] = weight_grad(cot_pre_mid, hidden_one, height, half_cols)
        grads[4][layer_id] = lax.optimization_barrier(jnp.sum(cot_pre_mid.astype(jnp.float32), axis=(0, 2, 3)))
        cot_h1 = conv_back(pad_both(cot_pre_mid), w_mid[layer_id], height, half_cols)
        cot_pre_one = (cot_h1 * silu_slope(pre_one)).astype(jnp.bfloat16)
        grads[0][layer_id] = weight_grad(cot_pre_one, cond_pad, height, half_cols)
        grads[3][layer_id] = lax.optimization_barrier(jnp.sum(cot_pre_one.astype(jnp.float32), axis=(0, 2, 3)))
        cot_cond = cot_cond + conv_back(pad_both(cot_pre_one), w_first[layer_id], height, half_cols)[:, 0]
        if layer_id % 2 == 0:
            cot_left, cot_right = (cot_cond, cot_target)
        else:
            cot_right, cot_left = (cot_cond, cot_target)
    grad_tuple = tuple((jnp.stack(entry) for entry in grads))
    return (image_out, data_term, logdet, grad_tuple)

def reference(latent, w_first, b_first, w_mid, b_mid, w_last, b_last, vis_u, vis_v, observed, vis_weight):
    batch_size, height, img_width = latent.shape
    zero_grads = (jnp.zeros(w_first.shape, jnp.float32), jnp.zeros(w_mid.shape, jnp.float32), jnp.zeros(w_last.shape, jnp.float32), jnp.zeros(b_first.shape, jnp.float32), jnp.zeros(b_mid.shape, jnp.float32), jnp.zeros(b_last.shape, jnp.float32))

    def step_fn(carry, latent_img):
        loss_acc, grad_acc = carry
        image_out, data_term, logdet, grad_tuple = one_sample(latent_img, w_first, b_first, w_mid, b_mid, w_last, b_last, vis_u, vis_v, observed, vis_weight, batch_size)
        loss_acc = loss_acc + (data_term - logdet / (height * img_width)) / batch_size
        grad_acc = tuple((prior + fresh for prior, fresh in zip(grad_acc, grad_tuple)))
        return ((loss_acc, grad_acc), image_out)
    (loss, grad_acc), images = lax.scan(step_fn, (jnp.float32(0.0), zero_grads), latent)
    return (images, loss, grad_acc[0], grad_acc[1], grad_acc[2], grad_acc[3], grad_acc[4], grad_acc[5])
```

```python
import functools
import math

import jax
import jax.numpy as jnp
import numpy as np
from jax import lax
from jax.experimental import pallas as pl
from jax.experimental.pallas import tpu as pltpu
from jax.sharding import PartitionSpec as P


def padded_2(block, sides, width):
    for axis, dim in sides:
        count = lax.axis_size(axis)
        forward = [(i, i + 1) for i in range(count - 1)]
        backward = [(target, source) for source, target in forward]
        low = lax.ppermute(
            lax.slice_in_dim(block, block.shape[dim] - width, None, axis=dim), axis, forward
        )
        high = lax.ppermute(lax.slice_in_dim(block, 0, width, axis=dim), axis, backward)
        block = jnp.concatenate([low, block, high], axis=dim)
    return block


def mult(pattern, first_op, second_op):
    if first_op.dtype == jnp.bfloat16 and second_op.dtype == jnp.bfloat16:
        return jnp.einsum(pattern, first_op, second_op, preferred_element_type=jnp.float32)
    return jnp.einsum(
        pattern,
        first_op.astype(jnp.float32),
        second_op.astype(jnp.float32),
        precision=lax.Precision.HIGHEST,
    )


def exact(pattern, first_op, second_op):
    return jnp.einsum(pattern, first_op, second_op, precision=lax.Precision.HIGHEST)


def conv_fwd(padded, weight, row_count, col_count):
    running = None
    for tap_id in range(9):
        off_row, off_col = divmod(tap_id, 3)
        window = padded[:, :, off_row : off_row + row_count, off_col : off_col + col_count]
        tap_term = mult("oi,sirw->sorw", weight[tap_id], window)
        running = tap_term if running is None else running + tap_term
    return running


def conv_back(padded_cot, weight, row_count, col_count):
    running = None
    for tap_id in range(9):
        off_row, off_col = divmod(tap_id, 3)
        window = padded_cot[
            :, :, 2 - off_row : 2 - off_row + row_count, 2 - off_col : 2 - off_col + col_count
        ]
        tap_term = mult("oi,sorw->sirw", weight[tap_id], window)
        running = tap_term if running is None else running + tap_term
    return running


def weight_grad(cotangent, padded, row_count, col_count):
    pieces = []
    for tap_id in range(9):
        off_row, off_col = divmod(tap_id, 3)
        window = padded[:, :, off_row : off_row + row_count, off_col : off_col + col_count]
        pieces.append(mult("sorw,sirw->oi", cotangent, window))
    return jnp.stack(pieces)


def widen(field):
    return jnp.pad(field, ((0, 0), (0, 0), (0, 0), (1, 1)))


def hidden_pad(field):
    return widen(padded_2(field, (("rows", 2),), 1))


def silu_slope(pre_act):
    sigma = jax.nn.sigmoid(pre_act)
    return sigma * (1.0 + pre_act * (1.0 - sigma))


def butterfly(value):
    for axis in ("grp", "rows"):
        count = lax.axis_size(axis)
        hop = 1
        while hop < count:
            value = value + lax.ppermute(value, axis, [(i, i ^ hop) for i in range(count)])
            hop *= 2
    return value


def grid_kernel(n_freq, pad_freq, height, img_width, r_ref, u_ref, v_ref, obs_ref, w_ref, sel_ref,
                out_ref, const_ref, u_s, c_s, f_s, acc):
    steps, width = u_ref.shape
    half = img_width // 2
    base = r_ref[0] * n_freq
    u = u_ref[...]
    v = v_ref[...]
    mirror = v > half
    v_fold = jnp.where(mirror, img_width - v, v)
    u_fold = jnp.where(mirror, jnp.where(u == 0, 0, height - u), u)
    col = v_fold - base
    col = jnp.where((col < 0) | (col >= n_freq), pad_freq, col)
    col = jnp.where(v_fold == half, n_freq, col)
    w = w_ref[...]
    o_re = obs_ref[0]
    o_im = obs_ref[1]
    const_ref[...] = jnp.sum(w * (o_re * o_re + o_im * o_im), axis=(0, 1), keepdims=True)
    u_s[...] = u_fold
    c_s[...] = col
    f_s[0] = w
    f_s[1] = w * o_re
    f_s[2] = w * jnp.where(mirror, -o_im, o_im)
    acc[...] = jnp.zeros_like(acc)

    def step(j, carry):
        row = pl.ds(j, 1)
        u_hot = lax.broadcasted_iota(jnp.int32, (height, width), 0) == u_s[row, :]
        u_hot = jnp.where(u_hot, 1.0, 0.0).astype(jnp.bfloat16)
        c_hot = lax.broadcasted_iota(jnp.int32, (pad_freq, width), 0) == c_s[row, :]
        parts = []
        for field in range(3):
            full = f_s[field, row, :]
            high = full.astype(jnp.bfloat16).astype(jnp.float32)
            parts.append(jnp.where(c_hot, high, 0.0).astype(jnp.bfloat16))
            parts.append(jnp.where(c_hot, full - high, 0.0).astype(jnp.bfloat16))
        values = jnp.concatenate(parts, axis=0)
        acc[...] += lax.dot_general(u_hot, values, (((1,), (1,)), ((), ())),
                                    preferred_element_type=jnp.float32)
        return carry

    lax.fori_loop(0, steps, step, 0)
    grid = acc[...]
    for field in range(3):
        out_ref[field] = jnp.dot(grid, sel_ref[field], precision=lax.Precision.HIGHEST,
                                 preferred_element_type=jnp.float32)


def gridded_lanes(vis_u, vis_v, observed, vis_weight, samples, height, img_width, n_rows):
    n_freq = img_width // 2 // n_rows
    pad_freq = 8 * ((n_freq + 8) // 8)
    lanes = 2 * samples * n_freq
    sel = np.zeros((2, 3, 6 * pad_freq, lanes), np.float32)
    for special in range(2):
        for lane in range(lanes):
            part, freq = lane // (samples * n_freq), lane % n_freq
            lone = special == 1 and freq == 0
            slot = n_freq if lone and part == 1 else freq
            fields = (0, 1, 2) if lone else (0, 1 + part, None)
            for out_id, field in enumerate(fields):
                if field is not None:
                    for split in range(2):
                        sel[special, out_id, (2 * field + split) * pad_freq + slot, lane] = 1.0
    index = lax.axis_index("rows")
    chosen = jnp.where(index == 0, jnp.asarray(sel[1]), jnp.asarray(sel[0]))
    width = min(2048, vis_u.shape[0])
    steps = vis_u.shape[0] // width
    vmem = pl.BlockSpec(memory_space=pltpu.VMEM)
    return pl.pallas_call(
        functools.partial(grid_kernel, n_freq, pad_freq, height, img_width),
        out_shape=(jax.ShapeDtypeStruct((3, height, lanes), jnp.float32),
                   jax.ShapeDtypeStruct((1, 1), jnp.float32)),
        in_specs=[pl.BlockSpec(memory_space=pltpu.SMEM)] + [vmem] * 5,
        out_specs=(vmem, vmem),
        scratch_shapes=[pltpu.VMEM((steps, width), jnp.int32), pltpu.VMEM((steps, width), jnp.int32),
                        pltpu.VMEM((3, steps, width), jnp.float32),
                        pltpu.VMEM((height, 6 * pad_freq), jnp.float32)],
        compiler_params=pltpu.CompilerParams(vmem_limit_bytes=48 * 2**20),
        cost_estimate=pl.CostEstimate(flops=2 * height * 256 * vis_u.shape[0],
                                      bytes_accessed=24 * vis_u.shape[0], transcendentals=0),
    )(index[None].astype(jnp.int32), vis_u.reshape(steps, width), vis_v.reshape(steps, width),
      observed.reshape(2, steps, width), vis_weight.reshape(steps, width), chosen)


def column_basis(img_width, n_rows):
    n_freq = img_width // 2 // n_rows
    cols = np.arange(img_width)
    freq = np.arange(img_width // 2)
    angle = 2.0 * np.pi * ((cols[:, None] * freq[None, :]) % img_width) / img_width
    re, im = np.cos(angle), -np.sin(angle)
    im[:, 0] = 1.0 - 2.0 * (cols % 2)
    both = np.stack([re.reshape(img_width, n_rows, n_freq), im.reshape(img_width, n_rows, n_freq)], 2)
    return both.reshape(img_width, img_width).astype(np.float32)


def spectral_kernel(scale, factor, half, n_freq, r_ref, z_ref, cs_ref, grid_ref, near_ref, data_ref):
    height, lanes = z_ref.shape
    lane = lax.broadcasted_iota(jnp.int32, (1, lanes), 1)
    lone = ((lane % n_freq) == 0) & (r_ref[0] == 0)
    sign = jnp.where(lane < half, 1.0, -1.0)
    hi = lax.Precision.HIGHEST
    z = z_ref[...] * scale
    a = jnp.dot(cs_ref[0], z, precision=hi, preferred_element_type=jnp.float32)
    b = jnp.dot(cs_ref[1], z, precision=hi, preferred_element_type=jnp.float32)
    w, t1, t2 = grid_ref[0], grid_ref[1], grid_ref[2]

    def swap(x):
        return jnp.concatenate([x[:, half:], x[:, :half]], axis=1)

    x = jnp.where(lone, a, a + sign * swap(b))
    p = w * x - t1
    q = jnp.where(lone, w * b + t2, -sign * swap(p))
    b_lone = jnp.where(lone, b, 0.0)
    terms = w * (x * x + b_lone * b_lone) - 2.0 * (x * t1 - b_lone * t2)
    data_ref[...] = jnp.sum(terms, axis=(0, 1), keepdims=True)
    near = jnp.dot(cs_ref[2], p, precision=hi, preferred_element_type=jnp.float32)
    near = near + jnp.dot(cs_ref[3], q, precision=hi, preferred_element_type=jnp.float32)
    near_ref[...] = near * (factor * scale)


def spectral(z, lanes_grid, scale, factor, samples):
    height, lanes = z.shape
    ids = np.arange(height)
    angle = 2.0 * np.pi * ((ids[:, None] * ids[None, :]) % height) / height
    cs = np.stack([np.cos(angle), np.sin(angle), np.cos(angle), np.sin(angle)]).astype(np.float32)
    vmem = pl.BlockSpec(memory_space=pltpu.VMEM)
    return pl.pallas_call(
        functools.partial(spectral_kernel, scale, factor, lanes // 2, lanes // (2 * samples)),
        out_shape=(jax.ShapeDtypeStruct((height, lanes), jnp.float32),
                   jax.ShapeDtypeStruct((1, 1), jnp.float32)),
        in_specs=[pl.BlockSpec(memory_space=pltpu.SMEM)] + [vmem] * 3,
        out_specs=(vmem, vmem),
        compiler_params=pltpu.CompilerParams(vmem_limit_bytes=48 * 2**20),
    )(lax.axis_index("rows")[None].astype(jnp.int32), z, jnp.asarray(cs), lanes_grid)


def body(
    latent, w_first, b_first, w_mid, b_mid, w_last, b_last, vis_u, vis_v, observed, vis_weight
):
    samples, row_count, img_width = latent.shape
    half_cols = img_width // 2
    n_rows = lax.axis_size("rows")
    n_grp = lax.axis_size("grp")
    height = row_count * n_rows
    batch_size = samples * n_grp
    layers = w_first.shape[0]
    vis_total = vis_u.shape[0]
    cells = height * img_width
    lanes_grid, obs_const = gridded_lanes(
        vis_u, vis_v, observed, vis_weight, samples, height, img_width, n_rows
    )
    left_half = latent[:, :, :half_cols]
    right_half = latent[:, :, half_cols:]
    logdet = jnp.float32(0.0)
    stored = []
    for layer_id in range(layers):
        if layer_id % 2 == 0:
            cond_half, target = (left_half, right_half)
        else:
            cond_half, target = (right_half, left_half)
        cond_pad = widen(padded_2(cond_half[:, None], (("rows", 2),), 1))
        pre_one = (
            conv_fwd(cond_pad, w_first[layer_id], row_count, half_cols)
            + b_first[layer_id][None, :, None, None]
        )
        hidden_one = hidden_pad(jax.nn.silu(pre_one).astype(jnp.bfloat16))
        pre_mid = (
            conv_fwd(hidden_one, w_mid[layer_id], row_count, half_cols)
            + b_mid[layer_id][None, :, None, None]
        )
        hidden_two = hidden_pad(jax.nn.silu(pre_mid).astype(jnp.bfloat16))
        raw_out = (
            conv_fwd(hidden_two, w_last[layer_id], row_count, half_cols)
            + b_last[layer_id][None, :, None, None]
        )
        log_scale = jnp.tanh(raw_out[:, 0])
        new_target = target * jnp.exp(log_scale) + raw_out[:, 1]
        logdet = logdet + jnp.sum(log_scale)
        stored.append((cond_pad, pre_one, hidden_one, pre_mid, hidden_two, log_scale, target))
        if layer_id % 2 == 0:
            right_half = new_target
        else:
            left_half = new_target
    image_out = jnp.concatenate([left_half, right_half], axis=2)
    norm_scale = 1.0 / math.sqrt(height * img_width)
    factor = 2.0 / (vis_total * batch_size)
    n_freq = img_width // 2 // n_rows
    basis = jnp.asarray(column_basis(img_width, n_rows))
    columns = exact("srw,wk->srk", image_out, basis)
    columns = columns.reshape(samples, row_count, n_rows, 2, n_freq).transpose(2, 1, 3, 0, 4)
    columns = columns.reshape(n_rows, row_count, 2 * samples * n_freq)
    columns = lax.all_to_all(columns, "rows", 0, 0, tiled=True)
    near, data_sum = spectral(
        columns.reshape(height, 2 * samples * n_freq), lanes_grid, norm_scale, factor, samples
    )
    near = lax.all_to_all(near.reshape(n_rows, row_count, -1), "rows", 0, 0, tiled=True)
    near = near.reshape(n_rows, row_count, 2, samples, n_freq).transpose(3, 1, 0, 2, 4)
    cot_image = exact("srk,wk->srw", near.reshape(samples, row_count, img_width), basis)
    data_part = (data_sum[0, 0] + samples * obs_const[0, 0] / n_rows) / vis_total
    loss_part = (data_part - logdet / (height * img_width)) / batch_size
    cot_left = cot_image[:, :, :half_cols]
    cot_right = cot_image[:, :, half_cols:]
    grads = [[None] * layers for unused in range(6)]
    for layer_id in reversed(range(layers)):
        cond_pad, pre_one, hidden_one, pre_mid, hidden_two, log_scale, target = stored[layer_id]
        if layer_id % 2 == 0:
            cot_cond, cot_new = (cot_left, cot_right)
        else:
            cot_cond, cot_new = (cot_right, cot_left)
        grow_by = jnp.exp(log_scale)
        cot_target = cot_new * grow_by
        cot_log = cot_new * target * grow_by - 1.0 / (batch_size * height * img_width)
        cot_raw = jnp.stack([cot_log * (1.0 - log_scale * log_scale), cot_new], axis=1).astype(
            jnp.bfloat16
        )
        raw_pad = widen(padded_2(cot_raw, (("rows", 2),), 1))
        grad_three = weight_grad(cot_raw, hidden_two, row_count, half_cols)
        bias_three = jnp.sum(cot_raw.astype(jnp.float32), axis=(0, 2, 3))
        cot_h2 = conv_back(raw_pad, w_last[layer_id], row_count, half_cols)
        cot_pre_mid = (cot_h2 * silu_slope(pre_mid)).astype(jnp.bfloat16)
        mid_pad = widen(padded_2(cot_pre_mid, (("rows", 2),), 1))
        grad_two = weight_grad(cot_pre_mid, hidden_one, row_count, half_cols)
        bias_two = jnp.sum(cot_pre_mid.astype(jnp.float32), axis=(0, 2, 3))
        cot_h1 = conv_back(mid_pad, w_mid[layer_id], row_count, half_cols)
        cot_pre_one = (cot_h1 * silu_slope(pre_one)).astype(jnp.bfloat16)
        first_pad = widen(padded_2(cot_pre_one, (("rows", 2),), 1))
        grad_one = weight_grad(cot_pre_one, cond_pad, row_count, half_cols)
        bias_one = jnp.sum(cot_pre_one.astype(jnp.float32), axis=(0, 2, 3))
        cot_cond = cot_cond + conv_back(first_pad, w_first[layer_id], row_count, half_cols)[:, 0]
        grads[0][layer_id] = grad_one
        grads[1][layer_id] = grad_two
        grads[2][layer_id] = grad_three
        grads[3][layer_id] = bias_one
        grads[4][layer_id] = bias_two
        grads[5][layer_id] = bias_three
        if layer_id % 2 == 0:
            cot_left, cot_right = (cot_cond, cot_target)
        else:
            cot_right, cot_left = (cot_cond, cot_target)
    stacked_grads = tuple((jnp.stack(entry) for entry in grads))
    flat = jnp.concatenate([entry.ravel() for entry in stacked_grads] + [loss_part[None]])
    length = flat.shape[0]
    flat = jnp.pad(flat, (0, -length % 1024)).reshape(-1, 128)
    flat = butterfly(flat).ravel()
    final_grads = []
    start = 0
    for entry in stacked_grads:
        final_grads.append(flat[start : start + entry.size].reshape(entry.shape))
        start += entry.size
    loss = flat[start]
    return (
        image_out,
        loss,
        final_grads[0],
        final_grads[1],
        final_grads[2],
        final_grads[3],
        final_grads[4],
        final_grads[5],
    )


def solution(mesh):
    in_specs = (P("grp", "rows", None), P(), P(), P(), P(), P(), P(), P(), P(), P(), P())
    out_specs = (P("grp", "rows", None), P(), P(), P(), P(), P(), P(), P())
    return jax.shard_map(body, mesh=mesh, in_specs=in_specs, out_specs=out_specs, check_vma=False)
```

```python
import functools
import math

import jax
import jax.numpy as jnp
import numpy as np
from jax import lax
from jax.experimental import pallas as pl
from jax.experimental.pallas import tpu as pltpu
from jax.sharding import PartitionSpec as P


BF = jnp.bfloat16
F32 = jnp.float32
GROUP = 4
LANE = 128
SLOT = 40
PLAN = (
    dict(o1=-10, n1=8, o2=-9, n2=8, h1=(2, 5), h2=(2, 4), s1=(2, 4), s2=(2, 4)),
    dict(o1=-7, n1=7, o2=-6, n2=6, h1=(1, 5), h2=(1, 4), s1=(1, 5), s2=(0, 6)),
)


def dot(a, b, dims=((1,), (0,))):
    return lax.dot_general(a, b, (dims, ((), ())), preferred_element_type=F32)


NT = ((1,), (1,))
TN = ((0,), (0,))


def split(x):
    high = x.astype(BF)
    return high, (x - high.astype(F32)).astype(BF)


def dot3(a, b, dims):
    return dot(a[0], b[0], dims) + dot(a[1], b[0], dims) + dot(a[0], b[1], dims)


def down(x):
    rows = lax.broadcasted_iota(jnp.int32, x.shape, 0)
    return jnp.where(rows == 0, 0.0, pltpu.roll(x, 1, 0))


def up(x):
    rows = lax.broadcasted_iota(jnp.int32, x.shape, 0)
    return jnp.where(rows == x.shape[0] - 1, 0.0, pltpu.roll(x, x.shape[0] - 1, 0))


def lane_ids(count):
    return lax.broadcasted_iota(jnp.int32, (1, count), 1)


def taps(cond):
    return down(cond) + pltpu.roll(cond, SLOT, 1) + pltpu.roll(up(cond), 2 * SLOT, 1)


def blk(start, count=1):
    return slice(start * LANE, (start + count) * LANE)


def forward_kernel(height, own, channels, r_ref, lat_ref, wf_a, wf_b, bf_ref, wm_ref, bm_ref, wl_a, wl_b, bl_ref,
                   basis_ref, img_ref, col_ref, logdet_ref, *rest):
    saved, scratch = rest[:-4], rest[-4:]
    hm, h0, hp, h2s = scratch
    first = r_ref[0] * own
    lane = lane_ids(LANE)
    image_row = lane - own + first
    image_mask = ((lane < 3 * own) & (image_row >= 0) & (image_row < height)).astype(F32)
    own_mask = ((lane >= own) & (lane < 2 * own)).astype(F32)

    @pl.when(pl.program_id(0) == 0)
    def _():
        logdet_ref[...] = jnp.zeros_like(logdet_ref)

    def mask_of(origin, block):
        row = origin + block * GROUP + lane // channels + first
        return ((row >= 0) & (row < height)).astype(F32)

    halves = [lat_ref[0, 0], lat_ref[0, 1]]
    for layer, (wf, wl) in enumerate(((wf_a, wl_a), (wf_b, wl_b))):
        plan = PLAN[layer]
        out_h1, out_h2, out_s1, out_s2, out_log = saved[5 * layer : 5 * layer + 5]
        cond, target = halves[layer], halves[1 - layer]
        if layer == 1:
            saved[10][0] = cond
        high, low = split(taps(cond))
        for k in range(plan["n1"]):
            weights = wf[0, :, blk(k)]
            pre = dot(high, weights) + dot(low, weights) + dot(high, wf[1, :, blk(k)])
            pre = pre + bf_ref[layer : layer + 1]
            sig = 0.5 + 0.5 * jnp.tanh(0.5 * pre)
            mask = mask_of(plan["o1"], k)
            hidden = pre * sig * mask
            start, count = plan["s1"]
            if start <= k < start + count:
                out_s1[0, :, blk(k - start)] = sig * (1.0 + pre * (1.0 - sig)) * mask
            plain = hidden.astype(BF)
            h0[:, blk(k)] = plain
            hm[:, blk(k)] = down(hidden).astype(BF)
            hp[:, blk(k)] = up(hidden).astype(BF)
            start, count = plan["h1"]
            if start <= k < start + count:
                out_h1[0, :, blk(k - start)] = plain
        for k in range(plan["n2"]):
            wide = min(2, plan["n1"] - k)
            pre = bm_ref[layer : layer + 1]
            for tap, part in enumerate((hm, h0, hp)):
                pre = pre + dot(part[:, blk(k, wide)], wm_ref[layer, tap, : wide * LANE])
            sig = 0.5 + 0.5 * jnp.tanh(0.5 * pre)
            mask = mask_of(plan["o2"], k)
            hidden = (pre * sig * mask).astype(BF)
            start, count = plan["s2"]
            if start <= k < start + count:
                out_s2[0, :, blk(k - start)] = sig * (1.0 + pre * (1.0 - sig)) * mask
            h2s[:, blk(k)] = hidden
            start, count = plan["h2"]
            if start <= k < start + count:
                out_h2[0, :, blk(k - start)] = hidden
        terms = dot(h2s[:, blk(0, plan["n2"])], wl[...])
        raw = down(terms[:, blk(0)]) + terms[:, blk(1)] + up(terms[:, blk(2)])
        raw = raw + bl_ref[layer : layer + 1]
        log_scale = jnp.tanh(raw)
        out_log[0] = log_scale
        logdet_ref[...] += jnp.sum(log_scale * own_mask, axis=0, keepdims=True)
        halves[1 - layer] = (target * jnp.exp(log_scale) + pltpu.roll(raw, LANE // 2, 1)) * image_mask
    cols = halves[0].shape[0]
    acc = None
    for side in range(2):
        mine = pltpu.roll(halves[side], LANE - own, 1).T
        img_ref[0, :, side * cols : (side + 1) * cols] = mine[:own]
        part = split(mine[:16])
        rows = slice(side * cols, (side + 1) * cols)
        term = dot3(part, (basis_ref[0, rows], basis_ref[1, rows]), ((1,), (0,)))
        acc = term if acc is None else acc + term
    col_ref[0] = acc[:own]


def backward_kernel(height, own, channels, reach, cells, r_ref, near_ref, lat_ref, loss_ref, wf_a, wf_b, wt_ref,
                    wl_a, wl_b, basis_ref, *rest):
    saved, out_ref, scratch = rest[:11], rest[11], rest[12:]
    near_s, dm, d0, dp, cpo_s, acc_mid, acc_last, acc_first, acc_bias = scratch
    step = pl.program_id(0)
    first = r_ref[0] * own
    lane = lane_ids(LANE)
    image_row = lane - own + first
    image_mask = ((lane < 3 * own) & (image_row >= 0) & (image_row < height)).astype(F32)
    raw_row = lane % (LANE // 2)
    own_mask = ((raw_row >= own) & (raw_row < 2 * own)).astype(F32)

    @pl.when(step == 0)
    def _():
        near_s[...] = jnp.zeros_like(near_s)
        for ref in (acc_mid, acc_last, acc_first, acc_bias):
            ref[...] = jnp.zeros_like(ref)

    def own_of(origin, block):
        row = origin + block * GROUP + lane // channels
        return ((row >= 0) & (row < own)).astype(F32)

    near_s[own - reach : 2 * own + reach, :] = near_ref[0]
    near = split(near_s[...])
    cols = lat_ref.shape[2]
    cots = []
    for side in range(2):
        rows = slice(side * cols, (side + 1) * cols)
        cots.append(dot3((basis_ref[0, rows], basis_ref[1, rows]), near, NT))
    cond_one = saved[10][0]
    for layer, wf, wl in ((1, wf_b, wl_b), (0, wf_a, wl_a)):
        plan = PLAN[layer]
        h1, h2, s1, s2, log_ref = saved[5 * layer : 5 * layer + 5]
        cond = cond_one if layer == 1 else lat_ref[0, 0]
        target = lat_ref[0, 1 - layer]
        cot_new = cots[1 - layer]
        log_scale = log_ref[0]
        cot_log = cot_new * target * jnp.exp(log_scale) - 1.0 / cells
        scale_part = cot_log * (1.0 - log_scale * log_scale) * image_mask
        raw = scale_part + pltpu.roll(cot_new * image_mask, LANE // 2, 1)
        raw = raw.astype(BF).astype(F32)
        mine = raw * own_mask
        spread = jnp.concatenate([up(raw).astype(BF), raw.astype(BF), down(raw).astype(BF)], 1)
        spread_own = jnp.concatenate([up(mine).astype(BF), mine.astype(BF), down(mine).astype(BF)], 1)
        acc_last[layer] += dot(spread_own, h2[0], TN)
        acc_bias[layer, 2:3] += jnp.sum(mine, axis=0, keepdims=True)
        start2, count2 = plan["s2"]
        base1, _ = plan["h1"]
        for k in range(start2, start2 + count2):
            cot = dot(spread, wl[blk(k), :], NT) * s2[0, :, blk(k - start2)]
            plain = cot.astype(BF)
            cot = plain.astype(F32)
            parts = (up(cot).astype(BF), plain, down(cot).astype(BF))
            for ref, part in zip((dm, d0, dp), parts):
                ref[:, blk(k - start2)] = part
            local = k - base1
            if 0 <= local < 4:
                mask = own_of(plan["o2"], k)
                acc_bias[layer, 1:2] += jnp.sum(cot * mask, axis=0, keepdims=True)
                lhs = jnp.concatenate([part * mask.astype(BF) for part in parts], 1)
                acc_mid[layer] += dot(lhs, h1[0, :, blk(local, 2)], TN)
        high, low = split(taps(cond))
        start1, count1 = plan["s1"]
        for k in range(start1, start1 + count1):
            back = min(1, k - start2)
            cot = None
            for tap, ref in enumerate((dm, d0, dp)):
                term = dot(ref[:, blk(k - start2 - back, 1 + back)], wt_ref[layer, tap, (1 - back) * LANE :])
                cot = term if cot is None else cot + term
            plain = (cot * s1[0, :, blk(k - start1)]).astype(BF)
            cpo_s[:, blk(k - start1)] = plain
            if k - start1 < 4:
                mask = own_of(plan["o1"], k)
                mine = plain.astype(F32) * mask
                acc_bias[layer, 0:1] += jnp.sum(mine, axis=0, keepdims=True)
                mine = mine.astype(BF)
                acc_first[layer, :, blk(k - start1)] += dot(high, mine, TN) + dot(low, mine, TN)
        if layer == 1:
            full = cpo_s[:, blk(0, count1)]
            lanes = blk(start1, count1)
            terms = dot(full, wf[0, :, lanes], NT) + dot(full, wf[1, :, lanes], NT)
            total = up(terms) + pltpu.roll(terms, LANE - SLOT, 1) * (lane < SLOT).astype(F32)
            total = jnp.where(lane < SLOT, total, 0.0)
            total = total + jnp.where(lane < SLOT, pltpu.roll(down(terms), LANE - 2 * SLOT, 1), 0.0)
            cots[1] = cots[1] + total

    @pl.when(step == pl.num_programs(0) - 1)
    def _():
        out_ref[...] = jnp.zeros_like(out_ref)
        layers = len(PLAN)
        tail = layers * 3 * channels
        fold_row = lax.broadcasted_iota(jnp.int32, (4 * LANE, channels), 0)
        fold_col = lax.broadcasted_iota(jnp.int32, (4 * LANE, channels), 1)
        fold = (fold_row % channels == fold_col).astype(F32)
        hi = lax.Precision.HIGHEST

        def folded(x):
            return jnp.dot(x, fold[: x.shape[1]], precision=hi, preferred_element_type=F32)

        def by_row(ref_value, groups, size, shift):
            shape = (groups * size, 4 * LANE)
            inner = lax.broadcasted_iota(jnp.int32, shape, 0) % size
            row = lax.broadcasted_iota(jnp.int32, shape, 1) // channels
            kept = jnp.where(row - inner == shift, ref_value, 0.0)
            return folded(jnp.sum(kept.reshape(groups, size, 4 * LANE), axis=1))

        for layer, plan in enumerate(PLAN):
            for dr in range(3):
                at = (layer * 3 + dr) * channels
                for dc in range(3):
                    total = None
                    for r in range(GROUP):
                        piece = acc_mid[layer, dc * LANE + r * channels : dc * LANE + (r + 1) * channels,
                                        (r + dr) * channels : (r + dr + 1) * channels]
                        total = piece if total is None else total + piece
                    out_ref[at : at + channels, dc * channels : (dc + 1) * channels] = total
                at = tail + (layer * 3 + dr) * 8
                shift = dr - 1 - own - plan["o2"] - GROUP * plan["h2"][0]
                out_ref[at : at + 6, :channels] = by_row(acc_last[layer], 6, LANE // 2, shift)
                shift = 1 - dr - own - plan["o1"] - GROUP * plan["s1"][0]
                out_ref[at : at + 3, channels : 2 * channels] = by_row(
                    acc_first[layer, : 3 * SLOT], 3, SLOT, shift)
            at = tail + layer * 24
            out_ref[at : at + 2, 2 * channels : 3 * channels] = folded(acc_bias[layer, 0:2])
            bias = acc_bias[layer, 2:3]
            pick = lane_ids(channels)
            low = jnp.sum(jnp.where(lane < LANE // 2, bias, 0.0), axis=1, keepdims=True)
            top = jnp.sum(jnp.where(lane >= LANE // 2, bias, 0.0), axis=1, keepdims=True)
            out_ref[at + 2 : at + 3, 2 * channels : 3 * channels] = jnp.where(
                pick == 0, low, jnp.where(pick == 1, top, jnp.where(pick == 2, loss_ref[...], 0.0)))


def banded_weights(layer, w_first, w_mid, w_last, own):
    plan = PLAN[layer]
    channels = w_mid.shape[2]
    ids = np.arange
    rows1, rows2 = plan["n1"] * GROUP, plan["n2"] * GROUP

    def hot(condition):
        return jnp.asarray(condition.astype(np.float32))

    first = w_first[layer, :, :, 0].reshape(3, 3, channels)
    mid = w_mid[layer].astype(F32).reshape(3, 3, channels, channels)
    last = w_last[layer].astype(F32).reshape(3, 3, 2, channels)
    wf, wm, wl = 0.0, 0.0, 0.0
    e = ids(SLOT)[:, None]
    half = ids(LANE // 2)[None, :]
    for dr in range(3):
        at = hot((e == ids(rows1)[None, :] + plan["o1"] + own - 1 + dr) & (e < 3 * own))
        wf = wf + at[None, :, :, None] * first[dr][:, None, None, :]
        at = hot(ids(8)[:, None] == ids(GROUP)[None, :] + dr)
        wm = wm + at[None, :, None, :, None] * mid[dr].transpose(0, 2, 1)[:, None, :, None, :]
        at = hot((ids(rows2)[:, None] == half - own - 1 + dr - plan["o2"]) & (half < 3 * own))
        wl = wl + at[:, None, None, None, :] * last[dr].transpose(2, 0, 1)[None, :, :, :, None]
    wf = jnp.pad(wf.reshape(3 * SLOT, rows1 * channels), ((0, LANE - 3 * SLOT), (0, 0)))
    high = lax.reduce_precision(wf, 8, 7)
    wf = jnp.stack([high.astype(BF), (wf - high).astype(BF)])
    wm = wm.reshape(3, 2 * LANE, LANE).astype(BF)
    wt = jnp.concatenate([wm[:, LANE:].transpose(0, 2, 1), wm[:, :LANE].transpose(0, 2, 1)], 1)
    return wf, wm, wt, wl.reshape(rows2 * channels, 3 * LANE).astype(BF)


def butterfly(value):
    for axis in ("grp", "rows"):
        count = lax.axis_size(axis)
        hop = 1
        while hop < count:
            value = value + lax.ppermute(value, axis, [(i, i ^ hop) for i in range(count)])
            hop *= 2
    return value


def grid_kernel(n_freq, pad_freq, height, img_width, r_ref, u_ref, v_ref, obs_ref, w_ref, sel_ref,
                out_ref, const_ref, u_s, c_s, f_s, acc):
    steps, width = u_ref.shape
    half = img_width // 2
    base = r_ref[0] * n_freq
    u = u_ref[...]
    v = v_ref[...]
    mirror = v > half
    v_fold = jnp.where(mirror, img_width - v, v)
    u_fold = jnp.where(mirror, jnp.where(u == 0, 0, height - u), u)
    col = v_fold - base
    col = jnp.where((col < 0) | (col >= n_freq), pad_freq, col)
    col = jnp.where(v_fold == half, n_freq, col)
    w = w_ref[...]
    o_re = obs_ref[0]
    o_im = obs_ref[1]
    const_ref[...] = jnp.sum(w * (o_re * o_re + o_im * o_im), axis=(0, 1), keepdims=True)
    u_s[...] = u_fold
    c_s[...] = col
    f_s[0] = w
    f_s[1] = w * o_re
    f_s[2] = w * jnp.where(mirror, -o_im, o_im)
    acc[...] = jnp.zeros_like(acc)

    def step(j, carry):
        row = pl.ds(j, 1)
        u_hot = lax.broadcasted_iota(jnp.int32, (height, width), 0) == u_s[row, :]
        u_hot = jnp.where(u_hot, 1.0, 0.0).astype(jnp.bfloat16)
        c_hot = lax.broadcasted_iota(jnp.int32, (pad_freq, width), 0) == c_s[row, :]
        parts = []
        for field in range(3):
            full = f_s[field, row, :]
            high = full.astype(jnp.bfloat16).astype(jnp.float32)
            parts.append(jnp.where(c_hot, high, 0.0).astype(jnp.bfloat16))
            parts.append(jnp.where(c_hot, full - high, 0.0).astype(jnp.bfloat16))
        values = jnp.concatenate(parts, axis=0)
        acc[...] += lax.dot_general(u_hot, values, (((1,), (1,)), ((), ())),
                                    preferred_element_type=jnp.float32)
        return carry

    lax.fori_loop(0, steps, step, 0)
    grid = acc[...]
    for field in range(3):
        out_ref[field] = jnp.dot(grid, sel_ref[field], precision=lax.Precision.HIGHEST,
                                 preferred_element_type=jnp.float32)


def gridded_lanes(vis_u, vis_v, observed, vis_weight, samples, height, img_width, n_rows):
    n_freq = img_width // 2 // n_rows
    pad_freq = 8 * ((n_freq + 8) // 8)
    lanes = 2 * samples * n_freq
    sel = np.zeros((2, 3, 6 * pad_freq, lanes), np.float32)
    for special in range(2):
        for lane in range(lanes):
            part, freq = lane // (samples * n_freq), lane % n_freq
            lone = special == 1 and freq == 0
            slot = n_freq if lone and part == 1 else freq
            fields = (0, 1, 2) if lone else (0, 1 + part, None)
            for out_id, field in enumerate(fields):
                if field is not None:
                    for split in range(2):
                        sel[special, out_id, (2 * field + split) * pad_freq + slot, lane] = 1.0
    index = lax.axis_index("rows")
    chosen = jnp.where(index == 0, jnp.asarray(sel[1]), jnp.asarray(sel[0]))
    width = min(2048, vis_u.shape[0])
    steps = vis_u.shape[0] // width
    vmem = pl.BlockSpec(memory_space=pltpu.VMEM)
    return pl.pallas_call(
        functools.partial(grid_kernel, n_freq, pad_freq, height, img_width),
        out_shape=(jax.ShapeDtypeStruct((3, height, lanes), jnp.float32),
                   jax.ShapeDtypeStruct((1, 1), jnp.float32)),
        in_specs=[pl.BlockSpec(memory_space=pltpu.SMEM)] + [vmem] * 5,
        out_specs=(vmem, vmem),
        scratch_shapes=[pltpu.VMEM((steps, width), jnp.int32), pltpu.VMEM((steps, width), jnp.int32),
                        pltpu.VMEM((3, steps, width), jnp.float32),
                        pltpu.VMEM((height, 6 * pad_freq), jnp.float32)],
        compiler_params=pltpu.CompilerParams(vmem_limit_bytes=48 * 2**20),
        cost_estimate=pl.CostEstimate(flops=2 * height * 256 * vis_u.shape[0],
                                      bytes_accessed=24 * vis_u.shape[0], transcendentals=0),
    )(index[None].astype(jnp.int32), vis_u.reshape(steps, width), vis_v.reshape(steps, width),
      observed.reshape(2, steps, width), vis_weight.reshape(steps, width), chosen)


def column_basis(img_width, n_rows):
    n_freq = img_width // 2 // n_rows
    cols = np.arange(img_width)
    freq = np.arange(img_width // 2)
    angle = 2.0 * np.pi * ((cols[:, None] * freq[None, :]) % img_width) / img_width
    re, im = np.cos(angle), -np.sin(angle)
    im[:, 0] = 1.0 - 2.0 * (cols % 2)
    both = np.stack([re.reshape(img_width, n_rows, n_freq), im.reshape(img_width, n_rows, n_freq)], 2)
    return both.reshape(img_width, img_width).astype(np.float32)


def spectral_kernel(scale, factor, half, n_freq, r_ref, z_ref, cs_ref, grid_ref, near_ref, data_ref):
    height, lanes = z_ref.shape
    lane = lax.broadcasted_iota(jnp.int32, (1, lanes), 1)
    lone = ((lane % n_freq) == 0) & (r_ref[0] == 0)
    sign = jnp.where(lane < half, 1.0, -1.0)
    hi = lax.Precision.HIGHEST
    z = z_ref[...] * scale
    a = jnp.dot(cs_ref[0], z, precision=hi, preferred_element_type=jnp.float32)
    b = jnp.dot(cs_ref[1], z, precision=hi, preferred_element_type=jnp.float32)
    w, t1, t2 = grid_ref[0], grid_ref[1], grid_ref[2]

    def swap(x):
        return jnp.concatenate([x[:, half:], x[:, :half]], axis=1)

    x = jnp.where(lone, a, a + sign * swap(b))
    p = w * x - t1
    q = jnp.where(lone, w * b + t2, -sign * swap(p))
    b_lone = jnp.where(lone, b, 0.0)
    terms = w * (x * x + b_lone * b_lone) - 2.0 * (x * t1 - b_lone * t2)
    data_ref[...] = jnp.sum(terms, axis=(0, 1), keepdims=True)
    near = jnp.dot(cs_ref[2], p, precision=hi, preferred_element_type=jnp.float32)
    near = near + jnp.dot(cs_ref[3], q, precision=hi, preferred_element_type=jnp.float32)
    near_ref[...] = near * (factor * scale)


def spectral(z, lanes_grid, scale, factor, samples):
    height, lanes = z.shape
    ids = np.arange(height)
    angle = 2.0 * np.pi * ((ids[:, None] * ids[None, :]) % height) / height
    cs = np.stack([np.cos(angle), np.sin(angle), np.cos(angle), np.sin(angle)]).astype(np.float32)
    vmem = pl.BlockSpec(memory_space=pltpu.VMEM)
    return pl.pallas_call(
        functools.partial(spectral_kernel, scale, factor, lanes // 2, lanes // (2 * samples)),
        out_shape=(jax.ShapeDtypeStruct((height, lanes), jnp.float32),
                   jax.ShapeDtypeStruct((1, 1), jnp.float32)),
        in_specs=[pl.BlockSpec(memory_space=pltpu.SMEM)] + [vmem] * 3,
        out_specs=(vmem, vmem),
        compiler_params=pltpu.CompilerParams(vmem_limit_bytes=48 * 2**20),
    )(lax.axis_index("rows")[None].astype(jnp.int32), z, jnp.asarray(cs), lanes_grid)


def body(
    latent, w_first, b_first, w_mid, b_mid, w_last, b_last, vis_u, vis_v, observed, vis_weight
):
    samples, row_count, img_width = latent.shape
    half_cols = img_width // 2
    n_rows = lax.axis_size("rows")
    n_grp = lax.axis_size("grp")
    height = row_count * n_rows
    batch_size = samples * n_grp
    layers = w_first.shape[0]
    vis_total = vis_u.shape[0]
    cells = height * img_width
    lanes_grid, obs_const = gridded_lanes(
        vis_u, vis_v, observed, vis_weight, samples, height, img_width, n_rows
    )
    channels = w_mid.shape[2]
    half = half_cols
    forward = [(i, i + 1) for i in range(n_rows - 1)]
    backward = [(target, source) for source, target in forward]
    low = lax.ppermute(latent, "rows", forward)
    high = lax.ppermute(latent, "rows", backward)
    wide = jnp.concatenate([low, latent, high], axis=1)
    wide = wide.reshape(samples, 3 * row_count, 2, half).transpose(0, 2, 3, 1)
    wide = jnp.pad(wide, ((0, 0), (0, 0), (0, 0), (0, LANE - 3 * row_count)))
    bands = [banded_weights(layer, w_first, w_mid, w_last, row_count) for layer in range(layers)]
    (wf_a, wm_a, wt_a, wl_a), (wf_b, wm_b, wt_b, wl_b) = bands
    wm = jnp.stack([wm_a, wm_b])
    wt = jnp.stack([wt_a, wt_b])
    bias_first = jnp.tile(b_first, (1, GROUP))
    bias_mid = jnp.tile(b_mid, (1, GROUP))
    bias_last = jnp.repeat(b_last, LANE // 2, axis=1)
    basis_np = column_basis(img_width, n_rows)
    basis_high = basis_np.astype(BF)
    basis_low = (basis_np - basis_high.astype(np.float32)).astype(BF)
    basis = jnp.asarray(np.stack([basis_high, basis_low]))
    index = lax.axis_index("rows")[None].astype(jnp.int32)
    smem = pl.BlockSpec(memory_space=pltpu.SMEM)

    def whole(value):
        rank = value.ndim
        return pl.BlockSpec(value.shape, lambda s: (0,) * rank)

    def per_sample(*shape):
        rank = len(shape)
        return pl.BlockSpec((1,) + shape, lambda s: (s,) + (0,) * rank)

    saved_shapes = []
    for plan in PLAN:
        for key, kind in (("h1", BF), ("h2", BF), ("s1", F32), ("s2", F32)):
            saved_shapes.append(((half, plan[key][1] * LANE), kind))
        saved_shapes.append(((half, LANE), F32))
    saved_shapes.append(((half, LANE), F32))
    saved_specs = [per_sample(*shape) for shape, kind in saved_shapes]
    saved_types = [jax.ShapeDtypeStruct((samples,) + shape, kind) for shape, kind in saved_shapes]
    weights = (wf_a, wf_b, bias_first, wm, bias_mid, wl_a, wl_b, bias_last, basis)
    max1 = max(plan["n1"] for plan in PLAN) * LANE
    max2 = max(plan["n2"] for plan in PLAN) * LANE
    params = pltpu.CompilerParams(vmem_limit_bytes=56 * 2**20)
    image_out, columns, logdet, *saved = pl.pallas_call(
        functools.partial(forward_kernel, height, row_count, channels),
        grid=(samples,),
        out_shape=(
            jax.ShapeDtypeStruct((samples, row_count, img_width), F32),
            jax.ShapeDtypeStruct((samples, row_count, img_width), F32),
            jax.ShapeDtypeStruct((1, LANE), F32),
            *saved_types,
        ),
        in_specs=[smem, per_sample(2, half, LANE)] + [whole(value) for value in weights],
        out_specs=(
            per_sample(row_count, img_width),
            per_sample(row_count, img_width),
            pl.BlockSpec((1, LANE), lambda s: (0, 0)),
            *saved_specs,
        ),
        scratch_shapes=[pltpu.VMEM((half, max1), BF)] * 3 + [pltpu.VMEM((half, max2), BF)],
        compiler_params=params,
    )(index, wide, *weights)
    logdet = jnp.sum(logdet)
    norm_scale = 1.0 / math.sqrt(height * img_width)
    factor = 2.0 / (vis_total * batch_size)
    n_freq = img_width // 2 // n_rows
    columns = columns.reshape(samples, row_count, n_rows, 2, n_freq).transpose(2, 1, 3, 0, 4)
    columns = columns.reshape(n_rows, row_count, 2 * samples * n_freq)
    columns = lax.all_to_all(columns, "rows", 0, 0, tiled=True)
    near, data_sum = spectral(
        columns.reshape(height, 2 * samples * n_freq), lanes_grid, norm_scale, factor, samples
    )
    reach = 6
    blocks = jnp.pad(near.reshape(n_rows, row_count, -1), ((1, 1), (0, 0), (0, 0)))
    blocks = jnp.concatenate(
        [blocks[:-2, row_count - reach :], blocks[1:-1], blocks[2:, :reach]], axis=1
    )
    near = lax.all_to_all(blocks, "rows", 0, 0, tiled=True)
    span = row_count + 2 * reach
    near = near.reshape(n_rows, span, 2, samples, n_freq).transpose(3, 1, 0, 2, 4)
    near = near.reshape(samples, span, img_width)
    data_part = (data_sum[0, 0] + samples * obs_const[0, 0] / n_rows) / vis_total
    loss_part = (data_part - logdet / (height * img_width)) / batch_size
    out_rows = layers * (3 * channels + 24)
    weights = (wf_a, wf_b, wt, wl_a, wl_b, basis)
    flat = pl.pallas_call(
        functools.partial(
            backward_kernel, height, row_count, channels, reach, batch_size * cells
        ),
        grid=(samples,),
        out_shape=jax.ShapeDtypeStruct((out_rows, LANE), F32),
        in_specs=[smem, per_sample(span, img_width), per_sample(2, half, LANE),
                  pl.BlockSpec((1, 1), lambda s: (0, 0))]
        + [whole(value) for value in weights] + saved_specs,
        out_specs=pl.BlockSpec((out_rows, LANE), lambda s: (0, 0)),
        scratch_shapes=[
            pltpu.VMEM((LANE, img_width), F32),
            *[pltpu.VMEM((half, max2), BF)] * 3,
            pltpu.VMEM((half, max1), BF),
            pltpu.VMEM((layers, 3 * LANE, 2 * LANE), F32),
            pltpu.VMEM((layers, 3 * LANE, 4 * LANE), F32),
            pltpu.VMEM((layers, LANE, 4 * LANE), F32),
            pltpu.VMEM((layers, 8, LANE), F32),
        ],
        compiler_params=params,
    )(index, near, wide, loss_part.reshape(1, 1), *weights, *saved)
    flat = butterfly(flat)
    main = flat[: layers * 3 * channels, : 3 * channels]
    main = main.reshape(layers, 3, channels, 3, channels).transpose(0, 1, 3, 2, 4)
    rest = flat[layers * 3 * channels :].reshape(layers, 3, 8, LANE)
    final_grads = [
        rest[:, :, :3, channels : 2 * channels].reshape(layers, 9, channels, 1),
        main.reshape(layers, 9, channels, channels),
        rest[:, :, :6, :channels].reshape(layers, 9, 2, channels),
        rest[:, 0, 0, 2 * channels : 3 * channels],
        rest[:, 0, 1, 2 * channels : 3 * channels],
        rest[:, 0, 2, 2 * channels : 2 * channels + 2],
    ]
    loss = rest[0, 0, 2, 2 * channels + 2]
    return (
        image_out,
        loss,
        final_grads[0],
        final_grads[1],
        final_grads[2],
        final_grads[3],
        final_grads[4],
        final_grads[5],
    )


def solution(mesh):
    in_specs = (P("grp", "rows", None), P(), P(), P(), P(), P(), P(), P(), P(), P(), P())
    out_specs = (P("grp", "rows", None), P(), P(), P(), P(), P(), P(), P())
    return jax.shard_map(body, mesh=mesh, in_specs=in_specs, out_specs=out_specs, check_vma=False)
```

```python
import functools
import math

import jax
import jax.numpy as jnp
import numpy as np
from jax import lax
from jax.experimental import pallas as pl
from jax.experimental.pallas import tpu as pltpu
from jax.sharding import PartitionSpec as P


BF = jnp.bfloat16
F32 = jnp.float32
GROUP = 4
LANE = 128
SLOT = 40
PLAN = (
    dict(o1=-10, n1=8, o2=-9, n2=8, h1=(2, 5), h2=(2, 4), s1=(2, 4), s2=(2, 4)),
    dict(o1=-7, n1=7, o2=-6, n2=6, h1=(1, 5), h2=(1, 4), s1=(1, 5), s2=(0, 6)),
)


def dot(a, b, dims=((1,), (0,))):
    return lax.dot_general(a, b, (dims, ((), ())), preferred_element_type=F32)


NT = ((1,), (1,))
TN = ((0,), (0,))


def split(x):
    high = x.astype(BF)
    return high, (x - high.astype(F32)).astype(BF)


def dot3(a, b, dims):
    return dot(a[0], b[0], dims) + dot(a[1], b[0], dims) + dot(a[0], b[1], dims)


def down(x):
    rows = lax.broadcasted_iota(jnp.int32, x.shape, 0)
    return jnp.where(rows == 0, 0.0, pltpu.roll(x, 1, 0))


def up(x):
    rows = lax.broadcasted_iota(jnp.int32, x.shape, 0)
    return jnp.where(rows == x.shape[0] - 1, 0.0, pltpu.roll(x, x.shape[0] - 1, 0))


def lane_ids(count):
    return lax.broadcasted_iota(jnp.int32, (1, count), 1)


def taps(cond):
    return down(cond) + pltpu.roll(cond, SLOT, 1) + pltpu.roll(up(cond), 2 * SLOT, 1)


def blk(start, count=1):
    return slice(start * LANE, (start + count) * LANE)


def forward_kernel(height, own, channels, r_ref, lat_ref, wf_a, wf_b, bf_ref, wm_ref, bm_ref, wl_a, wl_b, bl_ref,
                   basis_ref, img_ref, col_ref, logdet_ref, *rest):
    saved, scratch = rest[:-4], rest[-4:]
    hm, h0, hp, h2s = scratch
    first = r_ref[0] * own
    lane = lane_ids(LANE)
    image_row = lane - own + first
    image_mask = ((lane < 3 * own) & (image_row >= 0) & (image_row < height)).astype(F32)
    own_mask = ((lane >= own) & (lane < 2 * own)).astype(F32)

    @pl.when(pl.program_id(0) == 0)
    def _():
        logdet_ref[...] = jnp.zeros_like(logdet_ref)

    def mask_of(origin, block):
        row = origin + block * GROUP + lane // channels + first
        return ((row >= 0) & (row < height)).astype(F32)

    halves = [lat_ref[0, 0], lat_ref[0, 1]]
    for layer, (wf, wl) in enumerate(((wf_a, wl_a), (wf_b, wl_b))):
        plan = PLAN[layer]
        out_h1, out_h2, out_s1, out_s2, out_log = saved[5 * layer : 5 * layer + 5]
        cond, target = halves[layer], halves[1 - layer]
        if layer == 1:
            saved[10][0] = cond
        high, low = split(taps(cond))
        both = jnp.concatenate([high, low], axis=1)
        for k in range(plan["n1"]):
            if k % 2 == 0:
                lanes = blk(k, min(2, plan["n1"] - k))
                pair = dot(both, wf[: 2 * LANE, lanes]) + dot(high, wf[2 * LANE :, lanes])
            pre = pair[:, blk(k % 2)] + bf_ref[layer : layer + 1]
            sig = 0.5 + 0.5 * jnp.tanh(0.5 * pre)
            mask = mask_of(plan["o1"], k)
            hidden = pre * sig * mask
            start, count = plan["s1"]
            if start <= k < start + count:
                out_s1[0, :, blk(k - start)] = sig * (1.0 + pre * (1.0 - sig)) * mask
            plain = hidden.astype(BF)
            h0[:, blk(k)] = plain
            hm[:, blk(k)] = down(hidden).astype(BF)
            hp[:, blk(k)] = up(hidden).astype(BF)
            start, count = plan["h1"]
            if start <= k < start + count:
                out_h1[0, :, blk(k - start)] = plain
        for k in range(plan["n2"]):
            wide = min(2, plan["n1"] - k)
            pre = bm_ref[layer : layer + 1]
            for tap, part in enumerate((hm, h0, hp)):
                pre = pre + dot(part[:, blk(k, wide)], wm_ref[layer, tap, : wide * LANE])
            sig = 0.5 + 0.5 * jnp.tanh(0.5 * pre)
            mask = mask_of(plan["o2"], k)
            hidden = (pre * sig * mask).astype(BF)
            start, count = plan["s2"]
            if start <= k < start + count:
                out_s2[0, :, blk(k - start)] = sig * (1.0 + pre * (1.0 - sig)) * mask
            h2s[:, blk(k)] = hidden
            start, count = plan["h2"]
            if start <= k < start + count:
                out_h2[0, :, blk(k - start)] = hidden
        terms = dot(h2s[:, blk(0, plan["n2"])], wl[...])
        raw = down(terms[:, blk(0)]) + terms[:, blk(1)] + up(terms[:, blk(2)])
        raw = raw + bl_ref[layer : layer + 1]
        log_scale = jnp.tanh(raw)
        out_log[0] = log_scale
        logdet_ref[...] += jnp.sum(log_scale * own_mask, axis=0, keepdims=True)
        halves[1 - layer] = (target * jnp.exp(log_scale) + pltpu.roll(raw, LANE // 2, 1)) * image_mask
    cols = halves[0].shape[0]
    acc = None
    for side in range(2):
        mine = pltpu.roll(halves[side], LANE - own, 1).T
        img_ref[0, :, side * cols : (side + 1) * cols] = mine[:own]
        part = split(mine[:16])
        rows = slice(side * cols, (side + 1) * cols)
        term = dot3(part, (basis_ref[0, rows], basis_ref[1, rows]), ((1,), (0,)))
        acc = term if acc is None else acc + term
    col_ref[0] = acc[:own]


def backward_kernel(height, own, channels, reach, cells, r_ref, near_ref, lat_ref, loss_ref, wf_a, wf_b, wt_ref,
                    wl_a, wl_b, basis_ref, *rest):
    saved, out_ref, scratch = rest[:11], rest[11], rest[12:]
    near_s, dm, d0, dp, cpo_s, acc_mid, acc_last, acc_first, acc_bias = scratch
    step = pl.program_id(0)
    first = r_ref[0] * own
    lane = lane_ids(LANE)
    image_row = lane - own + first
    image_mask = ((lane < 3 * own) & (image_row >= 0) & (image_row < height)).astype(F32)
    raw_row = lane % (LANE // 2)
    own_mask = ((raw_row >= own) & (raw_row < 2 * own)).astype(F32)

    @pl.when(step == 0)
    def _():
        near_s[...] = jnp.zeros_like(near_s)
        for ref in (acc_mid, acc_last, acc_first, acc_bias):
            ref[...] = jnp.zeros_like(ref)

    def own_of(origin, block):
        row = origin + block * GROUP + lane // channels
        return ((row >= 0) & (row < own)).astype(F32)

    near_s[own - reach : 2 * own + reach, :] = near_ref[0]
    near = split(near_s[...])
    cols = lat_ref.shape[2]
    cots = []
    for side in range(2):
        rows = slice(side * cols, (side + 1) * cols)
        cots.append(dot3((basis_ref[0, rows], basis_ref[1, rows]), near, NT))
    cond_one = saved[10][0]
    for layer, wf, wl in ((1, wf_b, wl_b), (0, wf_a, wl_a)):
        plan = PLAN[layer]
        h1, h2, s1, s2, log_ref = saved[5 * layer : 5 * layer + 5]
        cond = cond_one if layer == 1 else lat_ref[0, 0]
        target = lat_ref[0, 1 - layer]
        cot_new = cots[1 - layer]
        log_scale = log_ref[0]
        cot_log = cot_new * target * jnp.exp(log_scale) - 1.0 / cells
        scale_part = cot_log * (1.0 - log_scale * log_scale) * image_mask
        raw = scale_part + pltpu.roll(cot_new * image_mask, LANE // 2, 1)
        raw = raw.astype(BF).astype(F32)
        mine = raw * own_mask
        spread = jnp.concatenate([up(raw).astype(BF), raw.astype(BF), down(raw).astype(BF)], 1)
        spread_own = jnp.concatenate([up(mine).astype(BF), mine.astype(BF), down(mine).astype(BF)], 1)
        acc_last[layer] += dot(spread_own, h2[0], TN)
        acc_bias[layer, 2:3] += jnp.sum(mine, axis=0, keepdims=True)
        start2, count2 = plan["s2"]
        base1, _ = plan["h1"]
        for k in range(start2, start2 + count2):
            cot = dot(spread, wl[blk(k), :], NT) * s2[0, :, blk(k - start2)]
            plain = cot.astype(BF)
            cot = plain.astype(F32)
            parts = (up(cot).astype(BF), plain, down(cot).astype(BF))
            for ref, part in zip((dm, d0, dp), parts):
                ref[:, blk(k - start2)] = part
            local = k - base1
            if 0 <= local < 4:
                mask = own_of(plan["o2"], k)
                acc_bias[layer, 1:2] += jnp.sum(cot * mask, axis=0, keepdims=True)
                lhs = jnp.concatenate([part * mask.astype(BF) for part in parts], 1)
                acc_mid[layer] += dot(lhs, h1[0, :, blk(local, 2)], TN)
        high, low = split(taps(cond))
        start1, count1 = plan["s1"]
        for k in range(start1, start1 + count1):
            back = min(1, k - start2)
            cot = None
            for tap, ref in enumerate((dm, d0, dp)):
                term = dot(ref[:, blk(k - start2 - back, 1 + back)], wt_ref[layer, tap, (1 - back) * LANE :])
                cot = term if cot is None else cot + term
            plain = (cot * s1[0, :, blk(k - start1)]).astype(BF)
            cpo_s[:, blk(k - start1)] = plain
            if k - start1 < 4:
                mask = own_of(plan["o1"], k)
                mine = plain.astype(F32) * mask
                acc_bias[layer, 0:1] += jnp.sum(mine, axis=0, keepdims=True)
                mine = mine.astype(BF)
                acc_first[layer, :, blk(k - start1)] += dot(high, mine, TN) + dot(low, mine, TN)
        if layer == 1:
            full = cpo_s[:, blk(0, count1)]
            lanes = blk(start1, count1)
            terms = dot(full, wf[:LANE, lanes], NT) + dot(full, wf[2 * LANE :, lanes], NT)
            total = up(terms) + pltpu.roll(terms, LANE - SLOT, 1) * (lane < SLOT).astype(F32)
            total = jnp.where(lane < SLOT, total, 0.0)
            total = total + jnp.where(lane < SLOT, pltpu.roll(down(terms), LANE - 2 * SLOT, 1), 0.0)
            cots[1] = cots[1] + total

    @pl.when(step == pl.num_programs(0) - 1)
    def _():
        out_ref[...] = jnp.zeros_like(out_ref)
        layers = len(PLAN)
        tail = layers * 3 * channels
        fold_row = lax.broadcasted_iota(jnp.int32, (4 * LANE, channels), 0)
        fold_col = lax.broadcasted_iota(jnp.int32, (4 * LANE, channels), 1)
        fold = (fold_row % channels == fold_col).astype(F32)
        hi = lax.Precision.HIGHEST

        def folded(x):
            return jnp.dot(x, fold[: x.shape[1]], precision=hi, preferred_element_type=F32)

        def by_row(ref_value, groups, size, shift):
            shape = (groups * size, 4 * LANE)
            inner = lax.broadcasted_iota(jnp.int32, shape, 0) % size
            row = lax.broadcasted_iota(jnp.int32, shape, 1) // channels
            kept = jnp.where(row - inner == shift, ref_value, 0.0)
            return folded(jnp.sum(kept.reshape(groups, size, 4 * LANE), axis=1))

        for layer, plan in enumerate(PLAN):
            for dr in range(3):
                at = (layer * 3 + dr) * channels
                for dc in range(3):
                    total = None
                    for r in range(GROUP):
                        piece = acc_mid[layer, dc * LANE + r * channels : dc * LANE + (r + 1) * channels,
                                        (r + dr) * channels : (r + dr + 1) * channels]
                        total = piece if total is None else total + piece
                    out_ref[at : at + channels, dc * channels : (dc + 1) * channels] = total
                at = tail + (layer * 3 + dr) * 8
                shift = dr - 1 - own - plan["o2"] - GROUP * plan["h2"][0]
                out_ref[at : at + 6, :channels] = by_row(acc_last[layer], 6, LANE // 2, shift)
                shift = 1 - dr - own - plan["o1"] - GROUP * plan["s1"][0]
                out_ref[at : at + 3, channels : 2 * channels] = by_row(
                    acc_first[layer, : 3 * SLOT], 3, SLOT, shift)
            at = tail + layer * 24
            out_ref[at : at + 2, 2 * channels : 3 * channels] = folded(acc_bias[layer, 0:2])
            bias = acc_bias[layer, 2:3]
            pick = lane_ids(channels)
            low = jnp.sum(jnp.where(lane < LANE // 2, bias, 0.0), axis=1, keepdims=True)
            top = jnp.sum(jnp.where(lane >= LANE // 2, bias, 0.0), axis=1, keepdims=True)
            out_ref[at + 2 : at + 3, 2 * channels : 3 * channels] = jnp.where(
                pick == 0, low, jnp.where(pick == 1, top, jnp.where(pick == 2, loss_ref[...], 0.0)))


def prepare_kernel(own, first_ref, mid_ref, last_ref, bf_ref, bm_ref, bl_ref, wf_a, wf_b, wm_ref, wt_ref, wl_a, wl_b,
                   bf_out, bm_out, bl_out):
    channels = mid_ref.shape[2]
    lane = lane_ids(LANE)

    def tiled(x):
        return jnp.concatenate([x] * GROUP, axis=1)

    bf_out[...] = tiled(bf_ref[...])
    bm_out[...] = tiled(bm_ref[...])
    bl_out[...] = jnp.where(lane < LANE // 2, bl_ref[:, 0:1], bl_ref[:, 1:2])
    spread = (lax.broadcasted_iota(jnp.int32, (channels, LANE), 0) == lane % channels).astype(BF)
    parts = lax.broadcasted_iota(jnp.int32, (8, 3 * LANE), 0)
    parts = (parts == lax.broadcasted_iota(jnp.int32, (8, 3 * LANE), 1) // (LANE // 2)).astype(BF)
    wide_lane = lane_ids(3 * LANE) % (LANE // 2)
    edge = lax.broadcasted_iota(jnp.int32, (SLOT, LANE), 0)
    for layer, (wf, wl) in enumerate(((wf_a, wl_a), (wf_b, wl_b))):
        plan = PLAN[layer]
        rows = tiled(first_ref[layer])
        for k in range(plan["n1"]):
            row = k * GROUP + lane // channels + plan["o1"] + own - 1
            pieces = []
            for dc in range(3):
                total = jnp.zeros((SLOT, LANE), F32)
                for dr in range(3):
                    hit = (edge == row + dr) & (edge < 3 * own)
                    total = total + jnp.where(hit, rows[3 * dr + dc : 3 * dr + dc + 1], 0.0)
                pieces.append(total)
            pieces.append(jnp.zeros((LANE - 3 * SLOT, LANE), F32))
            high, low = split(jnp.concatenate(pieces, axis=0))
            wf[:LANE, blk(k)] = high
            wf[LANE : 2 * LANE, blk(k)] = high
            wf[2 * LANE :, blk(k)] = low
        for dc in range(3):
            taps_t = [dot(mid_ref[layer, 3 * dr + dc], spread, TN) for dr in range(3)]
            band = []
            for row in range(2 * GROUP):
                total = jnp.zeros((channels, LANE), F32)
                for dr in range(3):
                    if 0 <= row - dr < GROUP:
                        total = total + jnp.where(lane // channels == row - dr, taps_t[dr], 0.0)
                band.append(total)
            top = jnp.concatenate(band[:GROUP], axis=0)
            low = jnp.concatenate(band[GROUP:], axis=0)
            wm_ref[layer, dc, :LANE] = top.astype(BF)
            wm_ref[layer, dc, LANE:] = low.astype(BF)
            wt_ref[layer, dc, :LANE] = low.T.astype(BF)
            wt_ref[layer, dc, LANE:] = top.T.astype(BF)
        columns = [dot(last_ref[layer, dr], parts, TN) for dr in range(3)]
        for row in range(plan["n2"] * GROUP):
            total = jnp.zeros((channels, 3 * LANE), F32)
            for dr in range(3):
                hit = (wide_lane == row + own + 1 - dr + plan["o2"]) & (wide_lane < 3 * own)
                total = total + jnp.where(hit, columns[dr], 0.0)
            wl[row * channels : (row + 1) * channels, :] = total.astype(BF)


def prepared(w_first, w_mid, w_last, b_first, b_mid, b_last, own):
    layers, channels = b_first.shape
    last = jnp.pad(w_last.reshape(layers, 3, 6, channels), ((0, 0), (0, 0), (0, 2), (0, 0)))
    vmem = pl.BlockSpec(memory_space=pltpu.VMEM)
    shapes = [((3 * LANE, plan["n1"] * LANE), BF) for plan in PLAN]
    shapes += [((layers, 3, 2 * LANE, LANE), BF)] * 2
    shapes += [((plan["n2"] * LANE, 3 * LANE), BF) for plan in PLAN]
    shapes += [((layers, LANE), F32)] * 3
    return pl.pallas_call(
        functools.partial(prepare_kernel, own),
        out_shape=tuple(jax.ShapeDtypeStruct(shape, kind) for shape, kind in shapes),
        in_specs=[vmem] * 6,
        out_specs=tuple(vmem for shape in shapes),
        compiler_params=pltpu.CompilerParams(vmem_limit_bytes=48 * 2**20),
    )(w_first.reshape(layers, 9, channels), w_mid, last, b_first, b_mid, b_last)


def butterfly(value):
    for axis in ("grp", "rows"):
        count = lax.axis_size(axis)
        hop = 1
        while hop < count:
            value = value + lax.ppermute(value, axis, [(i, i ^ hop) for i in range(count)])
            hop *= 2
    return value


def grid_kernel(n_freq, pad_freq, height, img_width, r_ref, u_ref, v_ref, obs_ref, w_ref, sel_ref,
                out_ref, const_ref, u_s, c_s, f_s, acc):
    steps, width = u_ref.shape
    half = img_width // 2
    base = r_ref[0] * n_freq
    u = u_ref[...]
    v = v_ref[...]
    mirror = v > half
    v_fold = jnp.where(mirror, img_width - v, v)
    u_fold = jnp.where(mirror, jnp.where(u == 0, 0, height - u), u)
    col = v_fold - base
    col = jnp.where((col < 0) | (col >= n_freq), pad_freq, col)
    col = jnp.where(v_fold == half, n_freq, col)
    w = w_ref[...]
    o_re = obs_ref[0]
    o_im = obs_ref[1]
    const_ref[...] = jnp.sum(w * (o_re * o_re + o_im * o_im), axis=(0, 1), keepdims=True)
    u_s[...] = u_fold
    c_s[...] = col
    f_s[0] = w
    f_s[1] = w * o_re
    f_s[2] = w * jnp.where(mirror, -o_im, o_im)
    acc[...] = jnp.zeros_like(acc)
    ids = lax.broadcasted_iota(jnp.int32, (16, width), 0).astype(jnp.int16)
    one = jnp.ones((16, width), jnp.bfloat16)
    zero = jnp.zeros((16, width), jnp.bfloat16)

    def step(j, carry):
        row = pl.ds(j, 1)
        u_row = jnp.broadcast_to(u_s[row, :], (16, width)).astype(jnp.int16)
        u_hot = [jnp.where(ids + jnp.int16(16 * g) == u_row, one, zero) for g in range(height // 16)]
        u_hot = jnp.concatenate(u_hot, axis=0)
        c_hot = lax.broadcasted_iota(jnp.int32, (pad_freq, width), 0) == c_s[row, :]
        parts = []
        for field in range(3):
            full = f_s[field, row, :]
            high = full.astype(jnp.bfloat16).astype(jnp.float32)
            parts.append(jnp.where(c_hot, high, 0.0).astype(jnp.bfloat16))
            parts.append(jnp.where(c_hot, full - high, 0.0).astype(jnp.bfloat16))
        values = jnp.concatenate(parts, axis=0)
        acc[...] += lax.dot_general(u_hot, values, (((1,), (1,)), ((), ())),
                                    preferred_element_type=jnp.float32)
        return carry

    lax.fori_loop(0, steps, step, 0)
    grid = acc[...]
    for field in range(3):
        out_ref[field] = jnp.dot(grid, sel_ref[field], precision=lax.Precision.HIGHEST,
                                 preferred_element_type=jnp.float32)


def gridded_lanes(vis_u, vis_v, observed, vis_weight, samples, height, img_width, n_rows):
    n_freq = img_width // 2 // n_rows
    pad_freq = 8 * ((n_freq + 8) // 8)
    lanes = 2 * samples * n_freq
    sel = np.zeros((2, 3, 6 * pad_freq, lanes), np.float32)
    for special in range(2):
        for lane in range(lanes):
            part, freq = lane // (samples * n_freq), lane % n_freq
            lone = special == 1 and freq == 0
            slot = n_freq if lone and part == 1 else freq
            fields = (0, 1, 2) if lone else (0, 1 + part, None)
            for out_id, field in enumerate(fields):
                if field is not None:
                    for split in range(2):
                        sel[special, out_id, (2 * field + split) * pad_freq + slot, lane] = 1.0
    index = lax.axis_index("rows")
    chosen = jnp.where(index == 0, jnp.asarray(sel[1]), jnp.asarray(sel[0]))
    width = min(2048, vis_u.shape[0])
    steps = vis_u.shape[0] // width
    vmem = pl.BlockSpec(memory_space=pltpu.VMEM)
    return pl.pallas_call(
        functools.partial(grid_kernel, n_freq, pad_freq, height, img_width),
        out_shape=(jax.ShapeDtypeStruct((3, height, lanes), jnp.float32),
                   jax.ShapeDtypeStruct((1, 1), jnp.float32)),
        in_specs=[pl.BlockSpec(memory_space=pltpu.SMEM)] + [vmem] * 5,
        out_specs=(vmem, vmem),
        scratch_shapes=[pltpu.VMEM((steps, width), jnp.int32), pltpu.VMEM((steps, width), jnp.int32),
                        pltpu.VMEM((3, steps, width), jnp.float32),
                        pltpu.VMEM((height, 6 * pad_freq), jnp.float32)],
        compiler_params=pltpu.CompilerParams(vmem_limit_bytes=48 * 2**20),
        cost_estimate=pl.CostEstimate(flops=2 * height * 256 * vis_u.shape[0],
                                      bytes_accessed=24 * vis_u.shape[0], transcendentals=0),
    )(index[None].astype(jnp.int32), vis_u.reshape(steps, width), vis_v.reshape(steps, width),
      observed.reshape(2, steps, width), vis_weight.reshape(steps, width), chosen)


def column_basis(img_width, n_rows):
    n_freq = img_width // 2 // n_rows
    cols = np.arange(img_width)
    freq = np.arange(img_width // 2)
    angle = 2.0 * np.pi * ((cols[:, None] * freq[None, :]) % img_width) / img_width
    re, im = np.cos(angle), -np.sin(angle)
    im[:, 0] = 1.0 - 2.0 * (cols % 2)
    both = np.stack([re.reshape(img_width, n_rows, n_freq), im.reshape(img_width, n_rows, n_freq)], 2)
    return both.reshape(img_width, img_width).astype(np.float32)


def spectral_kernel(scale, factor, half, n_freq, r_ref, z_ref, cs_ref, grid_ref, near_ref, data_ref):
    height, lanes = z_ref.shape
    lane = lax.broadcasted_iota(jnp.int32, (1, lanes), 1)
    lone = ((lane % n_freq) == 0) & (r_ref[0] == 0)
    sign = jnp.where(lane < half, 1.0, -1.0)
    hi = lax.Precision.HIGHEST
    z = z_ref[...] * scale
    a = jnp.dot(cs_ref[0], z, precision=hi, preferred_element_type=jnp.float32)
    b = jnp.dot(cs_ref[1], z, precision=hi, preferred_element_type=jnp.float32)
    w, t1, t2 = grid_ref[0], grid_ref[1], grid_ref[2]

    def swap(x):
        return jnp.concatenate([x[:, half:], x[:, :half]], axis=1)

    x = jnp.where(lone, a, a + sign * swap(b))
    p = w * x - t1
    q = jnp.where(lone, w * b + t2, -sign * swap(p))
    b_lone = jnp.where(lone, b, 0.0)
    terms = w * (x * x + b_lone * b_lone) - 2.0 * (x * t1 - b_lone * t2)
    data_ref[...] = jnp.sum(terms, axis=(0, 1), keepdims=True)
    near = jnp.dot(cs_ref[2], p, precision=hi, preferred_element_type=jnp.float32)
    near = near + jnp.dot(cs_ref[3], q, precision=hi, preferred_element_type=jnp.float32)
    near_ref[...] = near * (factor * scale)


def spectral(z, lanes_grid, scale, factor, samples):
    height, lanes = z.shape
    ids = np.arange(height)
    angle = 2.0 * np.pi * ((ids[:, None] * ids[None, :]) % height) / height
    cs = np.stack([np.cos(angle), np.sin(angle), np.cos(angle), np.sin(angle)]).astype(np.float32)
    vmem = pl.BlockSpec(memory_space=pltpu.VMEM)
    return pl.pallas_call(
        functools.partial(spectral_kernel, scale, factor, lanes // 2, lanes // (2 * samples)),
        out_shape=(jax.ShapeDtypeStruct((height, lanes), jnp.float32),
                   jax.ShapeDtypeStruct((1, 1), jnp.float32)),
        in_specs=[pl.BlockSpec(memory_space=pltpu.SMEM)] + [vmem] * 3,
        out_specs=(vmem, vmem),
        compiler_params=pltpu.CompilerParams(vmem_limit_bytes=48 * 2**20),
    )(lax.axis_index("rows")[None].astype(jnp.int32), z, jnp.asarray(cs), lanes_grid)


def body(
    latent, w_first, b_first, w_mid, b_mid, w_last, b_last, vis_u, vis_v, observed, vis_weight
):
    samples, row_count, img_width = latent.shape
    half_cols = img_width // 2
    n_rows = lax.axis_size("rows")
    n_grp = lax.axis_size("grp")
    height = row_count * n_rows
    batch_size = samples * n_grp
    layers = w_first.shape[0]
    vis_total = vis_u.shape[0]
    cells = height * img_width
    lanes_grid, obs_const = gridded_lanes(
        vis_u, vis_v, observed, vis_weight, samples, height, img_width, n_rows
    )
    channels = w_mid.shape[2]
    half = half_cols
    forward = [(i, i + 1) for i in range(n_rows - 1)]
    backward = [(target, source) for source, target in forward]
    low = lax.ppermute(latent, "rows", forward)
    high = lax.ppermute(latent, "rows", backward)
    wide = jnp.concatenate([low, latent, high], axis=1)
    wide = wide.reshape(samples, 3 * row_count, 2, half).transpose(0, 2, 3, 1)
    wide = jnp.pad(wide, ((0, 0), (0, 0), (0, 0), (0, LANE - 3 * row_count)))
    wf_a, wf_b, wm, wt, wl_a, wl_b, bias_first, bias_mid, bias_last = prepared(
        w_first, w_mid, w_last, b_first, b_mid, b_last, row_count
    )
    basis_np = column_basis(img_width, n_rows)
    basis_high = basis_np.astype(BF)
    basis_low = (basis_np - basis_high.astype(np.float32)).astype(BF)
    basis = jnp.asarray(np.stack([basis_high, basis_low]))
    index = lax.axis_index("rows")[None].astype(jnp.int32)
    smem = pl.BlockSpec(memory_space=pltpu.SMEM)

    def whole(value):
        rank = value.ndim
        return pl.BlockSpec(value.shape, lambda s: (0,) * rank)

    def per_sample(*shape):
        rank = len(shape)
        return pl.BlockSpec((1,) + shape, lambda s: (s,) + (0,) * rank)

    saved_shapes = []
    for plan in PLAN:
        for key, kind in (("h1", BF), ("h2", BF), ("s1", F32), ("s2", F32)):
            saved_shapes.append(((half, plan[key][1] * LANE), kind))
        saved_shapes.append(((half, LANE), F32))
    saved_shapes.append(((half, LANE), F32))
    saved_specs = [per_sample(*shape) for shape, kind in saved_shapes]
    saved_types = [jax.ShapeDtypeStruct((samples,) + shape, kind) for shape, kind in saved_shapes]
    weights = (wf_a, wf_b, bias_first, wm, bias_mid, wl_a, wl_b, bias_last, basis)
    max1 = max(plan["n1"] for plan in PLAN) * LANE
    max2 = max(plan["n2"] for plan in PLAN) * LANE
    params = pltpu.CompilerParams(vmem_limit_bytes=56 * 2**20)
    image_out, columns, logdet, *saved = pl.pallas_call(
        functools.partial(forward_kernel, height, row_count, channels),
        grid=(samples,),
        out_shape=(
            jax.ShapeDtypeStruct((samples, row_count, img_width), F32),
            jax.ShapeDtypeStruct((samples, row_count, img_width), F32),
            jax.ShapeDtypeStruct((1, LANE), F32),
            *saved_types,
        ),
        in_specs=[smem, per_sample(2, half, LANE)] + [whole(value) for value in weights],
        out_specs=(
            per_sample(row_count, img_width),
            per_sample(row_count, img_width),
            pl.BlockSpec((1, LANE), lambda s: (0, 0)),
            *saved_specs,
        ),
        scratch_shapes=[pltpu.VMEM((half, max1), BF)] * 3 + [pltpu.VMEM((half, max2), BF)],
        compiler_params=params,
    )(index, wide, *weights)
    logdet = jnp.sum(logdet)
    norm_scale = 1.0 / math.sqrt(height * img_width)
    factor = 2.0 / (vis_total * batch_size)
    n_freq = img_width // 2 // n_rows
    columns = columns.reshape(samples, row_count, n_rows, 2, n_freq).transpose(2, 1, 3, 0, 4)
    columns = columns.reshape(n_rows, row_count, 2 * samples * n_freq)
    columns = lax.all_to_all(columns, "rows", 0, 0, tiled=True)
    near, data_sum = spectral(
        columns.reshape(height, 2 * samples * n_freq), lanes_grid, norm_scale, factor, samples
    )
    reach = 6
    blocks = jnp.pad(near.reshape(n_rows, row_count, -1), ((1, 1), (0, 0), (0, 0)))
    blocks = jnp.concatenate(
        [blocks[:-2, row_count - reach :], blocks[1:-1], blocks[2:, :reach]], axis=1
    )
    near = lax.all_to_all(blocks, "rows", 0, 0, tiled=True)
    span = row_count + 2 * reach
    near = near.reshape(n_rows, span, 2, samples, n_freq).transpose(3, 1, 0, 2, 4)
    near = near.reshape(samples, span, img_width)
    data_part = (data_sum[0, 0] + samples * obs_const[0, 0] / n_rows) / vis_total
    loss_part = (data_part - logdet / (height * img_width)) / batch_size
    out_rows = layers * (3 * channels + 24)
    weights = (wf_a, wf_b, wt, wl_a, wl_b, basis)
    flat = pl.pallas_call(
        functools.partial(
            backward_kernel, height, row_count, channels, reach, batch_size * cells
        ),
        grid=(samples,),
        out_shape=jax.ShapeDtypeStruct((out_rows, LANE), F32),
        in_specs=[smem, per_sample(span, img_width), per_sample(2, half, LANE),
                  pl.BlockSpec((1, 1), lambda s: (0, 0))]
        + [whole(value) for value in weights] + saved_specs,
        out_specs=pl.BlockSpec((out_rows, LANE), lambda s: (0, 0)),
        scratch_shapes=[
            pltpu.VMEM((LANE, img_width), F32),
            *[pltpu.VMEM((half, max2), BF)] * 3,
            pltpu.VMEM((half, max1), BF),
            pltpu.VMEM((layers, 3 * LANE, 2 * LANE), F32),
            pltpu.VMEM((layers, 3 * LANE, 4 * LANE), F32),
            pltpu.VMEM((layers, LANE, 4 * LANE), F32),
            pltpu.VMEM((layers, 8, LANE), F32),
        ],
        compiler_params=params,
    )(index, near, wide, loss_part.reshape(1, 1), *weights, *saved)
    flat = butterfly(flat)
    main = flat[: layers * 3 * channels, : 3 * channels]
    main = main.reshape(layers, 3, channels, 3, channels).transpose(0, 1, 3, 2, 4)
    rest = flat[layers * 3 * channels :].reshape(layers, 3, 8, LANE)
    final_grads = [
        rest[:, :, :3, channels : 2 * channels].reshape(layers, 9, channels, 1),
        main.reshape(layers, 9, channels, channels),
        rest[:, :, :6, :channels].reshape(layers, 9, 2, channels),
        rest[:, 0, 0, 2 * channels : 3 * channels],
        rest[:, 0, 1, 2 * channels : 3 * channels],
        rest[:, 0, 2, 2 * channels : 2 * channels + 2],
    ]
    loss = rest[0, 0, 2, 2 * channels + 2]
    return (
        image_out,
        loss,
        final_grads[0],
        final_grads[1],
        final_grads[2],
        final_grads[3],
        final_grads[4],
        final_grads[5],
    )


def solution(mesh):
    in_specs = (P("grp", "rows", None), P(), P(), P(), P(), P(), P(), P(), P(), P(), P())
    out_specs = (P("grp", "rows", None), P(), P(), P(), P(), P(), P(), P())
    return jax.shard_map(body, mesh=mesh, in_specs=in_specs, out_specs=out_specs, check_vma=False)
```

```python
import functools
import math

import jax
import jax.numpy as jnp
import numpy as np
from jax import lax
from jax.experimental import pallas as pl
from jax.experimental.pallas import tpu as pltpu
from jax.sharding import PartitionSpec as P


BF = jnp.bfloat16
F32 = jnp.float32
GROUP = 4
LANE = 128
SLOT = 40
PLAN = (
    dict(o1=-10, n1=8, o2=-9, n2=8, h1=(2, 5), h2=(2, 4), s1=(2, 4), s2=(2, 4)),
    dict(o1=-7, n1=7, o2=-6, n2=6, h1=(1, 5), h2=(1, 4), s1=(1, 5), s2=(0, 6)),
)


def dot(a, b, dims=((1,), (0,))):
    return lax.dot_general(a, b, (dims, ((), ())), preferred_element_type=F32)


NT = ((1,), (1,))
TN = ((0,), (0,))


def split(x):
    high = x.astype(BF)
    return high, (x - high.astype(F32)).astype(BF)


def dot3(a, b, dims):
    return dot(a[0], b[0], dims) + dot(a[1], b[0], dims) + dot(a[0], b[1], dims)


def down(x):
    rows = lax.broadcasted_iota(jnp.int32, x.shape, 0)
    return jnp.where(rows == 0, 0.0, pltpu.roll(x, 1, 0))


def up(x):
    rows = lax.broadcasted_iota(jnp.int32, x.shape, 0)
    return jnp.where(rows == x.shape[0] - 1, 0.0, pltpu.roll(x, x.shape[0] - 1, 0))


def lane_ids(count):
    return lax.broadcasted_iota(jnp.int32, (1, count), 1)


def taps(cond):
    return down(cond) + pltpu.roll(cond, SLOT, 1) + pltpu.roll(up(cond), 2 * SLOT, 1)


def blk(start, count=1):
    return slice(start * LANE, (start + count) * LANE)


def forward_kernel(height, own, channels, r_ref, low_ref, mid_ref, high_ref, first_ref, taps_ref, last_ref, b1_ref,
                   b2_ref, b3_ref, basis_ref, img_ref, col_ref, logdet_ref, wf_a, wf_b, wt_ref, wl_a, wl_b, *rest):
    saved, scratch = rest[:-11], rest[-11:]
    wm_ref, bf_ref, bm_ref, bl_ref, hm, h0, hp, h2s, wide_s, lat_s, mine_s = scratch
    step = pl.program_id(0)
    samples, cols = lat_s.shape[0], lat_s.shape[2]
    first = r_ref[0] * own
    lane = lane_ids(LANE)
    image_row = lane - own + first
    image_mask = ((lane < 3 * own) & (image_row >= 0) & (image_row < height)).astype(F32)
    own_mask = ((lane >= own) & (lane < 2 * own)).astype(F32)

    @pl.when(step == 0)
    def _():
        logdet_ref[...] = jnp.zeros_like(logdet_ref)
        prepare(own, first_ref, taps_ref, last_ref, b1_ref, b2_ref, b3_ref, wf_a, wf_b, wm_ref, wt_ref, wl_a, wl_b,
                bf_ref, bm_ref, bl_ref)
        wide_s[...] = jnp.zeros_like(wide_s)
        for s in range(samples):
            for place, ref in enumerate((low_ref, mid_ref, high_ref)):
                wide_s[place * own : (place + 1) * own, :] = ref[:, s, :]
            turned = wide_s[...].T
            for side in range(2):
                lat_s[s, side] = turned[side * cols : (side + 1) * cols]

    def mask_of(origin, block):
        row = origin + block * GROUP + lane // channels + first
        return ((row >= 0) & (row < height)).astype(F32)

    halves = [lat_s[step, 0], lat_s[step, 1]]
    for side in range(2):
        saved[11][0, side] = halves[side]
    for layer, (wf, wl) in enumerate(((wf_a, wl_a), (wf_b, wl_b))):
        plan = PLAN[layer]
        out_h1, out_h2, out_s1, out_s2, out_log = saved[5 * layer : 5 * layer + 5]
        cond, target = halves[layer], halves[1 - layer]
        if layer == 1:
            saved[10][0] = cond
        high, low = split(taps(cond))
        both = jnp.concatenate([high, low], axis=1)
        for k in range(plan["n1"]):
            if k % 2 == 0:
                lanes = blk(k, min(2, plan["n1"] - k))
                pair = dot(both, wf[: 2 * LANE, lanes]) + dot(high, wf[2 * LANE :, lanes])
            pre = pair[:, blk(k % 2)] + bf_ref[layer : layer + 1]
            sig = 0.5 + 0.5 * jnp.tanh(0.5 * pre)
            mask = mask_of(plan["o1"], k)
            hidden = pre * sig * mask
            start, count = plan["s1"]
            if start <= k < start + count:
                out_s1[0, :, blk(k - start)] = (sig * (1.0 + pre * (1.0 - sig)) * mask).astype(BF)
            plain = hidden.astype(BF)
            h0[:, blk(k)] = plain
            hm[:, blk(k)] = down(hidden).astype(BF)
            hp[:, blk(k)] = up(hidden).astype(BF)
            start, count = plan["h1"]
            if start <= k < start + count:
                out_h1[0, :, blk(k - start)] = plain
        for k in range(plan["n2"]):
            wide = min(2, plan["n1"] - k)
            pre = bm_ref[layer : layer + 1]
            for tap, part in enumerate((hm, h0, hp)):
                pre = pre + dot(part[:, blk(k, wide)], wm_ref[layer, tap, : wide * LANE])
            sig = 0.5 + 0.5 * jnp.tanh(0.5 * pre)
            mask = mask_of(plan["o2"], k)
            hidden = (pre * sig * mask).astype(BF)
            start, count = plan["s2"]
            if start <= k < start + count:
                out_s2[0, :, blk(k - start)] = (sig * (1.0 + pre * (1.0 - sig)) * mask).astype(BF)
            h2s[:, blk(k)] = hidden
            start, count = plan["h2"]
            if start <= k < start + count:
                out_h2[0, :, blk(k - start)] = hidden
        terms = dot(h2s[:, blk(0, plan["n2"])], wl[...])
        raw = down(terms[:, blk(0)]) + terms[:, blk(1)] + up(terms[:, blk(2)])
        raw = raw + bl_ref[layer : layer + 1]
        log_scale = jnp.tanh(raw)
        out_log[0] = log_scale
        logdet_ref[...] += jnp.sum(log_scale * own_mask, axis=0, keepdims=True)
        halves[1 - layer] = (target * jnp.exp(log_scale) + pltpu.roll(raw, LANE // 2, 1)) * image_mask
    for side in range(2):
        mine = pltpu.roll(halves[side], LANE - own, 1).T
        mine_s[step, :, side * cols : (side + 1) * cols] = mine[:16]

    @pl.when(step == samples - 1)
    def _():
        for s in range(samples):
            img_ref[:, s, :] = mine_s[s, :own]
        image = split(mine_s[...].reshape(samples * 16, 2 * cols))
        spectrum = dot3(image, (basis_ref[0], basis_ref[1]), ((1,), (0,)))
        blocks, _, lanes = col_ref.shape
        n_freq = lanes // (2 * samples)
        for d in range(blocks):
            chunk, offset = divmod(d * n_freq, LANE)
            total = jnp.zeros((16, LANE), F32)
            for part in range(2):
                for s in range(samples):
                    at = (part * samples + s) * n_freq
                    piece = spectrum[s * 16 : (s + 1) * 16, blk(part * (cols // LANE) + chunk)]
                    if at != offset:
                        piece = pltpu.roll(piece, (at - offset) % LANE, 1)
                    total = jnp.where((lane >= at) & (lane < at + n_freq), piece, total)
            col_ref[d] = total[:own, :lanes]


def backward_kernel(height, own, channels, reach, cells, r_ref, near_ref, loss_ref, wf_a, wf_b, wt_ref,
                    wl_a, wl_b, basis_ref, *rest):
    saved, lat_ref, out_ref, scratch = rest[:11], rest[11], rest[12], rest[13:]
    near_s, cot_s, dm, d0, dp, cpo_s, acc_mid, acc_last, acc_first, acc_bias = scratch
    step = pl.program_id(0)
    first = r_ref[0] * own
    lane = lane_ids(LANE)
    image_row = lane - own + first
    image_mask = ((lane < 3 * own) & (image_row >= 0) & (image_row < height)).astype(F32)
    raw_row = lane % (LANE // 2)
    own_mask = ((raw_row >= own) & (raw_row < 2 * own)).astype(F32)

    @pl.when(step == 0)
    def _():
        near_s[...] = jnp.zeros_like(near_s)
        blocks, span, lanes = near_ref.shape
        samples = pl.num_programs(0)
        n_freq = lanes // (2 * samples)
        per = LANE // n_freq
        for s in range(samples):
            for part in range(2):
                for chunk in range(blocks // per):
                    at = (part * samples + s) * n_freq
                    total = jnp.zeros((span, LANE), F32)
                    for i in range(per):
                        piece = near_ref[chunk * per + i]
                        if lanes < LANE:
                            piece = jnp.concatenate([piece] * (LANE // lanes), axis=1)
                        if at != i * n_freq:
                            piece = pltpu.roll(piece, (i * n_freq - at) % LANE, 1)
                        total = jnp.where((lane >= i * n_freq) & (lane < (i + 1) * n_freq), piece, total)
                    near_s[s * 32 : s * 32 + span, blk(part * (blocks // per) + chunk)] = total
        cot_s[...] = dot3((basis_ref[0], basis_ref[1]), split(near_s[...]), NT)
        for ref in (acc_mid, acc_last, acc_first, acc_bias):
            ref[...] = jnp.zeros_like(ref)

    def own_of(origin, block):
        row = origin + block * GROUP + lane // channels
        return ((row >= 0) & (row < own)).astype(F32)

    cols = lat_ref.shape[2]
    cots = []
    valid = (lane >= own - reach) & (lane < 2 * own + reach)
    shift = (own - reach + LANE - 32 * step) % LANE
    for side in range(2):
        cot = pltpu.roll(cot_s[side * cols : (side + 1) * cols, :], shift, 1)
        cots.append(jnp.where(valid, cot, 0.0))
    cond_one = saved[10][0]
    for layer, wf, wl in ((1, wf_b, wl_b), (0, wf_a, wl_a)):
        plan = PLAN[layer]
        h1, h2, s1, s2, log_ref = saved[5 * layer : 5 * layer + 5]
        cond = cond_one if layer == 1 else lat_ref[0, 0]
        target = lat_ref[0, 1 - layer]
        cot_new = cots[1 - layer]
        log_scale = log_ref[0]
        cot_log = cot_new * target * jnp.exp(log_scale) - 1.0 / cells
        scale_part = cot_log * (1.0 - log_scale * log_scale) * image_mask
        raw = scale_part + pltpu.roll(cot_new * image_mask, LANE // 2, 1)
        raw = raw.astype(BF).astype(F32)
        mine = raw * own_mask
        spread = jnp.concatenate([up(raw).astype(BF), raw.astype(BF), down(raw).astype(BF)], 1)
        spread_own = jnp.concatenate([up(mine).astype(BF), mine.astype(BF), down(mine).astype(BF)], 1)
        acc_last[layer] += dot(spread_own, h2[0], TN)
        acc_bias[layer, 2:3] += jnp.sum(mine, axis=0, keepdims=True)
        start2, count2 = plan["s2"]
        base1, _ = plan["h1"]
        for k in range(start2, start2 + count2):
            cot = dot(spread, wl[blk(k), :], NT) * s2[0, :, blk(k - start2)].astype(F32)
            plain = cot.astype(BF)
            cot = plain.astype(F32)
            parts = (up(cot).astype(BF), plain, down(cot).astype(BF))
            for ref, part in zip((dm, d0, dp), parts):
                ref[:, blk(k - start2)] = part
            local = k - base1
            if 0 <= local < 4:
                mask = own_of(plan["o2"], k)
                acc_bias[layer, 1:2] += jnp.sum(cot * mask, axis=0, keepdims=True)
                lhs = jnp.concatenate([part * mask.astype(BF) for part in parts], 1)
                acc_mid[layer] += dot(lhs, h1[0, :, blk(local, 2)], TN)
        high, low = split(taps(cond))
        start1, count1 = plan["s1"]
        for k in range(start1, start1 + count1):
            back = min(1, k - start2)
            cot = None
            for tap, ref in enumerate((dm, d0, dp)):
                term = dot(ref[:, blk(k - start2 - back, 1 + back)], wt_ref[layer, tap, (1 - back) * LANE :])
                cot = term if cot is None else cot + term
            plain = (cot * s1[0, :, blk(k - start1)].astype(F32)).astype(BF)
            cpo_s[:, blk(k - start1)] = plain
            if k - start1 < 4:
                mask = own_of(plan["o1"], k)
                mine = plain.astype(F32) * mask
                acc_bias[layer, 0:1] += jnp.sum(mine, axis=0, keepdims=True)
                mine = mine.astype(BF)
                acc_first[layer, :, blk(k - start1)] += dot(high, mine, TN) + dot(low, mine, TN)
        if layer == 1:
            full = cpo_s[:, blk(0, count1)]
            lanes = blk(start1, count1)
            terms = dot(full, wf[:LANE, lanes], NT) + dot(full, wf[2 * LANE :, lanes], NT)
            total = up(terms) + pltpu.roll(terms, LANE - SLOT, 1) * (lane < SLOT).astype(F32)
            total = jnp.where(lane < SLOT, total, 0.0)
            total = total + jnp.where(lane < SLOT, pltpu.roll(down(terms), LANE - 2 * SLOT, 1), 0.0)
            cots[1] = cots[1] + total

    @pl.when(step == pl.num_programs(0) - 1)
    def _():
        out_ref[...] = jnp.zeros_like(out_ref)
        layers = len(PLAN)
        side = slice(3 * channels, 4 * channels)
        fold_row = lax.broadcasted_iota(jnp.int32, (4 * LANE, channels), 0)
        fold_col = lax.broadcasted_iota(jnp.int32, (4 * LANE, channels), 1)
        fold = (fold_row % channels == fold_col).astype(F32)
        hi = lax.Precision.HIGHEST

        def folded(x):
            return jnp.dot(x, fold[: x.shape[1]], precision=hi, preferred_element_type=F32)

        def by_row(ref_value, groups, size, shift):
            shape = (groups * size, 4 * LANE)
            inner = lax.broadcasted_iota(jnp.int32, shape, 0) % size
            row = lax.broadcasted_iota(jnp.int32, shape, 1) // channels
            kept = jnp.where(row - inner == shift, ref_value, 0.0)
            return folded(jnp.sum(kept.reshape(groups, size, 4 * LANE), axis=1))

        for layer, plan in enumerate(PLAN):
            for dr in range(3):
                at = (layer * 3 + dr) * channels
                for dc in range(3):
                    total = None
                    for r in range(GROUP):
                        piece = acc_mid[layer, dc * LANE + r * channels : dc * LANE + (r + 1) * channels,
                                        (r + dr) * channels : (r + dr + 1) * channels]
                        total = piece if total is None else total + piece
                    out_ref[at : at + channels, dc * channels : (dc + 1) * channels] = total
                shift = dr - 1 - own - plan["o2"] - GROUP * plan["h2"][0]
                out_ref[at : at + 6, side] = by_row(acc_last[layer], 6, LANE // 2, shift)
                shift = 1 - dr - own - plan["o1"] - GROUP * plan["s1"][0]
                out_ref[at + 8 : at + 11, side] = by_row(
                    acc_first[layer, : 3 * SLOT], 3, SLOT, shift)
            at = layer * 3 * channels + 16
            out_ref[at : at + 2, side] = folded(acc_bias[layer, 0:2])
            bias = acc_bias[layer, 2:3]
            pick = lane_ids(channels)
            low = jnp.sum(jnp.where(lane < LANE // 2, bias, 0.0), axis=1, keepdims=True)
            top = jnp.sum(jnp.where(lane >= LANE // 2, bias, 0.0), axis=1, keepdims=True)
            out_ref[at + 2 : at + 3, side] = jnp.where(
                pick == 0, low, jnp.where(pick == 1, top, jnp.where(pick == 2, loss_ref[...], 0.0)))


def prepare(own, first_ref, mid_ref, last_ref, bf_ref, bm_ref, bl_ref, wf_a, wf_b, wm_ref, wt_ref, wl_a, wl_b,
            bf_out, bm_out, bl_out):
    channels = mid_ref.shape[2]
    lane = lane_ids(LANE)

    def tiled(x):
        return jnp.concatenate([x] * GROUP, axis=1)

    bf_out[...] = tiled(bf_ref[...])
    bm_out[...] = tiled(bm_ref[...])
    bl_out[...] = jnp.where(lane < LANE // 2, bl_ref[:, 0:1], bl_ref[:, 1:2])
    spread = (lax.broadcasted_iota(jnp.int32, (channels, LANE), 0) == lane % channels).astype(BF)
    parts = lax.broadcasted_iota(jnp.int32, (8, 3 * LANE), 0)
    parts = (parts == lax.broadcasted_iota(jnp.int32, (8, 3 * LANE), 1) // (LANE // 2)).astype(BF)
    wide_lane = lane_ids(3 * LANE) % (LANE // 2)
    edge = lax.broadcasted_iota(jnp.int32, (SLOT, LANE), 0)
    for layer, (wf, wl) in enumerate(((wf_a, wl_a), (wf_b, wl_b))):
        plan = PLAN[layer]
        rows = tiled(first_ref[layer])
        for k in range(plan["n1"]):
            row = k * GROUP + lane // channels + plan["o1"] + own - 1
            pieces = []
            for dc in range(3):
                total = jnp.zeros((SLOT, LANE), F32)
                for dr in range(3):
                    hit = (edge == row + dr) & (edge < 3 * own)
                    total = total + jnp.where(hit, rows[3 * dr + dc : 3 * dr + dc + 1], 0.0)
                pieces.append(total)
            pieces.append(jnp.zeros((LANE - 3 * SLOT, LANE), F32))
            high, low = split(jnp.concatenate(pieces, axis=0))
            wf[:LANE, blk(k)] = high
            wf[LANE : 2 * LANE, blk(k)] = high
            wf[2 * LANE :, blk(k)] = low
        for dc in range(3):
            taps_t = [dot(mid_ref[layer, 3 * dr + dc], spread, TN) for dr in range(3)]
            band = []
            for row in range(2 * GROUP):
                total = jnp.zeros((channels, LANE), F32)
                for dr in range(3):
                    if 0 <= row - dr < GROUP:
                        total = total + jnp.where(lane // channels == row - dr, taps_t[dr], 0.0)
                band.append(total)
            top = jnp.concatenate(band[:GROUP], axis=0)
            low = jnp.concatenate(band[GROUP:], axis=0)
            wm_ref[layer, dc, :LANE] = top.astype(BF)
            wm_ref[layer, dc, LANE:] = low.astype(BF)
            wt_ref[layer, dc, :LANE] = low.T.astype(BF)
            wt_ref[layer, dc, LANE:] = top.T.astype(BF)
        columns = [dot(last_ref[layer, dr], parts, TN) for dr in range(3)]
        for row in range(plan["n2"] * GROUP):
            total = jnp.zeros((channels, 3 * LANE), F32)
            for dr in range(3):
                hit = (wide_lane == row + own + 1 - dr + plan["o2"]) & (wide_lane < 3 * own)
                total = total + jnp.where(hit, columns[dr], 0.0)
            wl[row * channels : (row + 1) * channels, :] = total.astype(BF)


def butterfly(value, axes=("grp", "rows")):
    for axis in axes:
        count = lax.axis_size(axis)
        hop = 1
        while hop < count:
            value = value + lax.ppermute(value, axis, [(i, i ^ hop) for i in range(count)])
            hop *= 2
    return value


def grid_kernel(n_freq, pad_freq, height, img_width, r_ref, u_ref, v_ref, obs_ref, w_ref, out_ref, const_ref,
                u_s, c_s, sign_s):
    share = u_s.shape[0]
    start = pl.multiple_of(r_ref[1] * share, share)
    half = img_width // 2
    u = u_ref[pl.ds(start, share), :]
    v = v_ref[pl.ds(start, share), :]
    mirror = v > half
    v_fold = jnp.where(mirror, img_width - v, v)
    col = v_fold - r_ref[0] * n_freq
    col = jnp.where((col < 0) | (col >= n_freq), pad_freq, col)
    u_s[...] = jnp.where(mirror & (u > 0), height - u, u)
    c_s[...] = jnp.where(v_fold == half, n_freq, col)
    sign_s[...] = jnp.where(mirror, -1.0, 1.0)
    out_ref[...] = jnp.zeros_like(out_ref)
    ids = lax.broadcasted_iota(jnp.int32, (16, LANE), 0).astype(jnp.int16)
    slots = lax.broadcasted_iota(jnp.int32, (pad_freq, LANE), 0)
    one = jnp.ones((16, LANE), BF)
    zero = jnp.zeros((16, LANE), BF)
    group = 16

    def one_step(j, total):
        hots, values = [], []
        for q in range(group):
            row = pl.ds(j * group + q, 1)
            u_row = jnp.broadcast_to(u_s[row, :], (16, LANE)).astype(jnp.int16)
            hots.append(jnp.concatenate(
                [jnp.where(ids + jnp.int16(16 * g) == u_row, one, zero) for g in range(height // 16)], axis=0))
            c_hot = slots == c_s[row, :]
            lanes = pl.ds(pl.multiple_of((start + j * group + q) * LANE, LANE), LANE)
            w = w_ref[pl.ds(start + j * group + q, 1), :]
            o_re, o_im = obs_ref[0:1, lanes], obs_ref[1:2, lanes]
            total = total + w * (o_re * o_re + o_im * o_im)
            parts = []
            for full in (w, w * o_re, w * o_im * sign_s[row, :]):
                high = full.astype(BF).astype(F32)
                parts += [jnp.where(c_hot, high, 0.0), jnp.where(c_hot, full - high, 0.0)]
            values.append(jnp.concatenate(parts, axis=0).astype(BF))
        out_ref[...] += dot(jnp.concatenate(hots, axis=1), jnp.concatenate(values, axis=1), NT)
        return total

    total = lax.fori_loop(0, share // group, one_step, jnp.zeros((1, LANE), F32))
    const_ref[...] = jnp.sum(total, axis=(0, 1), keepdims=True)


def slot_count(n_freq):
    return 8 * ((n_freq + 8) // 8)


def lane_selection(samples, n_freq):
    pad_freq = slot_count(n_freq)
    lanes = 2 * samples * n_freq
    sel = np.zeros((2, 3, 6 * pad_freq, lanes), np.float32)
    for special in range(2):
        for lane in range(lanes):
            part, freq = lane // (samples * n_freq), lane % n_freq
            lone = special == 1 and freq == 0
            slot = n_freq if lone and part == 1 else freq
            fields = (0, 1, 2) if lone else (0, 1 + part, None)
            for out_id, field in enumerate(fields):
                if field is not None:
                    for piece in range(2):
                        sel[special, out_id, (2 * field + piece) * pad_freq + slot, lane] = 1.0
    return sel


def gridded(vis_u, vis_v, observed, vis_weight, height, img_width, n_rows, n_grp):
    n_freq = img_width // 2 // n_rows
    pad_freq = slot_count(n_freq)
    rows = vis_u.shape[0] // LANE
    share = rows // n_grp
    vmem = pl.BlockSpec(memory_space=pltpu.VMEM)
    where = jnp.stack([lax.axis_index("rows"), lax.axis_index("grp")]).astype(jnp.int32)
    return pl.pallas_call(
        functools.partial(grid_kernel, n_freq, pad_freq, height, img_width),
        out_shape=(jax.ShapeDtypeStruct((height, 6 * pad_freq), F32),
                   jax.ShapeDtypeStruct((1, 1), F32)),
        in_specs=[pl.BlockSpec(memory_space=pltpu.SMEM)] + [vmem] * 4,
        out_specs=(vmem, vmem),
        scratch_shapes=[pltpu.VMEM((share, LANE), jnp.int32), pltpu.VMEM((share, LANE), jnp.int32),
                        pltpu.VMEM((share, LANE), F32)],
        compiler_params=pltpu.CompilerParams(vmem_limit_bytes=24 * 2**20),
        cost_estimate=pl.CostEstimate(flops=2 * height * 256 * share * LANE * 4,
                                      bytes_accessed=24 * share * LANE, transcendentals=0),
    )(where, vis_u.reshape(rows, LANE), vis_v.reshape(rows, LANE), observed, vis_weight.reshape(rows, LANE))


def column_basis(img_width):
    cols = np.arange(img_width)
    freq = np.arange(img_width // 2)
    angle = 2.0 * np.pi * ((cols[:, None] * freq[None, :]) % img_width) / img_width
    re, im = np.cos(angle), -np.sin(angle)
    im[:, 0] = 1.0 - 2.0 * (cols % 2)
    return np.concatenate([re, im], axis=1).astype(np.float32)


def spectral_kernel(scale, factor, half, n_freq, own, reach, r_ref, z_ref, cs_ref, grid_ref, sel_ref, near_ref,
                    data_ref, near_s):
    height, lanes = z_ref.shape
    lane = lax.broadcasted_iota(jnp.int32, (1, lanes), 1)
    lone = ((lane % n_freq) == 0) & (r_ref[0] == 0)
    sign = jnp.where(lane < half, 1.0, -1.0)
    hi = lax.Precision.HIGHEST
    z = z_ref[...] * scale
    a = jnp.dot(cs_ref[0], z, precision=hi, preferred_element_type=jnp.float32)
    b = jnp.dot(cs_ref[1], z, precision=hi, preferred_element_type=jnp.float32)
    kind = jnp.where(r_ref[0] == 0, 1, 0)
    w, t1, t2 = [
        jnp.dot(grid_ref[...], sel_ref[kind, i], precision=hi, preferred_element_type=F32) for i in range(3)
    ]

    def swap(x):
        return jnp.concatenate([x[:, half:], x[:, :half]], axis=1)

    x = jnp.where(lone, a, a + sign * swap(b))
    p = w * x - t1
    q = jnp.where(lone, w * b + t2, -sign * swap(p))
    b_lone = jnp.where(lone, b, 0.0)
    terms = w * (x * x + b_lone * b_lone) - 2.0 * (x * t1 - b_lone * t2)
    data_ref[...] = jnp.sum(terms, axis=(0, 1), keepdims=True)
    near = jnp.dot(cs_ref[2], p, precision=hi, preferred_element_type=jnp.float32)
    near = near + jnp.dot(cs_ref[3], q, precision=hi, preferred_element_type=jnp.float32)
    near_s[...] = jnp.zeros_like(near_s)
    near_s[8 : 8 + height, :] = near * (factor * scale)
    for d in range(near_ref.shape[0]):
        near_ref[d] = near_s[8 + d * own - reach : 8 + (d + 1) * own + reach, :]


def spectral(z, grid, scale, factor, samples, own, reach):
    height, lanes = z.shape
    ids = np.arange(height)
    angle = 2.0 * np.pi * ((ids[:, None] * ids[None, :]) % height) / height
    cs = np.stack([np.cos(angle), np.sin(angle), np.cos(angle), np.sin(angle)]).astype(np.float32)
    vmem = pl.BlockSpec(memory_space=pltpu.VMEM)
    return pl.pallas_call(
        functools.partial(spectral_kernel, scale, factor, lanes // 2, lanes // (2 * samples), own, reach),
        out_shape=(jax.ShapeDtypeStruct((height // own, own + 2 * reach, lanes), F32),
                   jax.ShapeDtypeStruct((1, 1), F32)),
        in_specs=[pl.BlockSpec(memory_space=pltpu.SMEM)] + [vmem] * 4,
        out_specs=(vmem, vmem),
        scratch_shapes=[pltpu.VMEM((height + 16, lanes), F32)],
        compiler_params=pltpu.CompilerParams(vmem_limit_bytes=24 * 2**20),
    )(lax.axis_index("rows")[None].astype(jnp.int32), z, jnp.asarray(cs), grid,
      jnp.asarray(lane_selection(samples, lanes // (2 * samples))))


def body(
    latent, w_first, b_first, w_mid, b_mid, w_last, b_last, vis_u, vis_v, observed, vis_weight
):
    samples, row_count, img_width = latent.shape
    half_cols = img_width // 2
    n_rows = lax.axis_size("rows")
    n_grp = lax.axis_size("grp")
    height = row_count * n_rows
    batch_size = samples * n_grp
    layers = w_first.shape[0]
    vis_total = vis_u.shape[0]
    cells = height * img_width
    channels = w_mid.shape[2]
    half = half_cols
    n_freq = img_width // 2 // n_rows
    forward = [(i, i + 1) for i in range(n_rows - 1)]
    backward = [(target, source) for source, target in forward]
    low = lax.ppermute(latent, "rows", forward)
    high = lax.ppermute(latent, "rows", backward)
    grid, obs_const = gridded(
        vis_u, vis_v, observed, vis_weight, height, img_width, n_rows, n_grp
    )
    low, high, grid = lax.optimization_barrier((low, high, grid))
    grid = butterfly(grid, ("grp",))
    pieces = [value.transpose(1, 0, 2) for value in (low, latent, high)]
    last = jnp.pad(w_last.reshape(layers, 3, 6, channels), ((0, 0), (0, 0), (0, 2), (0, 0)))
    weights = (w_first.reshape(layers, 9, channels), w_mid, last, b_first, b_mid, b_last)
    basis_np = column_basis(img_width)
    basis_high = basis_np.astype(BF)
    basis_low = (basis_np - basis_high.astype(np.float32)).astype(BF)
    basis = jnp.asarray(np.stack([basis_high, basis_low]))
    index = lax.axis_index("rows")[None].astype(jnp.int32)
    smem = pl.BlockSpec(memory_space=pltpu.SMEM)

    def whole(value):
        rank = len(value.shape)
        return pl.BlockSpec(value.shape, lambda s: (0,) * rank)

    def per_sample(*shape):
        rank = len(shape)
        return pl.BlockSpec((1,) + shape, lambda s: (s,) + (0,) * rank)

    saved_shapes = []
    for plan in PLAN:
        for key, kind in (("h1", BF), ("h2", BF), ("s1", BF), ("s2", BF)):
            saved_shapes.append(((half, plan[key][1] * LANE), kind))
        saved_shapes.append(((half, LANE), F32))
    saved_shapes.append(((half, LANE), F32))
    saved_shapes.append(((2, half, LANE), F32))
    saved_specs = [per_sample(*shape) for shape, kind in saved_shapes]
    saved_types = [jax.ShapeDtypeStruct((samples,) + shape, kind) for shape, kind in saved_shapes]
    weights = weights + (basis,)
    bands = [((3 * LANE, plan["n1"] * LANE), BF) for plan in PLAN]
    bands += [((layers, 3, 2 * LANE, LANE), BF)]
    bands += [((plan["n2"] * LANE, 3 * LANE), BF) for plan in PLAN]
    bands = [jax.ShapeDtypeStruct(shape, kind) for shape, kind in bands]
    max1 = max(plan["n1"] for plan in PLAN) * LANE
    max2 = max(plan["n2"] for plan in PLAN) * LANE
    params = pltpu.CompilerParams(vmem_limit_bytes=58 * 2**20)
    image_out, columns, logdet, wf_a, wf_b, wt, wl_a, wl_b, *saved = pl.pallas_call(
        functools.partial(forward_kernel, height, row_count, channels),
        grid=(samples,),
        out_shape=(
            jax.ShapeDtypeStruct((row_count, samples, img_width), F32),
            jax.ShapeDtypeStruct((n_rows, row_count, 2 * samples * n_freq), F32),
            jax.ShapeDtypeStruct((1, LANE), F32),
            *bands,
            *saved_types,
        ),
        in_specs=[smem] + [whole(value) for value in (*pieces, *weights)],
        out_specs=(
            pl.BlockSpec((row_count, samples, img_width), lambda s: (0, 0, 0)),
            pl.BlockSpec((n_rows, row_count, 2 * samples * n_freq), lambda s: (0, 0, 0)),
            pl.BlockSpec((1, LANE), lambda s: (0, 0)),
            *[whole(band) for band in bands],
            *saved_specs,
        ),
        scratch_shapes=[pltpu.VMEM((layers, 3, 2 * LANE, LANE), BF)]
        + [pltpu.VMEM((layers, LANE), F32)] * 3
        + [pltpu.VMEM((half, max1), BF)] * 3
        + [
            pltpu.VMEM((half, max2), BF),
            pltpu.VMEM((LANE, img_width), F32),
            pltpu.VMEM((samples, 2, half, LANE), F32),
            pltpu.VMEM((samples, 16, img_width), F32),
        ],
        compiler_params=params,
    )(index, *pieces, *weights)
    image_out = image_out.transpose(1, 0, 2)
    logdet = jnp.sum(logdet)
    norm_scale = 1.0 / math.sqrt(height * img_width)
    reach = 6
    factor = 2.0 / (vis_total * batch_size)
    columns = lax.all_to_all(columns, "rows", 0, 0, tiled=True)
    near, data_sum = spectral(
        columns.reshape(height, 2 * samples * n_freq), grid, norm_scale, factor, samples, row_count, reach
    )
    near = lax.all_to_all(near, "rows", 0, 0, tiled=True)
    span = row_count + 2 * reach
    data_part = (data_sum[0, 0] + batch_size * obs_const[0, 0] / n_rows) / vis_total
    loss_part = (data_part - logdet / (height * img_width)) / batch_size
    out_rows = layers * 3 * channels
    weights = (wf_a, wf_b, wt, wl_a, wl_b, basis)
    flat = pl.pallas_call(
        functools.partial(
            backward_kernel, height, row_count, channels, reach, batch_size * cells
        ),
        grid=(samples,),
        out_shape=jax.ShapeDtypeStruct((out_rows, LANE), F32),
        in_specs=[smem, whole(near), pl.BlockSpec((1, 1), lambda s: (0, 0))]
        + [whole(value) for value in weights] + saved_specs,
        out_specs=pl.BlockSpec((out_rows, LANE), lambda s: (0, 0)),
        scratch_shapes=[
            pltpu.VMEM((LANE, img_width), F32),
            pltpu.VMEM((img_width, LANE), F32),
            *[pltpu.VMEM((half, max2), BF)] * 3,
            pltpu.VMEM((half, max1), BF),
            pltpu.VMEM((layers, 3 * LANE, 2 * LANE), F32),
            pltpu.VMEM((layers, 3 * LANE, 4 * LANE), F32),
            pltpu.VMEM((layers, LANE, 4 * LANE), F32),
            pltpu.VMEM((layers, 8, LANE), F32),
        ],
        compiler_params=params,
    )(index, near, loss_part.reshape(1, 1), *weights, *saved)
    flat = butterfly(flat)
    main = flat[:, : 3 * channels]
    main = main.reshape(layers, 3, channels, 3, channels).transpose(0, 1, 3, 2, 4)
    rest = flat[:, 3 * channels :].reshape(layers, 3, channels, channels)
    final_grads = [
        rest[:, :, 8:11].reshape(layers, 9, channels, 1),
        main.reshape(layers, 9, channels, channels),
        rest[:, :, :6].reshape(layers, 9, 2, channels),
        rest[:, 0, 16],
        rest[:, 0, 17],
        rest[:, 0, 18, :2],
    ]
    loss = rest[0, 0, 18, 2]
    return (
        image_out,
        loss,
        final_grads[0],
        final_grads[1],
        final_grads[2],
        final_grads[3],
        final_grads[4],
        final_grads[5],
    )


def solution(mesh):
    in_specs = (P("grp", "rows", None), P(), P(), P(), P(), P(), P(), P(), P(), P(), P())
    out_specs = (P("grp", "rows", None), P(), P(), P(), P(), P(), P(), P())
    return jax.shard_map(body, mesh=mesh, in_specs=in_specs, out_specs=out_specs, check_vma=False)
```

```python
import functools
import math

import jax
import jax.numpy as jnp
import numpy as np
from jax import lax
from jax.experimental import pallas as pl
from jax.experimental.pallas import tpu as pltpu
from jax.sharding import PartitionSpec as P


BF = jnp.bfloat16
F32 = jnp.float32
GROUP = 4
LANE = 128
SLOT = 40
PLAN = (
    dict(o1=-10, n1=8, o2=-9, n2=8, h1=(2, 5), h2=(2, 4), s1=(2, 4), s2=(2, 4)),
    dict(o1=-7, n1=7, o2=-6, n2=6, h1=(1, 5), h2=(1, 4), s1=(1, 5), s2=(0, 6)),
)


def dot(a, b, dims=((1,), (0,))):
    return lax.dot_general(a, b, (dims, ((), ())), preferred_element_type=F32)


NT = ((1,), (1,))
TN = ((0,), (0,))


def split(x):
    high = x.astype(BF)
    return high, (x - high.astype(F32)).astype(BF)


def dot3(a, b, dims):
    return dot(a[0], b[0], dims) + dot(a[1], b[0], dims) + dot(a[0], b[1], dims)


def down(x):
    turned = pltpu.roll(x, 1, 0)
    rows = lax.broadcasted_iota(jnp.int32, (8, x.shape[1]), 0)
    return jnp.concatenate([jnp.where(rows == 0, 0.0, turned[:8]), turned[8:]], axis=0)


def up(x):
    turned = pltpu.roll(x, x.shape[0] - 1, 0)
    rows = lax.broadcasted_iota(jnp.int32, (8, x.shape[1]), 0)
    return jnp.concatenate([turned[:-8], jnp.where(rows == 7, 0.0, turned[-8:])], axis=0)


def lane_ids(count):
    return lax.broadcasted_iota(jnp.int32, (1, count), 1)


def taps(cond):
    return down(cond) + pltpu.roll(cond, SLOT, 1) + pltpu.roll(up(cond), 2 * SLOT, 1)


def blk(start, count=1):
    return slice(start * LANE, (start + count) * LANE)


def forward_kernel(height, own, channels, r_ref, low_ref, mid_ref, high_ref, first_ref, taps_ref, last_ref, b1_ref,
                   b2_ref, b3_ref, basis_ref, img_ref, col_ref, logdet_ref, wf_a, wf_b, wt_ref, wl_a, wl_b, *rest):
    saved, scratch = rest[:-9], rest[-9:]
    wm_ref, bf_ref, bm_ref, bl_ref, hs, h2s, wide_s, lat_s, mine_s = scratch
    step = pl.program_id(0)
    samples, cols = lat_s.shape[0], lat_s.shape[2]
    first = r_ref[0] * own
    lane = lane_ids(LANE)
    image_row = lane - own + first
    image_mask = ((lane < 3 * own) & (image_row >= 0) & (image_row < height)).astype(F32)
    own_mask = ((lane >= own) & (lane < 2 * own)).astype(F32)

    @pl.when(step == 0)
    def _():
        logdet_ref[...] = jnp.zeros_like(logdet_ref)
        prepare(own, first_ref, taps_ref, last_ref, b1_ref, b2_ref, b3_ref, wf_a, wf_b, wm_ref, wt_ref, wl_a, wl_b,
                bf_ref, bm_ref, bl_ref)
        wide_s[...] = jnp.zeros_like(wide_s)
        for s in range(samples):
            for place, ref in enumerate((low_ref, mid_ref, high_ref)):
                wide_s[place * own : (place + 1) * own, :] = ref[:, s, :]
            turned = wide_s[...].T
            for side in range(2):
                lat_s[s, side] = turned[side * cols : (side + 1) * cols]

    def mask_of(origin, block):
        row = origin + block * GROUP + lane // channels + first
        return ((row >= 0) & (row < height)).astype(F32)

    halves = [lat_s[step, 0], lat_s[step, 1]]
    for side in range(2):
        saved[11][0, side] = halves[side]
    for layer, (wf, wl) in enumerate(((wf_a, wl_a), (wf_b, wl_b))):
        plan = PLAN[layer]
        out_h1, out_h2, out_s1, out_s2, out_log = saved[5 * layer : 5 * layer + 5]
        cond, target = halves[layer], halves[1 - layer]
        if layer == 1:
            saved[10][0] = cond
        high, low = split(taps(cond))
        both = jnp.concatenate([high, low, high], axis=1)
        for k in range(plan["n1"]):
            if k % 2 == 0:
                lanes = blk(k, min(2, plan["n1"] - k))
                pair = dot(both, wf[:, lanes])
            pre = pair[:, blk(k % 2)] + bf_ref[layer : layer + 1]
            sig = 0.5 + 0.5 * jnp.tanh(0.5 * pre)
            kept = sig * mask_of(plan["o1"], k)
            hidden = pre * kept
            start, count = plan["s1"]
            if start <= k < start + count:
                out_s1[0, :, blk(k - start)] = (kept + hidden * (1.0 - sig)).astype(BF)
            plain = hidden.astype(BF)
            hs[:, blk(3 * k)] = down(hidden).astype(BF)
            hs[:, blk(3 * k + 1)] = plain
            hs[:, blk(3 * k + 2)] = up(hidden).astype(BF)
            start, count = plan["h1"]
            if start <= k < start + count:
                out_h1[0, :, blk(k - start)] = plain
        for k in range(plan["n2"]):
            wide = min(2, plan["n1"] - k)
            pre = dot(hs[:, blk(3 * k, 3 * wide)], wm_ref[layer, : 3 * wide * LANE])
            pre = pre + bm_ref[layer : layer + 1]
            sig = 0.5 + 0.5 * jnp.tanh(0.5 * pre)
            kept = sig * mask_of(plan["o2"], k)
            hidden = pre * kept
            start, count = plan["s2"]
            if start <= k < start + count:
                out_s2[0, :, blk(k - start)] = (kept + hidden * (1.0 - sig)).astype(BF)
            hidden = hidden.astype(BF)
            h2s[:, blk(k)] = hidden
            start, count = plan["h2"]
            if start <= k < start + count:
                out_h2[0, :, blk(k - start)] = hidden
        terms = dot(h2s[:, blk(0, plan["n2"])], wl[...])
        raw = down(terms[:, blk(0)]) + terms[:, blk(1)] + up(terms[:, blk(2)])
        raw = raw + bl_ref[layer : layer + 1]
        log_scale = jnp.tanh(raw)
        out_log[0] = log_scale
        logdet_ref[...] += jnp.sum(log_scale * own_mask, axis=0, keepdims=True)
        halves[1 - layer] = (target * jnp.exp(log_scale) + pltpu.roll(raw, LANE // 2, 1)) * image_mask
    for side in range(2):
        mine = pltpu.roll(halves[side], LANE - own, 1).T
        mine_s[step, :, side * cols : (side + 1) * cols] = mine[:16]

    @pl.when(step == samples - 1)
    def _():
        for s in range(samples):
            img_ref[:, s, :] = mine_s[s, :own]
        image = split(mine_s[...].reshape(samples * 16, 2 * cols))
        spectrum = dot3(image, (basis_ref[0], basis_ref[1]), ((1,), (0,)))
        blocks, _, lanes = col_ref.shape
        n_freq = lanes // (2 * samples)
        for d in range(blocks):
            chunk, offset = divmod(d * n_freq, LANE)
            total = jnp.zeros((16, LANE), F32)
            for part in range(2):
                for s in range(samples):
                    at = (part * samples + s) * n_freq
                    piece = spectrum[s * 16 : (s + 1) * 16, blk(part * (cols // LANE) + chunk)]
                    if at != offset:
                        piece = pltpu.roll(piece, (at - offset) % LANE, 1)
                    total = jnp.where((lane >= at) & (lane < at + n_freq), piece, total)
            col_ref[d] = total[:own, :lanes]


def backward_kernel(height, own, channels, reach, cells, r_ref, near_ref, loss_ref, wf_a, wf_b, wt_ref,
                    wl_a, wl_b, basis_ref, *rest):
    saved, lat_ref, out_ref, scratch = rest[:11], rest[11], rest[12], rest[13:]
    near_s, cot_s, ds, cpo_s, acc_mid, acc_last, acc_first, acc_bias = scratch
    step = pl.program_id(0)
    first = r_ref[0] * own
    lane = lane_ids(LANE)
    image_row = lane - own + first
    image_mask = ((lane < 3 * own) & (image_row >= 0) & (image_row < height)).astype(F32)
    raw_row = lane % (LANE // 2)
    own_mask = ((raw_row >= own) & (raw_row < 2 * own)).astype(F32)

    @pl.when(step == 0)
    def _():
        near_s[...] = jnp.zeros_like(near_s)
        blocks, span, lanes = near_ref.shape
        samples = pl.num_programs(0)
        n_freq = lanes // (2 * samples)
        per = LANE // n_freq
        for s in range(samples):
            for part in range(2):
                for chunk in range(blocks // per):
                    at = (part * samples + s) * n_freq
                    total = jnp.zeros((span, LANE), F32)
                    for i in range(per):
                        piece = near_ref[chunk * per + i]
                        if lanes < LANE:
                            piece = jnp.concatenate([piece] * (LANE // lanes), axis=1)
                        if at != i * n_freq:
                            piece = pltpu.roll(piece, (i * n_freq - at) % LANE, 1)
                        total = jnp.where((lane >= i * n_freq) & (lane < (i + 1) * n_freq), piece, total)
                    near_s[s * 32 : s * 32 + span, blk(part * (blocks // per) + chunk)] = total
        cot_s[...] = dot3((basis_ref[0], basis_ref[1]), split(near_s[...]), NT)
        for ref in (acc_mid, acc_last, acc_first, acc_bias):
            ref[...] = jnp.zeros_like(ref)

    def own_of(origin, block):
        row = origin + block * GROUP + lane // channels
        return ((row >= 0) & (row < own)).astype(F32)

    cols = lat_ref.shape[2]
    cots = []
    valid = (lane >= own - reach) & (lane < 2 * own + reach)
    shift = (own - reach + LANE - 32 * step) % LANE
    for side in range(2):
        cot = pltpu.roll(cot_s[side * cols : (side + 1) * cols, :], shift, 1)
        cots.append(jnp.where(valid, cot, 0.0))
    cond_one = saved[10][0]
    for layer, wf, wl in ((1, wf_b, wl_b), (0, wf_a, wl_a)):
        plan = PLAN[layer]
        h1, h2, s1, s2, log_ref = saved[5 * layer : 5 * layer + 5]
        cond = cond_one if layer == 1 else lat_ref[0, 0]
        target = lat_ref[0, 1 - layer]
        cot_new = cots[1 - layer]
        log_scale = log_ref[0]
        cot_log = cot_new * target * jnp.exp(log_scale) - 1.0 / cells
        scale_part = cot_log * (1.0 - log_scale * log_scale) * image_mask
        raw = scale_part + pltpu.roll(cot_new * image_mask, LANE // 2, 1)
        raw = raw.astype(BF).astype(F32)
        mine = raw * own_mask
        spread = jnp.concatenate([up(raw).astype(BF), raw.astype(BF), down(raw).astype(BF)], 1)
        spread_own = jnp.concatenate([up(mine).astype(BF), mine.astype(BF), down(mine).astype(BF)], 1)
        acc_last[layer] += dot(spread_own, h2[0], TN)
        acc_bias[layer, 2:3] += jnp.sum(mine, axis=0, keepdims=True)
        start2, count2 = plan["s2"]
        base1, _ = plan["h1"]
        lefts, rights = [], []
        for k in range(start2, start2 + count2):
            if (k - start2) % 2 == 0:
                pair = dot(spread, wl[blk(k, 2), :], NT)
            cot = pair[:, blk((k - start2) % 2)] * s2[0, :, blk(k - start2)].astype(F32)
            plain = cot.astype(BF)
            cot = plain.astype(F32)
            parts = (up(cot).astype(BF), plain, down(cot).astype(BF))
            for tap, part in enumerate(parts):
                ds[:, blk(3 * (k - start2) + tap)] = part
            local = k - base1
            if 0 <= local < 4:
                mask = own_of(plan["o2"], k)
                acc_bias[layer, 1:2] += jnp.sum(cot * mask, axis=0, keepdims=True)
                lefts.append(jnp.concatenate([part * mask.astype(BF) for part in parts], 1))
                rights.append(h1[0, :, blk(local, 2)])
        acc_mid[layer] += dot(jnp.concatenate(lefts, axis=0), jnp.concatenate(rights, axis=0), TN)
        high, low = split(taps(cond))
        own_cots = []
        start1, count1 = plan["s1"]
        for k in range(start1, start1 + count1):
            side = (k - start1) % 2
            if side == 0:
                outs = min(2, start1 + count1 - k)
                lowest, highest = max(k - 1, start2), k + outs - 1
                window = ds[:, blk(3 * (lowest - start2), 3 * (highest - lowest + 1))]
                band = wt_ref[layer, 3 * (lowest - k + 1) * LANE : 3 * (highest - k + 2) * LANE, : outs * LANE]
                pair = dot(window, band)
            cot = pair[:, blk(side)]
            plain = (cot * s1[0, :, blk(k - start1)].astype(F32)).astype(BF)
            cpo_s[:, blk(k - start1)] = plain
            if k - start1 < 4:
                mask = own_of(plan["o1"], k)
                mine = plain.astype(F32) * mask
                acc_bias[layer, 0:1] += jnp.sum(mine, axis=0, keepdims=True)
                own_cots.append(mine.astype(BF))
        own_cots = jnp.concatenate(own_cots, axis=1)
        acc_first[layer] += dot(
            jnp.concatenate([high, low], axis=0), jnp.concatenate([own_cots, own_cots], axis=0), TN)
        if layer == 1:
            full = cpo_s[:, blk(0, count1)]
            lanes = blk(start1, count1)
            terms = dot(full, wf[LANE:, lanes], NT)
            terms = terms[:, :LANE] + terms[:, LANE:]
            total = up(terms) + pltpu.roll(terms, LANE - SLOT, 1) * (lane < SLOT).astype(F32)
            total = jnp.where(lane < SLOT, total, 0.0)
            total = total + jnp.where(lane < SLOT, pltpu.roll(down(terms), LANE - 2 * SLOT, 1), 0.0)
            cots[1] = cots[1] + total

    @pl.when(step == pl.num_programs(0) - 1)
    def _():
        out_ref[...] = jnp.zeros_like(out_ref)
        layers = len(PLAN)
        side = slice(3 * channels, 4 * channels)
        fold_row = lax.broadcasted_iota(jnp.int32, (4 * LANE, channels), 0)
        fold_col = lax.broadcasted_iota(jnp.int32, (4 * LANE, channels), 1)
        fold = (fold_row % channels == fold_col).astype(F32)
        hi = lax.Precision.HIGHEST

        def folded(x):
            return jnp.dot(x, fold[: x.shape[1]], precision=hi, preferred_element_type=F32)

        def by_row(ref_value, groups, size, shift):
            shape = (groups * size, 4 * LANE)
            inner = lax.broadcasted_iota(jnp.int32, shape, 0) % size
            row = lax.broadcasted_iota(jnp.int32, shape, 1) // channels
            kept = jnp.where(row - inner == shift, ref_value, 0.0)
            return folded(jnp.sum(kept.reshape(groups, size, 4 * LANE), axis=1))

        for layer, plan in enumerate(PLAN):
            for dr in range(3):
                at = (layer * 3 + dr) * channels
                for dc in range(3):
                    total = None
                    for r in range(GROUP):
                        piece = acc_mid[layer, dc * LANE + r * channels : dc * LANE + (r + 1) * channels,
                                        (r + dr) * channels : (r + dr + 1) * channels]
                        total = piece if total is None else total + piece
                    out_ref[at : at + channels, dc * channels : (dc + 1) * channels] = total
                shift = dr - 1 - own - plan["o2"] - GROUP * plan["h2"][0]
                out_ref[at : at + 6, side] = by_row(acc_last[layer], 6, LANE // 2, shift)
                shift = 1 - dr - own - plan["o1"] - GROUP * plan["s1"][0]
                out_ref[at + 8 : at + 11, side] = by_row(
                    acc_first[layer, : 3 * SLOT], 3, SLOT, shift)
            at = layer * 3 * channels + 16
            out_ref[at : at + 2, side] = folded(acc_bias[layer, 0:2])
            bias = acc_bias[layer, 2:3]
            pick = lane_ids(channels)
            low = jnp.sum(jnp.where(lane < LANE // 2, bias, 0.0), axis=1, keepdims=True)
            top = jnp.sum(jnp.where(lane >= LANE // 2, bias, 0.0), axis=1, keepdims=True)
            out_ref[at + 2 : at + 3, side] = jnp.where(
                pick == 0, low, jnp.where(pick == 1, top, jnp.where(pick == 2, loss_ref[...], 0.0)))


def prepare(own, first_ref, mid_ref, last_ref, bf_ref, bm_ref, bl_ref, wf_a, wf_b, wm_ref, wt_ref, wl_a, wl_b,
            bf_out, bm_out, bl_out):
    channels = mid_ref.shape[2]
    lane = lane_ids(LANE)

    def tiled(x):
        return jnp.concatenate([x] * GROUP, axis=1)

    bf_out[...] = tiled(bf_ref[...])
    bm_out[...] = tiled(bm_ref[...])
    bl_out[...] = jnp.where(lane < LANE // 2, bl_ref[:, 0:1], bl_ref[:, 1:2])
    spread = (lax.broadcasted_iota(jnp.int32, (channels, LANE), 0) == lane % channels).astype(BF)
    parts = lax.broadcasted_iota(jnp.int32, (8, 3 * LANE), 0)
    parts = (parts == lax.broadcasted_iota(jnp.int32, (8, 3 * LANE), 1) // (LANE // 2)).astype(BF)
    wide_lane = lane_ids(3 * LANE) % (LANE // 2)
    edge = lax.broadcasted_iota(jnp.int32, (SLOT, LANE), 0)
    for layer, (wf, wl) in enumerate(((wf_a, wl_a), (wf_b, wl_b))):
        plan = PLAN[layer]
        rows = tiled(first_ref[layer])
        for k in range(plan["n1"]):
            row = k * GROUP + lane // channels + plan["o1"] + own - 1
            pieces = []
            for dc in range(3):
                total = jnp.zeros((SLOT, LANE), F32)
                for dr in range(3):
                    hit = (edge == row + dr) & (edge < 3 * own)
                    total = total + jnp.where(hit, rows[3 * dr + dc : 3 * dr + dc + 1], 0.0)
                pieces.append(total)
            pieces.append(jnp.zeros((LANE - 3 * SLOT, LANE), F32))
            high, low = split(jnp.concatenate(pieces, axis=0))
            wf[:LANE, blk(k)] = high
            wf[LANE : 2 * LANE, blk(k)] = high
            wf[2 * LANE :, blk(k)] = low
        for dc in range(3):
            taps_t = [dot(mid_ref[layer, 3 * dr + dc], spread, TN) for dr in range(3)]
            band = []
            for row in range(2 * GROUP):
                total = jnp.zeros((channels, LANE), F32)
                for dr in range(3):
                    if 0 <= row - dr < GROUP:
                        total = total + jnp.where(lane // channels == row - dr, taps_t[dr], 0.0)
                band.append(total)
            top = jnp.concatenate(band[:GROUP], axis=0)
            low = jnp.concatenate(band[GROUP:], axis=0)
            empty = jnp.zeros((LANE, LANE), BF)
            wm_ref[layer, blk(dc)] = top.astype(BF)
            wm_ref[layer, blk(3 + dc)] = low.astype(BF)
            near, far = low.T.astype(BF), top.T.astype(BF)
            for j, pair in enumerate(((near, empty), (far, near), (empty, far))):
                wt_ref[layer, blk(3 * j + dc), :LANE] = pair[0]
                wt_ref[layer, blk(3 * j + dc), LANE:] = pair[1]
        columns = [dot(last_ref[layer, dr], parts, TN) for dr in range(3)]
        for row in range(plan["n2"] * GROUP):
            total = jnp.zeros((channels, 3 * LANE), F32)
            for dr in range(3):
                hit = (wide_lane == row + own + 1 - dr + plan["o2"]) & (wide_lane < 3 * own)
                total = total + jnp.where(hit, columns[dr], 0.0)
            wl[row * channels : (row + 1) * channels, :] = total.astype(BF)


def butterfly(value, axes=("grp", "rows")):
    for axis in axes:
        count = lax.axis_size(axis)
        hop = 1
        if count % 4 == 0:
            near = [lax.ppermute(value, axis, [(i, i ^ far) for i in range(count)]) for far in (1, 2, 3)]
            value = (value + near[0]) + (near[1] + near[2])
            hop = 4
        while hop < count:
            value = value + lax.ppermute(value, axis, [(i, i ^ hop) for i in range(count)])
            hop *= 2
    return value


def grid_kernel(n_freq, pad_freq, height, img_width, r_ref, u_ref, v_ref, obs_ref, w_ref, out_ref, const_ref,
                u_s, c_s, sign_s):
    share = u_s.shape[0]
    half = img_width // 2
    u = u_ref[...]
    v = v_ref[...]
    mirror = v > half
    v_fold = jnp.where(mirror, img_width - v, v)
    col = v_fold - r_ref[0] * n_freq
    col = jnp.where((col < 0) | (col >= n_freq), pad_freq, col)
    u_s[...] = jnp.where(mirror & (u > 0), height - u, u)
    c_s[...] = jnp.where(v_fold == half, n_freq, col)
    sign_s[...] = jnp.where(mirror, -1.0, 1.0)
    out_ref[...] = jnp.zeros_like(out_ref)
    ids = lax.broadcasted_iota(jnp.int32, (16, LANE), 0).astype(jnp.int16)
    slots = lax.broadcasted_iota(jnp.int32, (pad_freq, LANE), 0)
    one = jnp.ones((16, LANE), BF)
    zero = jnp.zeros((16, LANE), BF)
    group = 16

    def one_step(j, total):
        hots, values = [], []
        for q in range(group):
            row = pl.ds(j * group + q, 1)
            u_row = jnp.broadcast_to(u_s[row, :], (16, LANE)).astype(jnp.int16)
            hots.append(jnp.concatenate(
                [jnp.where(ids + jnp.int16(16 * g) == u_row, one, zero) for g in range(height // 16)], axis=0))
            c_hot = slots == c_s[row, :]
            lanes = pl.ds(pl.multiple_of((j * group + q) * LANE, LANE), LANE)
            w = w_ref[row, :]
            o_re, o_im = obs_ref[0:1, lanes], obs_ref[1:2, lanes]
            total = total + w * (o_re * o_re + o_im * o_im)
            parts = []
            for full in (w, w * o_re, w * o_im * sign_s[row, :]):
                high = full.astype(BF).astype(F32)
                parts += [jnp.where(c_hot, high, 0.0), jnp.where(c_hot, full - high, 0.0)]
            values.append(jnp.concatenate(parts, axis=0).astype(BF))
        out_ref[...] += dot(jnp.concatenate(hots, axis=1), jnp.concatenate(values, axis=1), NT)
        return total

    total = lax.fori_loop(0, share // group, one_step, jnp.zeros((1, LANE), F32))
    const_ref[...] = jnp.sum(total, axis=(0, 1), keepdims=True)


def slot_count(n_freq):
    return 8 * ((n_freq + 8) // 8)


def lane_selection(samples, n_freq):
    pad_freq = slot_count(n_freq)
    lanes = 2 * samples * n_freq
    sel = np.zeros((2, 3, 6 * pad_freq, lanes), np.float32)
    for special in range(2):
        for lane in range(lanes):
            part, freq = lane // (samples * n_freq), lane % n_freq
            lone = special == 1 and freq == 0
            slot = n_freq if lone and part == 1 else freq
            fields = (0, 1, 2) if lone else (0, 1 + part, None)
            for out_id, field in enumerate(fields):
                if field is not None:
                    for piece in range(2):
                        sel[special, out_id, (2 * field + piece) * pad_freq + slot, lane] = 1.0
    return sel


def gridded(vis_u, vis_v, observed, vis_weight, height, img_width, n_rows, n_grp):
    n_freq = img_width // 2 // n_rows
    pad_freq = slot_count(n_freq)
    rows = vis_u.shape[0] // LANE
    share = rows // n_grp
    rows_spec = pl.BlockSpec((share, LANE), lambda i, r: (r[1], 0))
    where = jnp.stack([lax.axis_index("rows"), lax.axis_index("grp")]).astype(jnp.int32)
    return pl.pallas_call(
        functools.partial(grid_kernel, n_freq, pad_freq, height, img_width),
        out_shape=(jax.ShapeDtypeStruct((height, 6 * pad_freq), F32),
                   jax.ShapeDtypeStruct((1, 1), F32)),
        grid_spec=pltpu.PrefetchScalarGridSpec(
            num_scalar_prefetch=1,
            grid=(1,),
            in_specs=[rows_spec, rows_spec, pl.BlockSpec((2, share * LANE), lambda i, r: (0, r[1])), rows_spec],
            out_specs=(pl.BlockSpec((height, 6 * pad_freq), lambda i, r: (0, 0)),
                       pl.BlockSpec((1, 1), lambda i, r: (0, 0))),
            scratch_shapes=[pltpu.VMEM((share, LANE), jnp.int32), pltpu.VMEM((share, LANE), jnp.int32),
                            pltpu.VMEM((share, LANE), F32)],
        ),
        compiler_params=pltpu.CompilerParams(vmem_limit_bytes=60 * 2**20),
        cost_estimate=pl.CostEstimate(flops=2 * height * 256 * share * LANE * 4,
                                      bytes_accessed=24 * share * LANE, transcendentals=0),
    )(where, vis_u.reshape(rows, LANE), vis_v.reshape(rows, LANE), observed, vis_weight.reshape(rows, LANE))


def column_basis(img_width):
    cols = np.arange(img_width)
    freq = np.arange(img_width // 2)
    angle = 2.0 * np.pi * ((cols[:, None] * freq[None, :]) % img_width) / img_width
    re, im = np.cos(angle), -np.sin(angle)
    im[:, 0] = 1.0 - 2.0 * (cols % 2)
    return np.concatenate([re, im], axis=1).astype(np.float32)


def spectral_kernel(scale, factor, half, n_freq, own, reach, r_ref, z_ref, cs_ref, grid_ref, sel_ref, near_ref,
                    data_ref, near_s):
    height, lanes = z_ref.shape
    lane = lax.broadcasted_iota(jnp.int32, (1, lanes), 1)
    lone = ((lane % n_freq) == 0) & (r_ref[0] == 0)
    sign = jnp.where(lane < half, 1.0, -1.0)
    hi = lax.Precision.HIGHEST
    z = z_ref[...] * scale
    a = jnp.dot(cs_ref[0], z, precision=hi, preferred_element_type=jnp.float32)
    b = jnp.dot(cs_ref[1], z, precision=hi, preferred_element_type=jnp.float32)
    kind = jnp.where(r_ref[0] == 0, 1, 0)
    w, t1, t2 = [
        jnp.dot(grid_ref[...], sel_ref[kind, i], precision=hi, preferred_element_type=F32) for i in range(3)
    ]

    def swap(x):
        return jnp.concatenate([x[:, half:], x[:, :half]], axis=1)

    x = jnp.where(lone, a, a + sign * swap(b))
    p = w * x - t1
    q = jnp.where(lone, w * b + t2, -sign * swap(p))
    b_lone = jnp.where(lone, b, 0.0)
    terms = w * (x * x + b_lone * b_lone) - 2.0 * (x * t1 - b_lone * t2)
    data_ref[...] = jnp.sum(terms, axis=(0, 1), keepdims=True)
    near = jnp.dot(cs_ref[2], p, precision=hi, preferred_element_type=jnp.float32)
    near = near + jnp.dot(cs_ref[3], q, precision=hi, preferred_element_type=jnp.float32)
    near_s[...] = jnp.zeros_like(near_s)
    near_s[8 : 8 + height, :] = near * (factor * scale)
    for d in range(near_ref.shape[0]):
        near_ref[d] = near_s[8 + d * own - reach : 8 + (d + 1) * own + reach, :]


def spectral(z, grid, scale, factor, samples, own, reach):
    height, lanes = z.shape
    ids = np.arange(height)
    angle = 2.0 * np.pi * ((ids[:, None] * ids[None, :]) % height) / height
    cs = np.stack([np.cos(angle), np.sin(angle), np.cos(angle), np.sin(angle)]).astype(np.float32)
    vmem = pl.BlockSpec(memory_space=pltpu.VMEM)
    return pl.pallas_call(
        functools.partial(spectral_kernel, scale, factor, lanes // 2, lanes // (2 * samples), own, reach),
        out_shape=(jax.ShapeDtypeStruct((height // own, own + 2 * reach, lanes), F32),
                   jax.ShapeDtypeStruct((1, 1), F32)),
        in_specs=[pl.BlockSpec(memory_space=pltpu.SMEM)] + [vmem] * 4,
        out_specs=(vmem, vmem),
        scratch_shapes=[pltpu.VMEM((height + 16, lanes), F32)],
        compiler_params=pltpu.CompilerParams(vmem_limit_bytes=24 * 2**20),
    )(lax.axis_index("rows")[None].astype(jnp.int32), z, jnp.asarray(cs), grid,
      jnp.asarray(lane_selection(samples, lanes // (2 * samples))))


def body(
    latent, w_first, b_first, w_mid, b_mid, w_last, b_last, vis_u, vis_v, observed, vis_weight
):
    samples, row_count, img_width = latent.shape
    half_cols = img_width // 2
    n_rows = lax.axis_size("rows")
    n_grp = lax.axis_size("grp")
    height = row_count * n_rows
    batch_size = samples * n_grp
    layers = w_first.shape[0]
    vis_total = vis_u.shape[0]
    cells = height * img_width
    channels = w_mid.shape[2]
    half = half_cols
    n_freq = img_width // 2 // n_rows
    forward = [(i, i + 1) for i in range(n_rows - 1)]
    backward = [(target, source) for source, target in forward]
    low = lax.ppermute(latent, "rows", forward)
    high = lax.ppermute(latent, "rows", backward)
    grid, obs_const = gridded(
        vis_u, vis_v, observed, vis_weight, height, img_width, n_rows, n_grp
    )
    low, high, grid = lax.optimization_barrier((low, high, grid))
    grid = butterfly(grid, ("grp",))
    pieces = [value.transpose(1, 0, 2) for value in (low, latent, high)]
    last = jnp.pad(w_last.reshape(layers, 3, 6, channels), ((0, 0), (0, 0), (0, 2), (0, 0)))
    weights = (w_first.reshape(layers, 9, channels), w_mid, last, b_first, b_mid, b_last)
    basis_np = column_basis(img_width)
    basis_high = basis_np.astype(BF)
    basis_low = (basis_np - basis_high.astype(np.float32)).astype(BF)
    basis = jnp.asarray(np.stack([basis_high, basis_low]))
    index = lax.axis_index("rows")[None].astype(jnp.int32)
    smem = pl.BlockSpec(memory_space=pltpu.SMEM)

    def whole(value):
        rank = len(value.shape)
        return pl.BlockSpec(value.shape, lambda s: (0,) * rank)

    def per_sample(*shape):
        rank = len(shape)
        return pl.BlockSpec((1,) + shape, lambda s: (s,) + (0,) * rank)

    saved_shapes = []
    for plan in PLAN:
        for key, kind in (("h1", BF), ("h2", BF), ("s1", BF), ("s2", BF)):
            saved_shapes.append(((half, plan[key][1] * LANE), kind))
        saved_shapes.append(((half, LANE), F32))
    saved_shapes.append(((half, LANE), F32))
    saved_shapes.append(((2, half, LANE), F32))
    saved_specs = [per_sample(*shape) for shape, kind in saved_shapes]
    saved_types = [jax.ShapeDtypeStruct((samples,) + shape, kind) for shape, kind in saved_shapes]
    weights = weights + (basis,)
    bands = [((3 * LANE, plan["n1"] * LANE), BF) for plan in PLAN]
    bands += [((layers, 9 * LANE, 2 * LANE), BF)]
    bands += [((plan["n2"] * LANE, 3 * LANE), BF) for plan in PLAN]
    bands = [jax.ShapeDtypeStruct(shape, kind) for shape, kind in bands]
    max1 = max(plan["n1"] for plan in PLAN) * LANE
    max2 = max(plan["n2"] for plan in PLAN) * LANE
    params = pltpu.CompilerParams(vmem_limit_bytes=58 * 2**20)
    image_out, columns, logdet, wf_a, wf_b, wt, wl_a, wl_b, *saved = pl.pallas_call(
        functools.partial(forward_kernel, height, row_count, channels),
        grid=(samples,),
        out_shape=(
            jax.ShapeDtypeStruct((row_count, samples, img_width), F32),
            jax.ShapeDtypeStruct((n_rows, row_count, 2 * samples * n_freq), F32),
            jax.ShapeDtypeStruct((1, LANE), F32),
            *bands,
            *saved_types,
        ),
        in_specs=[smem] + [whole(value) for value in (*pieces, *weights)],
        out_specs=(
            pl.BlockSpec((row_count, samples, img_width), lambda s: (0, 0, 0)),
            pl.BlockSpec((n_rows, row_count, 2 * samples * n_freq), lambda s: (0, 0, 0)),
            pl.BlockSpec((1, LANE), lambda s: (0, 0)),
            *[whole(band) for band in bands],
            *saved_specs,
        ),
        scratch_shapes=[pltpu.VMEM((layers, 6 * LANE, LANE), BF)]
        + [pltpu.VMEM((layers, LANE), F32)] * 3
        + [pltpu.VMEM((half, 3 * max1), BF)]
        + [
            pltpu.VMEM((half, max2), BF),
            pltpu.VMEM((LANE, img_width), F32),
            pltpu.VMEM((samples, 2, half, LANE), F32),
            pltpu.VMEM((samples, 16, img_width), F32),
        ],
        compiler_params=params,
    )(index, *pieces, *weights)
    image_out = image_out.transpose(1, 0, 2)
    logdet = jnp.sum(logdet)
    norm_scale = 1.0 / math.sqrt(height * img_width)
    reach = 6
    factor = 2.0 / (vis_total * batch_size)
    columns = lax.all_to_all(columns, "rows", 0, 0, tiled=True)
    near, data_sum = spectral(
        columns.reshape(height, 2 * samples * n_freq), grid, norm_scale, factor, samples, row_count, reach
    )
    near = lax.all_to_all(near, "rows", 0, 0, tiled=True)
    span = row_count + 2 * reach
    data_part = (data_sum[0, 0] + batch_size * obs_const[0, 0] / n_rows) / vis_total
    loss_part = (data_part - logdet / (height * img_width)) / batch_size
    out_rows = layers * 3 * channels
    weights = (wf_a, wf_b, wt, wl_a, wl_b, basis)
    flat = pl.pallas_call(
        functools.partial(
            backward_kernel, height, row_count, channels, reach, batch_size * cells
        ),
        grid=(samples,),
        out_shape=jax.ShapeDtypeStruct((out_rows, LANE), F32),
        in_specs=[smem, whole(near), pl.BlockSpec((1, 1), lambda s: (0, 0))]
        + [whole(value) for value in weights] + saved_specs,
        out_specs=pl.BlockSpec((out_rows, LANE), lambda s: (0, 0)),
        scratch_shapes=[
            pltpu.VMEM((LANE, img_width), F32),
            pltpu.VMEM((img_width, LANE), F32),
            pltpu.VMEM((half, 3 * max2), BF),
            pltpu.VMEM((half, max1), BF),
            pltpu.VMEM((layers, 3 * LANE, 2 * LANE), F32),
            pltpu.VMEM((layers, 3 * LANE, 4 * LANE), F32),
            pltpu.VMEM((layers, LANE, 4 * LANE), F32),
            pltpu.VMEM((layers, 8, LANE), F32),
        ],
        compiler_params=params,
    )(index, near, loss_part.reshape(1, 1), *weights, *saved)
    flat = butterfly(flat)
    main = flat[:, : 3 * channels]
    main = main.reshape(layers, 3, channels, 3, channels).transpose(0, 1, 3, 2, 4)
    rest = flat[:, 3 * channels :].reshape(layers, 3, channels, channels)
    final_grads = [
        rest[:, :, 8:11].reshape(layers, 9, channels, 1),
        main.reshape(layers, 9, channels, channels),
        rest[:, :, :6].reshape(layers, 9, 2, channels),
        rest[:, 0, 16],
        rest[:, 0, 17],
        rest[:, 0, 18, :2],
    ]
    loss = rest[0, 0, 18, 2]
    return (
        image_out,
        loss,
        final_grads[0],
        final_grads[1],
        final_grads[2],
        final_grads[3],
        final_grads[4],
        final_grads[5],
    )


def solution(mesh):
    in_specs = (P("grp", "rows", None), P(), P(), P(), P(), P(), P(), P(), P(), P(), P())
    out_specs = (P("grp", "rows", None), P(), P(), P(), P(), P(), P(), P())
    return jax.shard_map(body, mesh=mesh, in_specs=in_specs, out_specs=out_specs, check_vma=False)
```

```python
import functools
import math

import jax
import jax.numpy as jnp
import numpy as np
from jax import lax
from jax.experimental import pallas as pl
from jax.experimental.pallas import tpu as pltpu
from jax.sharding import PartitionSpec as P


BF = jnp.bfloat16
F32 = jnp.float32
GROUP = 4
LANE = 128
SLOT = 40
PLAN = (
    dict(o1=-10, n1=8, o2=-9, n2=8, h1=(2, 5), h2=(2, 4), s1=(2, 4), s2=(2, 4)),
    dict(o1=-7, n1=7, o2=-6, n2=6, h1=(1, 5), h2=(1, 4), s1=(1, 5), s2=(0, 6)),
)


def dot(a, b, dims=((1,), (0,))):
    return lax.dot_general(a, b, (dims, ((), ())), preferred_element_type=F32)


NT = ((1,), (1,))
TN = ((0,), (0,))


def split(x):
    high = x.astype(BF)
    return high, (x - high.astype(F32)).astype(BF)


def dot3(a, b, dims):
    return dot(a[0], b[0], dims) + dot(a[1], b[0], dims) + dot(a[0], b[1], dims)


def down(x):
    turned = pltpu.roll(x, 1, 0)
    rows = lax.broadcasted_iota(jnp.int32, (8, x.shape[1]), 0)
    return jnp.concatenate([jnp.where(rows == 0, 0.0, turned[:8]), turned[8:]], axis=0)


def up(x):
    turned = pltpu.roll(x, x.shape[0] - 1, 0)
    rows = lax.broadcasted_iota(jnp.int32, (8, x.shape[1]), 0)
    return jnp.concatenate([turned[:-8], jnp.where(rows == 7, 0.0, turned[-8:])], axis=0)


def lane_ids(count):
    return lax.broadcasted_iota(jnp.int32, (1, count), 1)


def taps(cond):
    return down(cond) + pltpu.roll(cond, SLOT, 1) + pltpu.roll(up(cond), 2 * SLOT, 1)


def blk(start, count=1):
    return slice(start * LANE, (start + count) * LANE)


def forward_kernel(height, own, channels, r_ref, low_ref, mid_ref, high_ref, first_ref, taps_ref, last_ref, b1_ref,
                   b2_ref, b3_ref, basis_ref, img_ref, col_ref, logdet_ref, wf_a, wf_b, wt_ref, wl_a, wl_b, *rest):
    saved, scratch = rest[:-9], rest[-9:]
    wm_ref, bf_ref, bm_ref, bl_ref, hs, h2s, wide_s, lat_s, mine_s = scratch
    step = pl.program_id(0)
    samples, cols = lat_s.shape[0], lat_s.shape[2]
    first = r_ref[0] * own
    lane = lane_ids(LANE)
    image_row = lane - own + first
    image_mask = ((lane < 3 * own) & (image_row >= 0) & (image_row < height)).astype(F32)
    own_mask = ((lane >= own) & (lane < 2 * own)).astype(F32)

    @pl.when(step == 0)
    def _():
        logdet_ref[...] = jnp.zeros_like(logdet_ref)
        prepare(own, first_ref, taps_ref, last_ref, b1_ref, b2_ref, b3_ref, wf_a, wf_b, wm_ref, wt_ref, wl_a, wl_b,
                bf_ref, bm_ref, bl_ref)
        wide_s[...] = jnp.zeros_like(wide_s)
        for s in range(samples):
            for place, ref in enumerate((low_ref, mid_ref, high_ref)):
                wide_s[place * own : (place + 1) * own, :] = ref[:, s, :]
            turned = wide_s[...].T
            for side in range(2):
                lat_s[s, side] = turned[side * cols : (side + 1) * cols]

    def mask_of(origin, block):
        row = origin + block * GROUP + lane // channels + first
        return ((row >= 0) & (row < height)).astype(F32)

    halves = [lat_s[step, 0], lat_s[step, 1]]
    for side in range(2):
        saved[11][0, side] = halves[side]
    for layer, (wf, wl) in enumerate(((wf_a, wl_a), (wf_b, wl_b))):
        plan = PLAN[layer]
        out_h1, out_h2, out_s1, out_s2, out_log = saved[5 * layer : 5 * layer + 5]
        cond, target = halves[layer], halves[1 - layer]
        if layer == 1:
            saved[10][0] = cond
        high, low = split(taps(cond))
        both = jnp.concatenate([high, low, high], axis=1)
        for k in range(plan["n1"]):
            if k % 2 == 0:
                lanes = blk(k, min(2, plan["n1"] - k))
                pair = dot(both, wf[:, lanes])
            pre = pair[:, blk(k % 2)] + bf_ref[layer : layer + 1]
            sig = 0.5 + 0.5 * jnp.tanh(0.5 * pre)
            kept = sig * mask_of(plan["o1"], k)
            hidden = pre * kept
            start, count = plan["s1"]
            if start <= k < start + count:
                out_s1[0, :, blk(k - start)] = (kept + hidden * (1.0 - sig)).astype(BF)
            plain = hidden.astype(BF)
            hs[:, blk(3 * k)] = down(hidden).astype(BF)
            hs[:, blk(3 * k + 1)] = plain
            hs[:, blk(3 * k + 2)] = up(hidden).astype(BF)
            start, count = plan["h1"]
            if start <= k < start + count:
                out_h1[0, :, blk(k - start)] = plain
        for k in range(plan["n2"]):
            wide = min(2, plan["n1"] - k)
            pre = dot(hs[:, blk(3 * k, 3 * wide)], wm_ref[layer, : 3 * wide * LANE])
            pre = pre + bm_ref[layer : layer + 1]
            sig = 0.5 + 0.5 * jnp.tanh(0.5 * pre)
            kept = sig * mask_of(plan["o2"], k)
            hidden = pre * kept
            start, count = plan["s2"]
            if start <= k < start + count:
                out_s2[0, :, blk(k - start)] = (kept + hidden * (1.0 - sig)).astype(BF)
            hidden = hidden.astype(BF)
            h2s[:, blk(k)] = hidden
            start, count = plan["h2"]
            if start <= k < start + count:
                out_h2[0, :, blk(k - start)] = hidden
        terms = dot(h2s[:, blk(0, plan["n2"])], wl[...])
        raw = down(terms[:, blk(0)]) + terms[:, blk(1)] + up(terms[:, blk(2)])
        raw = raw + bl_ref[layer : layer + 1]
        log_scale = jnp.tanh(raw)
        out_log[0] = log_scale
        logdet_ref[...] += jnp.sum(log_scale * own_mask, axis=0, keepdims=True)
        halves[1 - layer] = (target * jnp.exp(log_scale) + pltpu.roll(raw, LANE // 2, 1)) * image_mask
    for side in range(2):
        mine = pltpu.roll(halves[side], LANE - own, 1).T
        mine_s[step, :, side * cols : (side + 1) * cols] = mine[:16]

    @pl.when(step == samples - 1)
    def _():
        for s in range(samples):
            img_ref[:, s, :] = mine_s[s, :own]
        image = split(mine_s[...].reshape(samples * 16, 2 * cols))
        spectrum = dot3(image, (basis_ref[0], basis_ref[1]), ((1,), (0,)))
        blocks, _, lanes = col_ref.shape
        n_freq = lanes // (2 * samples)
        for d in range(blocks):
            chunk, offset = divmod(d * n_freq, LANE)
            total = jnp.zeros((16, LANE), F32)
            for part in range(2):
                for s in range(samples):
                    at = (part * samples + s) * n_freq
                    piece = spectrum[s * 16 : (s + 1) * 16, blk(part * (cols // LANE) + chunk)]
                    if at != offset:
                        piece = pltpu.roll(piece, (at - offset) % LANE, 1)
                    total = jnp.where((lane >= at) & (lane < at + n_freq), piece, total)
            col_ref[d] = total[:own, :lanes]


def backward_kernel(height, own, channels, reach, cells, r_ref, near_ref, loss_ref, wf_a, wf_b, wt_ref,
                    wl_a, wl_b, basis_ref, *rest):
    saved, lat_ref, out_ref, scratch = rest[:11], rest[11], rest[12], rest[13:]
    near_s, cot_s, ds, cpo_s, acc_mid, acc_last, acc_first, acc_bias = scratch
    step = pl.program_id(0)
    first = r_ref[0] * own
    lane = lane_ids(LANE)
    image_row = lane - own + first
    image_mask = ((lane < 3 * own) & (image_row >= 0) & (image_row < height)).astype(F32)
    raw_row = lane % (LANE // 2)
    own_mask = ((raw_row >= own) & (raw_row < 2 * own)).astype(F32)

    @pl.when(step == 0)
    def _():
        near_s[...] = jnp.zeros_like(near_s)
        blocks, span, lanes = near_ref.shape
        samples = pl.num_programs(0)
        n_freq = lanes // (2 * samples)
        per = LANE // n_freq
        for s in range(samples):
            for part in range(2):
                for chunk in range(blocks // per):
                    at = (part * samples + s) * n_freq
                    total = jnp.zeros((span, LANE), F32)
                    for i in range(per):
                        piece = near_ref[chunk * per + i]
                        if lanes < LANE:
                            piece = jnp.concatenate([piece] * (LANE // lanes), axis=1)
                        if at != i * n_freq:
                            piece = pltpu.roll(piece, (i * n_freq - at) % LANE, 1)
                        total = jnp.where((lane >= i * n_freq) & (lane < (i + 1) * n_freq), piece, total)
                    near_s[s * 32 : s * 32 + span, blk(part * (blocks // per) + chunk)] = total
        cot_s[...] = dot3((basis_ref[0], basis_ref[1]), split(near_s[...]), NT)
        for ref in (acc_mid, acc_last, acc_first, acc_bias):
            ref[...] = jnp.zeros_like(ref)

    def own_of(origin, block):
        row = origin + block * GROUP + lane // channels
        return ((row >= 0) & (row < own)).astype(F32)

    cols = lat_ref.shape[2]
    cots = []
    valid = (lane >= own - reach) & (lane < 2 * own + reach)
    shift = (own - reach + LANE - 32 * step) % LANE
    for side in range(2):
        cot = pltpu.roll(cot_s[side * cols : (side + 1) * cols, :], shift, 1)
        cots.append(jnp.where(valid, cot, 0.0))
    cond_one = saved[10][0]
    for layer, wf, wl in ((1, wf_b, wl_b), (0, wf_a, wl_a)):
        plan = PLAN[layer]
        h1, h2, s1, s2, log_ref = saved[5 * layer : 5 * layer + 5]
        cond = cond_one if layer == 1 else lat_ref[0, 0]
        target = lat_ref[0, 1 - layer]
        cot_new = cots[1 - layer]
        log_scale = log_ref[0]
        cot_log = cot_new * target * jnp.exp(log_scale) - 1.0 / cells
        scale_part = cot_log * (1.0 - log_scale * log_scale) * image_mask
        raw = scale_part + pltpu.roll(cot_new * image_mask, LANE // 2, 1)
        raw = raw.astype(BF).astype(F32)
        mine = raw * own_mask
        spread = jnp.concatenate([up(raw).astype(BF), raw.astype(BF), down(raw).astype(BF)], 1)
        spread_own = jnp.concatenate([up(mine).astype(BF), mine.astype(BF), down(mine).astype(BF)], 1)
        acc_last[layer] += dot(spread_own, h2[0], TN)
        acc_bias[layer, 2:3] += jnp.sum(mine, axis=0, keepdims=True)
        start2, count2 = plan["s2"]
        base1, _ = plan["h1"]
        lefts, rights = [], []
        for k in range(start2, start2 + count2):
            if (k - start2) % 2 == 0:
                pair = dot(spread, wl[blk(k, 2), :], NT)
            cot = pair[:, blk((k - start2) % 2)] * s2[0, :, blk(k - start2)].astype(F32)
            plain = cot.astype(BF)
            cot = plain.astype(F32)
            parts = (up(cot).astype(BF), plain, down(cot).astype(BF))
            for tap, part in enumerate(parts):
                ds[:, blk(3 * (k - start2) + tap)] = part
            local = k - base1
            if 0 <= local < 4:
                mask = own_of(plan["o2"], k)
                acc_bias[layer, 1:2] += jnp.sum(cot * mask, axis=0, keepdims=True)
                lefts.append(jnp.concatenate([part * mask.astype(BF) for part in parts], 1))
                rights.append(h1[0, :, blk(local, 2)])
        acc_mid[layer] += dot(jnp.concatenate(lefts, axis=0), jnp.concatenate(rights, axis=0), TN)
        high, low = split(taps(cond))
        own_cots = []
        start1, count1 = plan["s1"]
        for k in range(start1, start1 + count1):
            side = (k - start1) % 2
            if side == 0:
                outs = min(2, start1 + count1 - k)
                lowest, highest = max(k - 1, start2), k + outs - 1
                window = ds[:, blk(3 * (lowest - start2), 3 * (highest - lowest + 1))]
                band = wt_ref[layer, 3 * (lowest - k + 1) * LANE : 3 * (highest - k + 2) * LANE, : outs * LANE]
                pair = dot(window, band)
            cot = pair[:, blk(side)]
            plain = (cot * s1[0, :, blk(k - start1)].astype(F32)).astype(BF)
            cpo_s[:, blk(k - start1)] = plain
            if k - start1 < 4:
                mask = own_of(plan["o1"], k)
                mine = plain.astype(F32) * mask
                acc_bias[layer, 0:1] += jnp.sum(mine, axis=0, keepdims=True)
                own_cots.append(mine.astype(BF))
        own_cots = jnp.concatenate(own_cots, axis=1)
        acc_first[layer] += dot(
            jnp.concatenate([high, low], axis=0), jnp.concatenate([own_cots, own_cots], axis=0), TN)
        if layer == 1:
            full = cpo_s[:, blk(0, count1)]
            lanes = blk(start1, count1)
            terms = dot(full, wf[LANE:, lanes], NT)
            terms = terms[:, :LANE] + terms[:, LANE:]
            total = up(terms) + pltpu.roll(terms, LANE - SLOT, 1) * (lane < SLOT).astype(F32)
            total = jnp.where(lane < SLOT, total, 0.0)
            total = total + jnp.where(lane < SLOT, pltpu.roll(down(terms), LANE - 2 * SLOT, 1), 0.0)
            cots[1] = cots[1] + total

    @pl.when(step == pl.num_programs(0) - 1)
    def _():
        out_ref[...] = jnp.zeros_like(out_ref)
        layers = len(PLAN)
        side = slice(3 * channels, 4 * channels)
        fold_row = lax.broadcasted_iota(jnp.int32, (4 * LANE, channels), 0)
        fold_col = lax.broadcasted_iota(jnp.int32, (4 * LANE, channels), 1)
        fold = (fold_row % channels == fold_col).astype(F32)
        hi = lax.Precision.HIGHEST

        def folded(x):
            return jnp.dot(x, fold[: x.shape[1]], precision=hi, preferred_element_type=F32)

        def by_row(ref_value, groups, size, shift):
            shape = (groups * size, 4 * LANE)
            inner = lax.broadcasted_iota(jnp.int32, shape, 0) % size
            row = lax.broadcasted_iota(jnp.int32, shape, 1) // channels
            kept = jnp.where(row - inner == shift, ref_value, 0.0)
            return folded(jnp.sum(kept.reshape(groups, size, 4 * LANE), axis=1))

        for layer, plan in enumerate(PLAN):
            for dr in range(3):
                at = (layer * 3 + dr) * channels
                for dc in range(3):
                    total = None
                    for r in range(GROUP):
                        piece = acc_mid[layer, dc * LANE + r * channels : dc * LANE + (r + 1) * channels,
                                        (r + dr) * channels : (r + dr + 1) * channels]
                        total = piece if total is None else total + piece
                    out_ref[at : at + channels, dc * channels : (dc + 1) * channels] = total
                shift = dr - 1 - own - plan["o2"] - GROUP * plan["h2"][0]
                out_ref[at : at + 6, side] = by_row(acc_last[layer], 6, LANE // 2, shift)
                shift = 1 - dr - own - plan["o1"] - GROUP * plan["s1"][0]
                out_ref[at + 8 : at + 11, side] = by_row(
                    acc_first[layer, : 3 * SLOT], 3, SLOT, shift)
            at = layer * 3 * channels + 16
            out_ref[at : at + 2, side] = folded(acc_bias[layer, 0:2])
            bias = acc_bias[layer, 2:3]
            pick = lane_ids(channels)
            low = jnp.sum(jnp.where(lane < LANE // 2, bias, 0.0), axis=1, keepdims=True)
            top = jnp.sum(jnp.where(lane >= LANE // 2, bias, 0.0), axis=1, keepdims=True)
            out_ref[at + 2 : at + 3, side] = jnp.where(
                pick == 0, low, jnp.where(pick == 1, top, jnp.where(pick == 2, loss_ref[...], 0.0)))


def prepare(own, first_ref, mid_ref, last_ref, bf_ref, bm_ref, bl_ref, wf_a, wf_b, wm_ref, wt_ref, wl_a, wl_b,
            bf_out, bm_out, bl_out):
    channels = mid_ref.shape[2]
    lane = lane_ids(LANE)

    def tiled(x):
        return jnp.concatenate([x] * GROUP, axis=1)

    bf_out[...] = tiled(bf_ref[...])
    bm_out[...] = tiled(bm_ref[...])
    bl_out[...] = jnp.where(lane < LANE // 2, bl_ref[:, 0:1], bl_ref[:, 1:2])
    spread = (lax.broadcasted_iota(jnp.int32, (channels, LANE), 0) == lane % channels).astype(BF)
    parts = lax.broadcasted_iota(jnp.int32, (8, 3 * LANE), 0)
    parts = (parts == lax.broadcasted_iota(jnp.int32, (8, 3 * LANE), 1) // (LANE // 2)).astype(BF)
    wide_lane = lane_ids(3 * LANE) % (LANE // 2)
    edge = lax.broadcasted_iota(jnp.int32, (SLOT, LANE), 0)
    for layer, (wf, wl) in enumerate(((wf_a, wl_a), (wf_b, wl_b))):
        plan = PLAN[layer]
        rows = [tiled(first_ref[layer, tap]) for tap in range(9)]
        for k in range(plan["n1"]):
            row = k * GROUP + lane // channels + plan["o1"] + own - 1
            pieces = []
            for dc in range(3):
                total = jnp.zeros((SLOT, LANE), F32)
                for dr in range(3):
                    hit = (edge == row + dr) & (edge < 3 * own)
                    total = total + jnp.where(hit, rows[3 * dr + dc], 0.0)
                pieces.append(total)
            pieces.append(jnp.zeros((LANE - 3 * SLOT, LANE), F32))
            high, low = split(jnp.concatenate(pieces, axis=0))
            wf[:LANE, blk(k)] = high
            wf[LANE : 2 * LANE, blk(k)] = high
            wf[2 * LANE :, blk(k)] = low
        for dc in range(3):
            taps_t = [dot(mid_ref[layer, 3 * dr + dc], spread, TN) for dr in range(3)]
            band = []
            for row in range(2 * GROUP):
                total = jnp.zeros((channels, LANE), F32)
                for dr in range(3):
                    if 0 <= row - dr < GROUP:
                        total = total + jnp.where(lane // channels == row - dr, taps_t[dr], 0.0)
                band.append(total)
            top = jnp.concatenate(band[:GROUP], axis=0)
            low = jnp.concatenate(band[GROUP:], axis=0)
            empty = jnp.zeros((LANE, LANE), BF)
            wm_ref[layer, blk(dc)] = top.astype(BF)
            wm_ref[layer, blk(3 + dc)] = low.astype(BF)
            near, far = low.T.astype(BF), top.T.astype(BF)
            for j, pair in enumerate(((near, empty), (far, near), (empty, far))):
                wt_ref[layer, blk(3 * j + dc), :LANE] = pair[0]
                wt_ref[layer, blk(3 * j + dc), LANE:] = pair[1]
        blank = jnp.zeros((2, channels), F32)
        columns = []
        for dr in range(3):
            pieces = [last_ref[layer, 3 * dr + dc].astype(F32) for dc in range(3)] + [blank]
            columns.append(dot(jnp.concatenate(pieces, axis=0).astype(BF), parts, TN))
        for row in range(plan["n2"] * GROUP):
            total = jnp.zeros((channels, 3 * LANE), F32)
            for dr in range(3):
                hit = (wide_lane == row + own + 1 - dr + plan["o2"]) & (wide_lane < 3 * own)
                total = total + jnp.where(hit, columns[dr], 0.0)
            wl[row * channels : (row + 1) * channels, :] = total.astype(BF)


def butterfly(value, axes=("grp", "rows")):
    for axis in axes:
        count = lax.axis_size(axis)
        hop = 1
        if count % 4 == 0:
            near = [lax.ppermute(value, axis, [(i, i ^ far) for i in range(count)]) for far in (1, 2, 3)]
            value = (value + near[0]) + (near[1] + near[2])
            hop = 4
        while hop < count:
            value = value + lax.ppermute(value, axis, [(i, i ^ hop) for i in range(count)])
            hop *= 2
    return value


def grid_kernel(n_freq, pad_freq, height, img_width, r_ref, u_ref, v_ref, obs_ref, w_ref, out_ref, const_ref,
                u_s, c_s, sign_s):
    share = u_s.shape[0]
    half = img_width // 2
    u = u_ref[...]
    v = v_ref[...]
    mirror = v > half
    v_fold = jnp.where(mirror, img_width - v, v)
    col = v_fold - r_ref[0] * n_freq
    col = jnp.where((col < 0) | (col >= n_freq), pad_freq, col)
    u_s[...] = jnp.where(mirror & (u > 0), height - u, u)
    c_s[...] = jnp.where(v_fold == half, n_freq, col)
    sign_s[...] = jnp.where(mirror, -1.0, 1.0)
    out_ref[...] = jnp.zeros_like(out_ref)
    ids = lax.broadcasted_iota(jnp.int32, (16, LANE), 0).astype(jnp.int16)
    slots = lax.broadcasted_iota(jnp.int32, (pad_freq, LANE), 0)
    one = jnp.ones((16, LANE), BF)
    zero = jnp.zeros((16, LANE), BF)
    group = 16

    def one_step(j, total):
        hots, values = [], []
        for q in range(group):
            row = pl.ds(j * group + q, 1)
            u_row = jnp.broadcast_to(u_s[row, :], (16, LANE)).astype(jnp.int16)
            hots.append(jnp.concatenate(
                [jnp.where(ids + jnp.int16(16 * g) == u_row, one, zero) for g in range(height // 16)], axis=0))
            c_hot = slots == c_s[row, :]
            lanes = pl.ds(pl.multiple_of((j * group + q) * LANE, LANE), LANE)
            w = w_ref[row, :]
            o_re, o_im = obs_ref[0:1, lanes], obs_ref[1:2, lanes]
            total = total + w * (o_re * o_re + o_im * o_im)
            parts = []
            for full in (w, w * o_re, w * o_im * sign_s[row, :]):
                high = full.astype(BF).astype(F32)
                parts += [jnp.where(c_hot, high, 0.0), jnp.where(c_hot, full - high, 0.0)]
            values.append(jnp.concatenate(parts, axis=0).astype(BF))
        out_ref[...] += dot(jnp.concatenate(hots, axis=1), jnp.concatenate(values, axis=1), NT)
        return total

    total = lax.fori_loop(0, share // group, one_step, jnp.zeros((1, LANE), F32))
    const_ref[...] = jnp.sum(total, axis=(0, 1), keepdims=True)


def slot_count(n_freq):
    return 8 * ((n_freq + 8) // 8)


def lane_selection(samples, n_freq):
    pad_freq = slot_count(n_freq)
    lanes = 2 * samples * n_freq
    sel = np.zeros((2, 3, 6 * pad_freq, lanes), np.float32)
    for special in range(2):
        for lane in range(lanes):
            part, freq = lane // (samples * n_freq), lane % n_freq
            lone = special == 1 and freq == 0
            slot = n_freq if lone and part == 1 else freq
            fields = (0, 1, 2) if lone else (0, 1 + part, None)
            for out_id, field in enumerate(fields):
                if field is not None:
                    for piece in range(2):
                        sel[special, out_id, (2 * field + piece) * pad_freq + slot, lane] = 1.0
    return sel


def gridded(vis_u, vis_v, observed, vis_weight, height, img_width, n_rows, n_grp):
    n_freq = img_width // 2 // n_rows
    pad_freq = slot_count(n_freq)
    rows = vis_u.shape[0] // LANE
    share = rows // n_grp
    rows_spec = pl.BlockSpec((share, LANE), lambda i, r: (r[1], 0))
    where = jnp.stack([lax.axis_index("rows"), lax.axis_index("grp")]).astype(jnp.int32)
    return pl.pallas_call(
        functools.partial(grid_kernel, n_freq, pad_freq, height, img_width),
        out_shape=(jax.ShapeDtypeStruct((height, 6 * pad_freq), F32),
                   jax.ShapeDtypeStruct((1, 1), F32)),
        grid_spec=pltpu.PrefetchScalarGridSpec(
            num_scalar_prefetch=1,
            grid=(1,),
            in_specs=[rows_spec, rows_spec, pl.BlockSpec((2, share * LANE), lambda i, r: (0, r[1])), rows_spec],
            out_specs=(pl.BlockSpec((height, 6 * pad_freq), lambda i, r: (0, 0)),
                       pl.BlockSpec((1, 1), lambda i, r: (0, 0))),
            scratch_shapes=[pltpu.VMEM((share, LANE), jnp.int32), pltpu.VMEM((share, LANE), jnp.int32),
                            pltpu.VMEM((share, LANE), F32)],
        ),
        compiler_params=pltpu.CompilerParams(vmem_limit_bytes=60 * 2**20),
        cost_estimate=pl.CostEstimate(flops=2 * height * 256 * share * LANE * 4,
                                      bytes_accessed=24 * share * LANE, transcendentals=0),
    )(where, vis_u.reshape(rows, LANE), vis_v.reshape(rows, LANE), observed, vis_weight.reshape(rows, LANE))


def column_basis(img_width):
    cols = np.arange(img_width)
    freq = np.arange(img_width // 2)
    angle = 2.0 * np.pi * ((cols[:, None] * freq[None, :]) % img_width) / img_width
    re, im = np.cos(angle), -np.sin(angle)
    im[:, 0] = 1.0 - 2.0 * (cols % 2)
    return np.concatenate([re, im], axis=1).astype(np.float32)


def spectral_kernel(scale, factor, half, n_freq, own, reach, r_ref, z_ref, cs_ref, grid_ref, sel_ref, near_ref,
                    data_ref, near_s):
    height, lanes = z_ref.shape
    lane = lax.broadcasted_iota(jnp.int32, (1, lanes), 1)
    lone = ((lane % n_freq) == 0) & (r_ref[0] == 0)
    sign = jnp.where(lane < half, 1.0, -1.0)
    hi = lax.Precision.HIGHEST
    z = z_ref[...] * scale
    a = jnp.dot(cs_ref[0], z, precision=hi, preferred_element_type=jnp.float32)
    b = jnp.dot(cs_ref[1], z, precision=hi, preferred_element_type=jnp.float32)
    kind = jnp.where(r_ref[0] == 0, 1, 0)
    w, t1, t2 = [
        jnp.dot(grid_ref[...], sel_ref[kind, i], precision=hi, preferred_element_type=F32) for i in range(3)
    ]

    def swap(x):
        return jnp.concatenate([x[:, half:], x[:, :half]], axis=1)

    x = jnp.where(lone, a, a + sign * swap(b))
    p = w * x - t1
    q = jnp.where(lone, w * b + t2, -sign * swap(p))
    b_lone = jnp.where(lone, b, 0.0)
    terms = w * (x * x + b_lone * b_lone) - 2.0 * (x * t1 - b_lone * t2)
    data_ref[...] = jnp.sum(terms, axis=(0, 1), keepdims=True)
    near = jnp.dot(cs_ref[2], p, precision=hi, preferred_element_type=jnp.float32)
    near = near + jnp.dot(cs_ref[3], q, precision=hi, preferred_element_type=jnp.float32)
    near_s[...] = jnp.zeros_like(near_s)
    near_s[8 : 8 + height, :] = near * (factor * scale)
    for d in range(near_ref.shape[0]):
        near_ref[d] = near_s[8 + d * own - reach : 8 + (d + 1) * own + reach, :]


def spectral(z, grid, scale, factor, samples, own, reach):
    height, lanes = z.shape
    ids = np.arange(height)
    angle = 2.0 * np.pi * ((ids[:, None] * ids[None, :]) % height) / height
    cs = np.stack([np.cos(angle), np.sin(angle), np.cos(angle), np.sin(angle)]).astype(np.float32)
    vmem = pl.BlockSpec(memory_space=pltpu.VMEM)
    return pl.pallas_call(
        functools.partial(spectral_kernel, scale, factor, lanes // 2, lanes // (2 * samples), own, reach),
        out_shape=(jax.ShapeDtypeStruct((height // own, own + 2 * reach, lanes), F32),
                   jax.ShapeDtypeStruct((1, 1), F32)),
        in_specs=[pl.BlockSpec(memory_space=pltpu.SMEM)] + [vmem] * 4,
        out_specs=(vmem, vmem),
        scratch_shapes=[pltpu.VMEM((height + 16, lanes), F32)],
        compiler_params=pltpu.CompilerParams(vmem_limit_bytes=24 * 2**20),
    )(lax.axis_index("rows")[None].astype(jnp.int32), z, jnp.asarray(cs), grid,
      jnp.asarray(lane_selection(samples, lanes // (2 * samples))))


def body(
    latent, w_first, b_first, w_mid, b_mid, w_last, b_last, vis_u, vis_v, observed, vis_weight
):
    samples, row_count, img_width = latent.shape
    half_cols = img_width // 2
    n_rows = lax.axis_size("rows")
    n_grp = lax.axis_size("grp")
    height = row_count * n_rows
    batch_size = samples * n_grp
    layers = w_first.shape[0]
    vis_total = vis_u.shape[0]
    cells = height * img_width
    channels = w_mid.shape[2]
    half = half_cols
    n_freq = img_width // 2 // n_rows
    forward = [(i, i + 1) for i in range(n_rows - 1)]
    backward = [(target, source) for source, target in forward]
    low = lax.ppermute(latent, "rows", forward)
    high = lax.ppermute(latent, "rows", backward)
    grid, obs_const = gridded(
        vis_u, vis_v, observed, vis_weight, height, img_width, n_rows, n_grp
    )
    low, high, grid = lax.optimization_barrier((low, high, grid))
    grid = butterfly(grid, ("grp",))
    pieces = [value.transpose(1, 0, 2) for value in (low, latent, high)]
    weights = (w_first.reshape(layers, 9, 1, channels), w_mid, w_last, b_first, b_mid, b_last)
    basis_np = column_basis(img_width)
    basis_high = basis_np.astype(BF)
    basis_low = (basis_np - basis_high.astype(np.float32)).astype(BF)
    basis = jnp.asarray(np.stack([basis_high, basis_low]))
    index = lax.axis_index("rows")[None].astype(jnp.int32)
    smem = pl.BlockSpec(memory_space=pltpu.SMEM)

    def whole(value):
        rank = len(value.shape)
        return pl.BlockSpec(value.shape, lambda s: (0,) * rank)

    def per_sample(*shape):
        rank = len(shape)
        return pl.BlockSpec((1,) + shape, lambda s: (s,) + (0,) * rank)

    saved_shapes = []
    for plan in PLAN:
        for key, kind in (("h1", BF), ("h2", BF), ("s1", BF), ("s2", BF)):
            saved_shapes.append(((half, plan[key][1] * LANE), kind))
        saved_shapes.append(((half, LANE), F32))
    saved_shapes.append(((half, LANE), F32))
    saved_shapes.append(((2, half, LANE), F32))
    saved_specs = [per_sample(*shape) for shape, kind in saved_shapes]
    saved_types = [jax.ShapeDtypeStruct((samples,) + shape, kind) for shape, kind in saved_shapes]
    weights = weights + (basis,)
    bands = [((3 * LANE, plan["n1"] * LANE), BF) for plan in PLAN]
    bands += [((layers, 9 * LANE, 2 * LANE), BF)]
    bands += [((plan["n2"] * LANE, 3 * LANE), BF) for plan in PLAN]
    bands = [jax.ShapeDtypeStruct(shape, kind) for shape, kind in bands]
    max1 = max(plan["n1"] for plan in PLAN) * LANE
    max2 = max(plan["n2"] for plan in PLAN) * LANE
    params = pltpu.CompilerParams(vmem_limit_bytes=58 * 2**20)
    image_out, columns, logdet, wf_a, wf_b, wt, wl_a, wl_b, *saved = pl.pallas_call(
        functools.partial(forward_kernel, height, row_count, channels),
        grid=(samples,),
        out_shape=(
            jax.ShapeDtypeStruct((row_count, samples, img_width), F32),
            jax.ShapeDtypeStruct((n_rows, row_count, 2 * samples * n_freq), F32),
            jax.ShapeDtypeStruct((1, LANE), F32),
            *bands,
            *saved_types,
        ),
        in_specs=[smem] + [whole(value) for value in (*pieces, *weights)],
        out_specs=(
            pl.BlockSpec((row_count, samples, img_width), lambda s: (0, 0, 0)),
            pl.BlockSpec((n_rows, row_count, 2 * samples * n_freq), lambda s: (0, 0, 0)),
            pl.BlockSpec((1, LANE), lambda s: (0, 0)),
            *[whole(band) for band in bands],
            *saved_specs,
        ),
        scratch_shapes=[pltpu.VMEM((layers, 6 * LANE, LANE), BF)]
        + [pltpu.VMEM((layers, LANE), F32)] * 3
        + [pltpu.VMEM((half, 3 * max1), BF)]
        + [
            pltpu.VMEM((half, max2), BF),
            pltpu.VMEM((LANE, img_width), F32),
            pltpu.VMEM((samples, 2, half, LANE), F32),
            pltpu.VMEM((samples, 16, img_width), F32),
        ],
        compiler_params=params,
    )(index, *pieces, *weights)
    image_out = image_out.transpose(1, 0, 2)
    logdet = jnp.sum(logdet)
    norm_scale = 1.0 / math.sqrt(height * img_width)
    reach = 6
    factor = 2.0 / (vis_total * batch_size)
    columns = lax.all_to_all(columns, "rows", 0, 0, tiled=True)
    near, data_sum = spectral(
        columns.reshape(height, 2 * samples * n_freq), grid, norm_scale, factor, samples, row_count, reach
    )
    near = lax.all_to_all(near, "rows", 0, 0, tiled=True)
    span = row_count + 2 * reach
    data_part = (data_sum[0, 0] + batch_size * obs_const[0, 0] / n_rows) / vis_total
    loss_part = (data_part - logdet / (height * img_width)) / batch_size
    out_rows = layers * 3 * channels
    weights = (wf_a, wf_b, wt, wl_a, wl_b, basis)
    flat = pl.pallas_call(
        functools.partial(
            backward_kernel, height, row_count, channels, reach, batch_size * cells
        ),
        grid=(samples,),
        out_shape=jax.ShapeDtypeStruct((out_rows, LANE), F32),
        in_specs=[smem, whole(near), pl.BlockSpec((1, 1), lambda s: (0, 0))]
        + [whole(value) for value in weights] + saved_specs,
        out_specs=pl.BlockSpec((out_rows, LANE), lambda s: (0, 0)),
        scratch_shapes=[
            pltpu.VMEM((LANE, img_width), F32),
            pltpu.VMEM((img_width, LANE), F32),
            pltpu.VMEM((half, 3 * max2), BF),
            pltpu.VMEM((half, max1), BF),
            pltpu.VMEM((layers, 3 * LANE, 2 * LANE), F32),
            pltpu.VMEM((layers, 3 * LANE, 4 * LANE), F32),
            pltpu.VMEM((layers, LANE, 4 * LANE), F32),
            pltpu.VMEM((layers, 8, LANE), F32),
        ],
        compiler_params=params,
    )(index, near, loss_part.reshape(1, 1), *weights, *saved)
    flat = butterfly(flat)
    main = flat[:, : 3 * channels]
    main = main.reshape(layers, 3, channels, 3, channels).transpose(0, 1, 3, 2, 4)
    rest = flat[:, 3 * channels :].reshape(layers, 3, channels, channels)
    final_grads = [
        rest[:, :, 8:11].reshape(layers, 9, channels, 1),
        main.reshape(layers, 9, channels, channels),
        rest[:, :, :6].reshape(layers, 9, 2, channels),
        rest[:, 0, 16],
        rest[:, 0, 17],
        rest[:, 0, 18, :2],
    ]
    loss = rest[0, 0, 18, 2]
    return (
        image_out,
        loss,
        final_grads[0],
        final_grads[1],
        final_grads[2],
        final_grads[3],
        final_grads[4],
        final_grads[5],
    )


def solution(mesh):
    in_specs = (P("grp", "rows", None), P(), P(), P(), P(), P(), P(), P(), P(), P(), P())
    out_specs = (P("grp", "rows", None), P(), P(), P(), P(), P(), P(), P())
    return jax.shard_map(body, mesh=mesh, in_specs=in_specs, out_specs=out_specs, check_vma=False)
```

```python
import functools
import math

import jax
import jax.numpy as jnp
import numpy as np
from jax import lax
from jax.experimental import pallas as pl
from jax.experimental.pallas import tpu as pltpu
from jax.sharding import PartitionSpec as P


BF = jnp.bfloat16
F32 = jnp.float32
GROUP = 4
LANE = 128
SLOT = 40
PLAN = (
    dict(o1=-10, n1=8, o2=-9, n2=8, h1=(2, 5), h2=(2, 4), s1=(2, 4), s2=(2, 4)),
    dict(o1=-7, n1=7, o2=-6, n2=6, h1=(1, 5), h2=(1, 4), s1=(1, 5), s2=(0, 6)),
)


def dot(a, b, dims=((1,), (0,))):
    return lax.dot_general(a, b, (dims, ((), ())), preferred_element_type=F32)


NT = ((1,), (1,))
TN = ((0,), (0,))


def split(x):
    high = x.astype(BF)
    return high, (x - high.astype(F32)).astype(BF)


def dot3(a, b, dims):
    return dot(a[0], b[0], dims) + dot(a[1], b[0], dims) + dot(a[0], b[1], dims)


def down(x):
    turned = pltpu.roll(x, 1, 0)
    rows = lax.broadcasted_iota(jnp.int32, (8, x.shape[1]), 0)
    return jnp.concatenate([jnp.where(rows == 0, 0.0, turned[:8]), turned[8:]], axis=0)


def up(x):
    turned = pltpu.roll(x, x.shape[0] - 1, 0)
    rows = lax.broadcasted_iota(jnp.int32, (8, x.shape[1]), 0)
    return jnp.concatenate([turned[:-8], jnp.where(rows == 7, 0.0, turned[-8:])], axis=0)


def lane_ids(count):
    return lax.broadcasted_iota(jnp.int32, (1, count), 1)


def taps(cond):
    return down(cond) + pltpu.roll(cond, SLOT, 1) + pltpu.roll(up(cond), 2 * SLOT, 1)


def blk(start, count=1):
    return slice(start * LANE, (start + count) * LANE)


def forward_kernel(height, own, channels, r_ref, low_ref, mid_ref, high_ref, first_ref, taps_ref, last_ref, b1_ref,
                   b2_ref, b3_ref, basis_ref, img_ref, col_ref, logdet_ref, wf_a, wf_b, wt_ref, wl_a, wl_b, *rest):
    saved, scratch = rest[:-9], rest[-9:]
    wm_ref, bf_ref, bm_ref, bl_ref, hs, h2s, wide_s, lat_s, mine_s = scratch
    step = pl.program_id(0)
    samples, cols = lat_s.shape[0], lat_s.shape[2]
    first = r_ref[0] * own
    lane = lane_ids(LANE)
    image_row = lane - own + first
    image_mask = ((lane < 3 * own) & (image_row >= 0) & (image_row < height)).astype(F32)
    own_mask = ((lane >= own) & (lane < 2 * own)).astype(F32)

    @pl.when(step == 0)
    def _():
        logdet_ref[...] = jnp.zeros_like(logdet_ref)
        prepare(own, first_ref, taps_ref, last_ref, b1_ref, b2_ref, b3_ref, wf_a, wf_b, wm_ref, wt_ref, wl_a, wl_b,
                bf_ref, bm_ref, bl_ref)
        wide_s[...] = jnp.zeros_like(wide_s)
        for s in range(samples):
            for place, ref in enumerate((low_ref, mid_ref, high_ref)):
                wide_s[place * own : (place + 1) * own, :] = ref[:, s, :]
            turned = wide_s[...].T
            for side in range(2):
                lat_s[s, side] = turned[side * cols : (side + 1) * cols]

    def mask_of(origin, block):
        row = origin + block * GROUP + lane // channels + first
        return ((row >= 0) & (row < height)).astype(F32)

    halves = [lat_s[step, 0], lat_s[step, 1]]
    for side in range(2):
        saved[11][0, side] = halves[side]
    for layer, (wf, wl) in enumerate(((wf_a, wl_a), (wf_b, wl_b))):
        plan = PLAN[layer]
        out_h1, out_h2, out_s1, out_s2, out_log = saved[5 * layer : 5 * layer + 5]
        cond, target = halves[layer], halves[1 - layer]
        if layer == 1:
            saved[10][0] = cond
        high, low = split(taps(cond))
        both = jnp.concatenate([high, low, high], axis=1)
        for k in range(plan["n1"]):
            if k % 2 == 0:
                lanes = blk(k, min(2, plan["n1"] - k))
                pair = dot(both, wf[:, lanes])
            pre = pair[:, blk(k % 2)] + bf_ref[layer : layer + 1]
            sig = 0.5 + 0.5 * jnp.tanh(0.5 * pre)
            kept = sig * mask_of(plan["o1"], k)
            hidden = pre * kept
            start, count = plan["s1"]
            if start <= k < start + count:
                out_s1[0, :, blk(k - start)] = (kept + hidden * (1.0 - sig)).astype(BF)
            plain = hidden.astype(BF)
            hs[:, blk(3 * k)] = down(hidden).astype(BF)
            hs[:, blk(3 * k + 1)] = plain
            hs[:, blk(3 * k + 2)] = up(hidden).astype(BF)
            start, count = plan["h1"]
            if start <= k < start + count:
                out_h1[0, :, blk(k - start)] = plain
        for k in range(plan["n2"]):
            wide = min(2, plan["n1"] - k)
            pre = dot(hs[:, blk(3 * k, 3 * wide)], wm_ref[layer, : 3 * wide * LANE])
            pre = pre + bm_ref[layer : layer + 1]
            sig = 0.5 + 0.5 * jnp.tanh(0.5 * pre)
            kept = sig * mask_of(plan["o2"], k)
            hidden = pre * kept
            start, count = plan["s2"]
            if start <= k < start + count:
                out_s2[0, :, blk(k - start)] = (kept + hidden * (1.0 - sig)).astype(BF)
            hidden = hidden.astype(BF)
            h2s[:, blk(k)] = hidden
            start, count = plan["h2"]
            if start <= k < start + count:
                out_h2[0, :, blk(k - start)] = hidden
        terms = dot(h2s[:, blk(0, plan["n2"])], wl[...])
        raw = down(terms[:, blk(0)]) + terms[:, blk(1)] + up(terms[:, blk(2)])
        raw = raw + bl_ref[layer : layer + 1]
        log_scale = jnp.tanh(raw)
        out_log[0] = log_scale
        logdet_ref[...] += jnp.sum(log_scale * own_mask, axis=0, keepdims=True)
        halves[1 - layer] = (target * jnp.exp(log_scale) + pltpu.roll(raw, LANE // 2, 1)) * image_mask
    for side in range(2):
        mine = pltpu.roll(halves[side], LANE - own, 1).T
        mine_s[step, :, side * cols : (side + 1) * cols] = mine[:16]

    @pl.when(step == samples - 1)
    def _():
        for s in range(samples):
            img_ref[:, s, :] = mine_s[s, :own]
        image = split(mine_s[...].reshape(samples * 16, 2 * cols))
        spectrum = dot3(image, (basis_ref[0], basis_ref[1]), ((1,), (0,)))
        blocks, _, lanes = col_ref.shape
        n_freq = lanes // (2 * samples)
        for d in range(blocks):
            chunk, offset = divmod(d * n_freq, LANE)
            total = jnp.zeros((16, LANE), F32)
            for part in range(2):
                for s in range(samples):
                    at = (part * samples + s) * n_freq
                    piece = spectrum[s * 16 : (s + 1) * 16, blk(part * (cols // LANE) + chunk)]
                    if at != offset:
                        piece = pltpu.roll(piece, (at - offset) % LANE, 1)
                    total = jnp.where((lane >= at) & (lane < at + n_freq), piece, total)
            col_ref[d] = total[:own, :lanes]


def backward_kernel(height, own, channels, reach, cells, r_ref, near_ref, loss_ref, wf_a, wf_b, wt_ref,
                    wl_a, wl_b, basis_ref, *rest):
    saved, lat_ref, out_ref, scratch = rest[:11], rest[11], rest[12], rest[13:]
    near_s, cot_s, ds, cpo_s, acc_mid, acc_last, acc_first, acc_bias = scratch
    step = pl.program_id(0)
    first = r_ref[0] * own
    lane = lane_ids(LANE)
    image_row = lane - own + first
    image_mask = ((lane < 3 * own) & (image_row >= 0) & (image_row < height)).astype(F32)
    raw_row = lane % (LANE // 2)
    own_mask = ((raw_row >= own) & (raw_row < 2 * own)).astype(F32)

    @pl.when(step == 0)
    def _():
        near_s[...] = jnp.zeros_like(near_s)
        blocks, span, lanes = near_ref.shape
        samples = pl.num_programs(0)
        n_freq = lanes // (2 * samples)
        per = LANE // n_freq
        for s in range(samples):
            for part in range(2):
                for chunk in range(blocks // per):
                    at = (part * samples + s) * n_freq
                    total = jnp.zeros((span, LANE), F32)
                    for i in range(per):
                        piece = near_ref[chunk * per + i]
                        if lanes < LANE:
                            piece = jnp.concatenate([piece] * (LANE // lanes), axis=1)
                        if at != i * n_freq:
                            piece = pltpu.roll(piece, (i * n_freq - at) % LANE, 1)
                        total = jnp.where((lane >= i * n_freq) & (lane < (i + 1) * n_freq), piece, total)
                    near_s[s * 32 : s * 32 + span, blk(part * (blocks // per) + chunk)] = total
        cot_s[...] = dot3((basis_ref[0], basis_ref[1]), split(near_s[...]), NT)
        for ref in (acc_mid, acc_last, acc_first, acc_bias):
            ref[...] = jnp.zeros_like(ref)

    def own_of(origin, block):
        row = origin + block * GROUP + lane // channels
        return ((row >= 0) & (row < own)).astype(F32)

    cols = lat_ref.shape[2]
    cots = []
    valid = (lane >= own - reach) & (lane < 2 * own + reach)
    shift = (own - reach + LANE - 32 * step) % LANE
    for side in range(2):
        cot = pltpu.roll(cot_s[side * cols : (side + 1) * cols, :], shift, 1)
        cots.append(jnp.where(valid, cot, 0.0))
    cond_one = saved[10][0]
    for layer, wf, wl in ((1, wf_b, wl_b), (0, wf_a, wl_a)):
        plan = PLAN[layer]
        h1, h2, s1, s2, log_ref = saved[5 * layer : 5 * layer + 5]
        cond = cond_one if layer == 1 else lat_ref[0, 0]
        target = lat_ref[0, 1 - layer]
        cot_new = cots[1 - layer]
        log_scale = log_ref[0]
        cot_log = cot_new * target * jnp.exp(log_scale) - 1.0 / cells
        scale_part = cot_log * (1.0 - log_scale * log_scale) * image_mask
        raw = scale_part + pltpu.roll(cot_new * image_mask, LANE // 2, 1)
        raw = raw.astype(BF).astype(F32)
        mine = raw * own_mask
        spread = jnp.concatenate([up(raw).astype(BF), raw.astype(BF), down(raw).astype(BF)], 1)
        spread_own = jnp.concatenate([up(mine).astype(BF), mine.astype(BF), down(mine).astype(BF)], 1)
        acc_last[layer] += dot(spread_own, h2[0], TN)
        acc_bias[layer, 2:3] += jnp.sum(mine, axis=0, keepdims=True)
        start2, count2 = plan["s2"]
        base1, _ = plan["h1"]
        lefts, rights = [], []
        for k in range(start2, start2 + count2):
            if (k - start2) % 2 == 0:
                pair = dot(spread, wl[blk(k, 2), :], NT)
            cot = pair[:, blk((k - start2) % 2)] * s2[0, :, blk(k - start2)].astype(F32)
            plain = cot.astype(BF)
            cot = plain.astype(F32)
            parts = (up(cot).astype(BF), plain, down(cot).astype(BF))
            for tap, part in enumerate(parts):
                ds[:, blk(3 * (k - start2) + tap)] = part
            local = k - base1
            if 0 <= local < 4:
                mask = own_of(plan["o2"], k)
                acc_bias[layer, 1:2] += jnp.sum(cot * mask, axis=0, keepdims=True)
                lefts.append(jnp.concatenate([part * mask.astype(BF) for part in parts], 1))
                rights.append(h1[0, :, blk(local, 2)])
        acc_mid[layer] += dot(jnp.concatenate(lefts, axis=0), jnp.concatenate(rights, axis=0), TN)
        high, low = split(taps(cond))
        own_cots = []
        start1, count1 = plan["s1"]
        for k in range(start1, start1 + count1):
            side = (k - start1) % 2
            if side == 0:
                outs = min(2, start1 + count1 - k)
                lowest, highest = max(k - 1, start2), k + outs - 1
                window = ds[:, blk(3 * (lowest - start2), 3 * (highest - lowest + 1))]
                band = wt_ref[layer, 3 * (lowest - k + 1) * LANE : 3 * (highest - k + 2) * LANE, : outs * LANE]
                pair = dot(window, band)
            cot = pair[:, blk(side)]
            plain = (cot * s1[0, :, blk(k - start1)].astype(F32)).astype(BF)
            cpo_s[:, blk(k - start1)] = plain
            if k - start1 < 4:
                mask = own_of(plan["o1"], k)
                mine = plain.astype(F32) * mask
                acc_bias[layer, 0:1] += jnp.sum(mine, axis=0, keepdims=True)
                own_cots.append(mine.astype(BF))
        own_cots = jnp.concatenate(own_cots, axis=1)
        acc_first[layer] += dot(
            jnp.concatenate([high, low], axis=0), jnp.concatenate([own_cots, own_cots], axis=0), TN)
        if layer == 1:
            full = cpo_s[:, blk(0, count1)]
            lanes = blk(start1, count1)
            terms = dot(full, wf[LANE:, lanes], NT)
            terms = terms[:, :LANE] + terms[:, LANE:]
            total = up(terms) + pltpu.roll(terms, LANE - SLOT, 1) * (lane < SLOT).astype(F32)
            total = jnp.where(lane < SLOT, total, 0.0)
            total = total + jnp.where(lane < SLOT, pltpu.roll(down(terms), LANE - 2 * SLOT, 1), 0.0)
            cots[1] = cots[1] + total

    @pl.when(step == pl.num_programs(0) - 1)
    def _():
        out_ref[...] = jnp.zeros_like(out_ref)
        layers = len(PLAN)
        side = slice(3 * channels, 4 * channels)
        fold_row = lax.broadcasted_iota(jnp.int32, (4 * LANE, channels), 0)
        fold_col = lax.broadcasted_iota(jnp.int32, (4 * LANE, channels), 1)
        fold = (fold_row % channels == fold_col).astype(F32)
        hi = lax.Precision.HIGHEST

        def folded(x):
            return jnp.dot(x, fold[: x.shape[1]], precision=hi, preferred_element_type=F32)

        def by_row(ref_value, groups, size, shift):
            shape = (groups * size, 4 * LANE)
            inner = lax.broadcasted_iota(jnp.int32, shape, 0) % size
            row = lax.broadcasted_iota(jnp.int32, shape, 1) // channels
            kept = jnp.where(row - inner == shift, ref_value, 0.0)
            return folded(jnp.sum(kept.reshape(groups, size, 4 * LANE), axis=1))

        for layer, plan in enumerate(PLAN):
            for dr in range(3):
                at = (layer * 3 + dr) * channels
                for dc in range(3):
                    total = None
                    for r in range(GROUP):
                        piece = acc_mid[layer, dc * LANE + r * channels : dc * LANE + (r + 1) * channels,
                                        (r + dr) * channels : (r + dr + 1) * channels]
                        total = piece if total is None else total + piece
                    out_ref[at : at + channels, dc * channels : (dc + 1) * channels] = total
                shift = dr - 1 - own - plan["o2"] - GROUP * plan["h2"][0]
                out_ref[at : at + 6, side] = by_row(acc_last[layer], 6, LANE // 2, shift)
                shift = 1 - dr - own - plan["o1"] - GROUP * plan["s1"][0]
                out_ref[at + 8 : at + 11, side] = by_row(
                    acc_first[layer, : 3 * SLOT], 3, SLOT, shift)
            at = layer * 3 * channels + 16
            out_ref[at : at + 2, side] = folded(acc_bias[layer, 0:2])
            bias = acc_bias[layer, 2:3]
            pick = lane_ids(channels)
            low = jnp.sum(jnp.where(lane < LANE // 2, bias, 0.0), axis=1, keepdims=True)
            top = jnp.sum(jnp.where(lane >= LANE // 2, bias, 0.0), axis=1, keepdims=True)
            out_ref[at + 2 : at + 3, side] = jnp.where(
                pick == 0, low, jnp.where(pick == 1, top, jnp.where(pick == 2, loss_ref[...], 0.0)))


def prepare(own, first_ref, mid_ref, last_ref, bf_ref, bm_ref, bl_ref, wf_a, wf_b, wm_ref, wt_ref, wl_a, wl_b,
            bf_out, bm_out, bl_out):
    channels = mid_ref.shape[2]
    lane = lane_ids(LANE)

    def tiled(x):
        return jnp.concatenate([x] * GROUP, axis=1)

    bf_out[...] = tiled(bf_ref[...])
    bm_out[...] = tiled(bm_ref[...])
    bl_out[...] = jnp.where(lane < LANE // 2, bl_ref[:, 0:1], bl_ref[:, 1:2])
    spread = (lax.broadcasted_iota(jnp.int32, (channels, LANE), 0) == lane % channels).astype(BF)
    parts = lax.broadcasted_iota(jnp.int32, (8, 3 * LANE), 0)
    parts = (parts == lax.broadcasted_iota(jnp.int32, (8, 3 * LANE), 1) // (LANE // 2)).astype(BF)
    wide_lane = lane_ids(3 * LANE) % (LANE // 2)
    edge = lax.broadcasted_iota(jnp.int32, (SLOT, LANE), 0)
    for layer, (wf, wl) in enumerate(((wf_a, wl_a), (wf_b, wl_b))):
        plan = PLAN[layer]
        rows = [tiled(first_ref[layer, tap]) for tap in range(9)]
        for k in range(plan["n1"]):
            row = k * GROUP + lane // channels + plan["o1"] + own - 1
            pieces = []
            for dc in range(3):
                total = jnp.zeros((SLOT, LANE), F32)
                for dr in range(3):
                    hit = (edge == row + dr) & (edge < 3 * own)
                    total = total + jnp.where(hit, rows[3 * dr + dc], 0.0)
                pieces.append(total)
            pieces.append(jnp.zeros((LANE - 3 * SLOT, LANE), F32))
            high, low = split(jnp.concatenate(pieces, axis=0))
            wf[:LANE, blk(k)] = high
            wf[LANE : 2 * LANE, blk(k)] = high
            wf[2 * LANE :, blk(k)] = low
        for dc in range(3):
            taps_t = [dot(mid_ref[layer, 3 * dr + dc], spread, TN) for dr in range(3)]
            band = []
            for row in range(2 * GROUP):
                total = jnp.zeros((channels, LANE), F32)
                for dr in range(3):
                    if 0 <= row - dr < GROUP:
                        total = total + jnp.where(lane // channels == row - dr, taps_t[dr], 0.0)
                band.append(total)
            top = jnp.concatenate(band[:GROUP], axis=0)
            low = jnp.concatenate(band[GROUP:], axis=0)
            empty = jnp.zeros((LANE, LANE), BF)
            wm_ref[layer, blk(dc)] = top.astype(BF)
            wm_ref[layer, blk(3 + dc)] = low.astype(BF)
            near, far = low.T.astype(BF), top.T.astype(BF)
            for j, pair in enumerate(((near, empty), (far, near), (empty, far))):
                wt_ref[layer, blk(3 * j + dc), :LANE] = pair[0]
                wt_ref[layer, blk(3 * j + dc), LANE:] = pair[1]
        blank = jnp.zeros((2, channels), F32)
        columns = []
        for dr in range(3):
            pieces = [last_ref[layer, 3 * dr + dc].astype(F32) for dc in range(3)] + [blank]
            columns.append(dot(jnp.concatenate(pieces, axis=0).astype(BF), parts, TN))
        for row in range(plan["n2"] * GROUP):
            total = jnp.zeros((channels, 3 * LANE), F32)
            for dr in range(3):
                hit = (wide_lane == row + own + 1 - dr + plan["o2"]) & (wide_lane < 3 * own)
                total = total + jnp.where(hit, columns[dr], 0.0)
            wl[row * channels : (row + 1) * channels, :] = total.astype(BF)


def butterfly(value, axes=("grp", "rows")):
    for axis in axes:
        count = lax.axis_size(axis)
        hop = 1
        if count % 4 == 0:
            near = [lax.ppermute(value, axis, [(i, i ^ far) for i in range(count)]) for far in (1, 2, 3)]
            value = (value + near[0]) + (near[1] + near[2])
            hop = 4
        while hop < count:
            value = value + lax.ppermute(value, axis, [(i, i ^ hop) for i in range(count)])
            hop *= 2
    return value


def grid_kernel(n_freq, pad_freq, height, img_width, r_ref, g_ref, u_ref, v_ref, obs_ref, w_ref, out_ref, const_ref,
                u_s, c_s, sign_s):
    share = u_s.shape[0]
    half = img_width // 2
    u = u_ref[...]
    v = v_ref[...]
    mirror = v > half
    v_fold = jnp.where(mirror, img_width - v, v)
    col = v_fold - r_ref[0] * n_freq
    col = jnp.where((col < 0) | (col >= n_freq), pad_freq, col)
    u_s[...] = jnp.where(mirror & (u > 0), height - u, u)
    c_s[...] = jnp.where(v_fold == half, n_freq, col)
    sign_s[...] = jnp.where(mirror, -1.0, 1.0)
    out_ref[...] = jnp.zeros_like(out_ref)
    ids = lax.broadcasted_iota(jnp.int32, (16, LANE), 0).astype(jnp.int16)
    slots = lax.broadcasted_iota(jnp.int32, (pad_freq, LANE), 0)
    one = jnp.ones((16, LANE), BF)
    zero = jnp.zeros((16, LANE), BF)
    group = 16

    def one_step(j, total):
        hots, values = [], []
        for q in range(group):
            row = pl.ds(j * group + q, 1)
            u_row = jnp.broadcast_to(u_s[row, :], (16, LANE)).astype(jnp.int16)
            hots.append(jnp.concatenate(
                [jnp.where(ids + jnp.int16(16 * g) == u_row, one, zero) for g in range(height // 16)], axis=0))
            c_hot = slots == c_s[row, :]
            lanes = pl.ds(pl.multiple_of((j * group + q) * LANE, LANE), LANE)
            w = w_ref[row, :]
            o_re, o_im = obs_ref[0:1, lanes], obs_ref[1:2, lanes]
            total = total + w * (o_re * o_re + o_im * o_im)
            parts = []
            for full in (w, w * o_re, w * o_im * sign_s[row, :]):
                high = full.astype(BF).astype(F32)
                parts += [jnp.where(c_hot, high, 0.0), jnp.where(c_hot, full - high, 0.0)]
            values.append(jnp.concatenate(parts, axis=0).astype(BF))
        out_ref[...] += dot(jnp.concatenate(hots, axis=1), jnp.concatenate(values, axis=1), NT)
        return total

    total = lax.fori_loop(0, share // group, one_step, jnp.zeros((1, LANE), F32))
    const_ref[...] = jnp.sum(total, axis=(0, 1), keepdims=True)


def slot_count(n_freq):
    return 8 * ((n_freq + 8) // 8)


def lane_selection(samples, n_freq):
    pad_freq = slot_count(n_freq)
    lanes = 2 * samples * n_freq
    sel = np.zeros((2, 3, 6 * pad_freq, lanes), np.float32)
    for special in range(2):
        for lane in range(lanes):
            part, freq = lane // (samples * n_freq), lane % n_freq
            lone = special == 1 and freq == 0
            slot = n_freq if lone and part == 1 else freq
            fields = (0, 1, 2) if lone else (0, 1 + part, None)
            for out_id, field in enumerate(fields):
                if field is not None:
                    for piece in range(2):
                        sel[special, out_id, (2 * field + piece) * pad_freq + slot, lane] = 1.0
    return sel


def gridded(vis_u, vis_v, observed, vis_weight, height, img_width, n_rows, n_grp):
    n_freq = img_width // 2 // n_rows
    pad_freq = slot_count(n_freq)
    rows = vis_u.shape[0] // LANE
    share = rows // n_grp
    rows_spec = pl.BlockSpec((share, LANE), lambda i, r, g: (g[0], 0))
    where = [lax.axis_index(axis)[None].astype(jnp.int32) for axis in ("rows", "grp")]
    return pl.pallas_call(
        functools.partial(grid_kernel, n_freq, pad_freq, height, img_width),
        out_shape=(jax.ShapeDtypeStruct((height, 6 * pad_freq), F32),
                   jax.ShapeDtypeStruct((1, 1), F32)),
        grid_spec=pltpu.PrefetchScalarGridSpec(
            num_scalar_prefetch=2,
            grid=(1,),
            in_specs=[rows_spec, rows_spec, pl.BlockSpec((2, share * LANE), lambda i, r, g: (0, g[0])), rows_spec],
            out_specs=(pl.BlockSpec((height, 6 * pad_freq), lambda i, r, g: (0, 0)),
                       pl.BlockSpec((1, 1), lambda i, r, g: (0, 0))),
            scratch_shapes=[pltpu.VMEM((share, LANE), jnp.int32), pltpu.VMEM((share, LANE), jnp.int32),
                            pltpu.VMEM((share, LANE), F32)],
        ),
        compiler_params=pltpu.CompilerParams(vmem_limit_bytes=60 * 2**20),
        cost_estimate=pl.CostEstimate(flops=2 * height * 256 * share * LANE * 4,
                                      bytes_accessed=24 * share * LANE, transcendentals=0),
    )(*where, vis_u.reshape(rows, LANE), vis_v.reshape(rows, LANE), observed, vis_weight.reshape(rows, LANE))


def column_basis(img_width):
    cols = np.arange(img_width)
    freq = np.arange(img_width // 2)
    angle = 2.0 * np.pi * ((cols[:, None] * freq[None, :]) % img_width) / img_width
    re, im = np.cos(angle), -np.sin(angle)
    im[:, 0] = 1.0 - 2.0 * (cols % 2)
    return np.concatenate([re, im], axis=1).astype(np.float32)


def spectral_kernel(scale, factor, half, n_freq, own, reach, r_ref, z_ref, cs_ref, grid_ref, sel_ref, near_ref,
                    data_ref, near_s):
    height, lanes = z_ref.shape
    lane = lax.broadcasted_iota(jnp.int32, (1, lanes), 1)
    lone = ((lane % n_freq) == 0) & (r_ref[0] == 0)
    sign = jnp.where(lane < half, 1.0, -1.0)
    hi = lax.Precision.HIGHEST
    z = z_ref[...] * scale
    a = jnp.dot(cs_ref[0], z, precision=hi, preferred_element_type=jnp.float32)
    b = jnp.dot(cs_ref[1], z, precision=hi, preferred_element_type=jnp.float32)
    kind = jnp.where(r_ref[0] == 0, 1, 0)
    w, t1, t2 = [
        jnp.dot(grid_ref[...], sel_ref[kind, i], precision=hi, preferred_element_type=F32) for i in range(3)
    ]

    def swap(x):
        return jnp.concatenate([x[:, half:], x[:, :half]], axis=1)

    x = jnp.where(lone, a, a + sign * swap(b))
    p = w * x - t1
    q = jnp.where(lone, w * b + t2, -sign * swap(p))
    b_lone = jnp.where(lone, b, 0.0)
    terms = w * (x * x + b_lone * b_lone) - 2.0 * (x * t1 - b_lone * t2)
    data_ref[...] = jnp.sum(terms, axis=(0, 1), keepdims=True)
    near = jnp.dot(cs_ref[2], p, precision=hi, preferred_element_type=jnp.float32)
    near = near + jnp.dot(cs_ref[3], q, precision=hi, preferred_element_type=jnp.float32)
    near_s[...] = jnp.zeros_like(near_s)
    near_s[8 : 8 + height, :] = near * (factor * scale)
    for d in range(near_ref.shape[0]):
        near_ref[d] = near_s[8 + d * own - reach : 8 + (d + 1) * own + reach, :]


def spectral(z, grid, scale, factor, samples, own, reach):
    height, lanes = z.shape
    ids = np.arange(height)
    angle = 2.0 * np.pi * ((ids[:, None] * ids[None, :]) % height) / height
    cs = np.stack([np.cos(angle), np.sin(angle), np.cos(angle), np.sin(angle)]).astype(np.float32)
    vmem = pl.BlockSpec(memory_space=pltpu.VMEM)
    return pl.pallas_call(
        functools.partial(spectral_kernel, scale, factor, lanes // 2, lanes // (2 * samples), own, reach),
        out_shape=(jax.ShapeDtypeStruct((height // own, own + 2 * reach, lanes), F32),
                   jax.ShapeDtypeStruct((1, 1), F32)),
        in_specs=[pl.BlockSpec(memory_space=pltpu.SMEM)] + [vmem] * 4,
        out_specs=(vmem, vmem),
        scratch_shapes=[pltpu.VMEM((height + 16, lanes), F32)],
        compiler_params=pltpu.CompilerParams(vmem_limit_bytes=24 * 2**20),
    )(lax.axis_index("rows")[None].astype(jnp.int32), z, jnp.asarray(cs), grid,
      jnp.asarray(lane_selection(samples, lanes // (2 * samples))))


def body(
    latent, w_first, b_first, w_mid, b_mid, w_last, b_last, vis_u, vis_v, observed, vis_weight
):
    samples, row_count, img_width = latent.shape
    half_cols = img_width // 2
    n_rows = lax.axis_size("rows")
    n_grp = lax.axis_size("grp")
    height = row_count * n_rows
    batch_size = samples * n_grp
    layers = w_first.shape[0]
    vis_total = vis_u.shape[0]
    cells = height * img_width
    channels = w_mid.shape[2]
    half = half_cols
    n_freq = img_width // 2 // n_rows
    forward = [(i, i + 1) for i in range(n_rows - 1)]
    backward = [(target, source) for source, target in forward]
    low = lax.ppermute(latent, "rows", forward)
    high = lax.ppermute(latent, "rows", backward)
    grid, obs_const = gridded(
        vis_u, vis_v, observed, vis_weight, height, img_width, n_rows, n_grp
    )
    low, high, grid = lax.optimization_barrier((low, high, grid))
    grid = butterfly(grid, ("grp",))
    pieces = [value.transpose(1, 0, 2) for value in (low, latent, high)]
    weights = (w_first.reshape(layers, 9, 1, channels), w_mid, w_last, b_first, b_mid, b_last)
    basis_np = column_basis(img_width)
    basis_high = basis_np.astype(BF)
    basis_low = (basis_np - basis_high.astype(np.float32)).astype(BF)
    basis = jnp.asarray(np.stack([basis_high, basis_low]))
    index = lax.axis_index("rows")[None].astype(jnp.int32)
    smem = pl.BlockSpec(memory_space=pltpu.SMEM)

    def whole(value):
        rank = len(value.shape)
        return pl.BlockSpec(value.shape, lambda s: (0,) * rank)

    def per_sample(*shape):
        rank = len(shape)
        return pl.BlockSpec((1,) + shape, lambda s: (s,) + (0,) * rank)

    saved_shapes = []
    for plan in PLAN:
        for key, kind in (("h1", BF), ("h2", BF), ("s1", BF), ("s2", BF)):
            saved_shapes.append(((half, plan[key][1] * LANE), kind))
        saved_shapes.append(((half, LANE), F32))
    saved_shapes.append(((half, LANE), F32))
    saved_shapes.append(((2, half, LANE), F32))
    saved_specs = [per_sample(*shape) for shape, kind in saved_shapes]
    saved_types = [jax.ShapeDtypeStruct((samples,) + shape, kind) for shape, kind in saved_shapes]
    weights = weights + (basis,)
    bands = [((3 * LANE, plan["n1"] * LANE), BF) for plan in PLAN]
    bands += [((layers, 9 * LANE, 2 * LANE), BF)]
    bands += [((plan["n2"] * LANE, 3 * LANE), BF) for plan in PLAN]
    bands = [jax.ShapeDtypeStruct(shape, kind) for shape, kind in bands]
    max1 = max(plan["n1"] for plan in PLAN) * LANE
    max2 = max(plan["n2"] for plan in PLAN) * LANE
    params = pltpu.CompilerParams(vmem_limit_bytes=58 * 2**20)
    image_out, columns, logdet, wf_a, wf_b, wt, wl_a, wl_b, *saved = pl.pallas_call(
        functools.partial(forward_kernel, height, row_count, channels),
        grid=(samples,),
        out_shape=(
            jax.ShapeDtypeStruct((row_count, samples, img_width), F32),
            jax.ShapeDtypeStruct((n_rows, row_count, 2 * samples * n_freq), F32),
            jax.ShapeDtypeStruct((1, LANE), F32),
            *bands,
            *saved_types,
        ),
        in_specs=[smem] + [whole(value) for value in (*pieces, *weights)],
        out_specs=(
            pl.BlockSpec((row_count, samples, img_width), lambda s: (0, 0, 0)),
            pl.BlockSpec((n_rows, row_count, 2 * samples * n_freq), lambda s: (0, 0, 0)),
            pl.BlockSpec((1, LANE), lambda s: (0, 0)),
            *[whole(band) for band in bands],
            *saved_specs,
        ),
        scratch_shapes=[pltpu.VMEM((layers, 6 * LANE, LANE), BF)]
        + [pltpu.VMEM((layers, LANE), F32)] * 3
        + [pltpu.VMEM((half, 3 * max1), BF)]
        + [
            pltpu.VMEM((half, max2), BF),
            pltpu.VMEM((LANE, img_width), F32),
            pltpu.VMEM((samples, 2, half, LANE), F32),
            pltpu.VMEM((samples, 16, img_width), F32),
        ],
        compiler_params=params,
    )(index, *pieces, *weights)
    image_out = image_out.transpose(1, 0, 2)
    logdet = jnp.sum(logdet)
    norm_scale = 1.0 / math.sqrt(height * img_width)
    reach = 6
    factor = 2.0 / (vis_total * batch_size)
    columns = lax.all_to_all(columns, "rows", 0, 0, tiled=True)
    near, data_sum = spectral(
        columns.reshape(height, 2 * samples * n_freq), grid, norm_scale, factor, samples, row_count, reach
    )
    near = lax.all_to_all(near, "rows", 0, 0, tiled=True)
    span = row_count + 2 * reach
    data_part = (data_sum[0, 0] + batch_size * obs_const[0, 0] / n_rows) / vis_total
    loss_part = (data_part - logdet / (height * img_width)) / batch_size
    out_rows = layers * 3 * channels
    weights = (wf_a, wf_b, wt, wl_a, wl_b, basis)
    flat = pl.pallas_call(
        functools.partial(
            backward_kernel, height, row_count, channels, reach, batch_size * cells
        ),
        grid=(samples,),
        out_shape=jax.ShapeDtypeStruct((out_rows, LANE), F32),
        in_specs=[smem, whole(near), pl.BlockSpec((1, 1), lambda s: (0, 0))]
        + [whole(value) for value in weights] + saved_specs,
        out_specs=pl.BlockSpec((out_rows, LANE), lambda s: (0, 0)),
        scratch_shapes=[
            pltpu.VMEM((LANE, img_width), F32),
            pltpu.VMEM((img_width, LANE), F32),
            pltpu.VMEM((half, 3 * max2), BF),
            pltpu.VMEM((half, max1), BF),
            pltpu.VMEM((layers, 3 * LANE, 2 * LANE), F32),
            pltpu.VMEM((layers, 3 * LANE, 4 * LANE), F32),
            pltpu.VMEM((layers, LANE, 4 * LANE), F32),
            pltpu.VMEM((layers, 8, LANE), F32),
        ],
        compiler_params=params,
    )(index, near, loss_part.reshape(1, 1), *weights, *saved)
    flat = butterfly(flat)
    main = flat[:, : 3 * channels]
    main = main.reshape(layers, 3, channels, 3, channels).transpose(0, 1, 3, 2, 4)
    rest = flat[:, 3 * channels :].reshape(layers, 3, channels, channels)
    final_grads = [
        rest[:, :, 8:11].reshape(layers, 9, channels, 1),
        main.reshape(layers, 9, channels, channels),
        rest[:, :, :6].reshape(layers, 9, 2, channels),
        rest[:, 0, 16],
        rest[:, 0, 17],
        rest[:, 0, 18, :2],
    ]
    loss = rest[0, 0, 18, 2]
    return (
        image_out,
        loss,
        final_grads[0],
        final_grads[1],
        final_grads[2],
        final_grads[3],
        final_grads[4],
        final_grads[5],
    )


def solution(mesh):
    in_specs = (P("grp", "rows", None), P(), P(), P(), P(), P(), P(), P(), P(), P(), P())
    out_specs = (P("grp", "rows", None), P(), P(), P(), P(), P(), P(), P())
    return jax.shard_map(body, mesh=mesh, in_specs=in_specs, out_specs=out_specs, check_vma=False)
```
